128 devices in a mesh: flow: 32 (over y, x, core), cross: 4 (over z).
Axes of the slice: x: 4, y: 4, z: 4, core: 2. Of those that a mesh axis runs over, the one named last changes fastest.
Arguments:
- fluid_pop: float32 [384, 19, 4096], P(('flow', 'cross'))
- heat_pop: float32 [384, 7, 4096], P(('flow', 'cross'))
- solid_temp: float32 [256, 4096], P(('flow', 'cross'))
- material: int32 [256, 4096], P(('flow', 'cross')), may hold values from 0 to 7
- conductivity: float32 [8], replicated, may hold values from 0.1 to 2
- fluid_nbr: int32 [384, 18], P(('flow', 'cross')), may hold values from -1 to 383, as said below
- solid_face: int32 [384, 6], P(('flow', 'cross')), may hold values from -1 to 255, as said below
- solid_nbr: int32 [256, 6], P(('flow', 'cross')), may hold values from -1 to 255, as said below
- solid_fluid: int32 [256, 6], P(('flow', 'cross')), may hold values from -1 to 383, as said below
Outputs:
- fluid_out: float32 [384, 19, 4096], P(('flow', 'cross'))
- heat_out: float32 [384, 7, 4096], P(('flow', 'cross'))
- solid_out: float32 [256, 4096], P(('flow', 'cross'))
The draws below stay inside these ranges and needn't reach their ends.
Inputs may be any that keep to these rules, and one draw needn't show every extreme that they name: `fluid_nbr`: the blocks tile a lattice of 32 x 4 x 5 block positions. Fluid block b is held by device b // 3 and solid block s by device s // 2, devices counted along flow, then cross; each device's blocks fill its own region of 1 x 1 x 5 positions, with 3 fluid and 2 solid blocks in ascending position order, so every neighbour of a block is held by a device whose flow and cross indices differ by at most one from its own. Entry [b, n] is the fluid block at b's position plus c_(n+1), or -1 where that position is solid or outside the lattice. `solid_face`: entry [b, k] is the solid block at fluid block b's position plus c_(k+1), or -1. `solid_nbr`: entry [s, k] is the solid block at solid block s's position plus c_(k+1), or -1. `solid_fluid`: entry [s, k] is the fluid block at solid block s's position plus c_(k+1), or -1; it is b exactly when solid_face holds s for b in the opposite direction.
All inputs are finite; a program needn't handle non-finite values.
Results may differ from the reference program's by a relative error of at most 0.0003.
Values sent between devices are 32-bit elements; how exact they have to be, the bound alone decides.
A program may use at most 192 MiB of HBM per device.

```python
import math
import jax
import jax.numpy as jnp
import numpy as np

BLK = 16
XR = 1
BYC = 1
BZ = 5
ITERS = 3
NMAT = 8
CELLS = 4096
FB = 3
NF_TOT = 384
NS_TOT = 256
LAT_X = 32
LAT_Y = 4


VELOCITY = np.array([[0, 0, 0], [1, 0, 0], [-1, 0, 0], [0, 1, 0], [0, -1, 0], [0, 0, 1], [0, 0, -1], [1, 1, 0], [-1, -1, 0], [1, -1, 0], [-1, 1, 0], [1, 0, 1], [-1, 0, -1], [1, 0, -1], [-1, 0, 1], [0, 1, 1], [0, -1, -1], [0, 1, -1], [0, -1, 1]])


def block_geometry(key):
    flow_count = LAT_X // XR
    cross_count = LAT_Y // BYC
    region_count = flow_count * cross_count
    per_region = XR * BYC * BZ
    region_keys = jax.random.split(key, region_count)
    shuffled = jax.vmap(lambda region_key: jax.random.permutation(region_key, per_region))(region_keys)
    fluid_local = jnp.sort(shuffled[:, :FB], axis=1)
    solid_local = jnp.sort(shuffled[:, FB:], axis=1)
    region_ids = jnp.arange(region_count)
    region_flow = (region_ids // cross_count)[:, None]
    region_cross = (region_ids % cross_count)[:, None]

    def place_rows(local_ids):
        slab_index = local_ids // (BYC * BZ)
        across_index = local_ids // BZ % BYC
        depth_index = local_ids % BZ
        return (((region_flow * XR + slab_index) * LAT_Y + region_cross * BYC + across_index) * BZ + depth_index).reshape(-1)
    fluid_place = place_rows(fluid_local)
    solid_place = place_rows(solid_local)
    lattice_cells = LAT_X * LAT_Y * BZ
    fluid_table = jnp.full((lattice_cells,), -1, jnp.int32).at[fluid_place].set(jnp.arange(fluid_place.shape[0], dtype=jnp.int32))
    solid_table = jnp.full((lattice_cells,), -1, jnp.int32).at[solid_place].set(jnp.arange(solid_place.shape[0], dtype=jnp.int32))

    def beside_all(place_ids, step_list, id_table):
        along_index = place_ids // (LAT_Y * BZ)
        across_index = place_ids // BZ % LAT_Y
        depth_index = place_ids % BZ
        next_along = along_index[:, None] + step_list[None, :, 0]
        next_across = across_index[:, None] + step_list[None, :, 1]
        next_depth = depth_index[:, None] + step_list[None, :, 2]
        inside = (next_along >= 0) & (next_along < LAT_X) & (next_across >= 0) & (next_across < LAT_Y) & (next_depth >= 0) & (next_depth < BZ)
        spot_ids = (jnp.clip(next_along, 0, LAT_X - 1) * LAT_Y + jnp.clip(next_across, 0, LAT_Y - 1)) * BZ + jnp.clip(next_depth, 0, BZ - 1)
        return jnp.where(inside, id_table[spot_ids], -1).astype(jnp.int32)
    moving_steps = jnp.asarray(VELOCITY[1:], jnp.int32)
    face_steps = jnp.asarray(VELOCITY[1:7], jnp.int32)
    return (beside_all(fluid_place, moving_steps, fluid_table), beside_all(fluid_place, face_steps, solid_table), beside_all(solid_place, face_steps, solid_table), beside_all(solid_place, face_steps, fluid_table))


def draw_fluid_nbr(key, part):
    tables = block_geometry(key)
    key = jax.random.fold_in(key, 1)
    return tables[0]


def draw_solid_face(key, part):
    tables = block_geometry(key)
    key = jax.random.fold_in(key, 2)
    return tables[1]


def draw_solid_nbr(key, part):
    tables = block_geometry(key)
    key = jax.random.fold_in(key, 3)
    return tables[2]


def draw_solid_fluid(key, part):
    tables = block_geometry(key)
    key = jax.random.fold_in(key, 4)
    return tables[3]


def draw_fluid_pop(key, part):
    key = jax.random.fold_in(key, 11)
    density_key, speed_key, noise_key = jax.random.split(key, 3)
    cell_shape = (NF_TOT, 1, CELLS)
    density = 0.8 + 0.4 * jax.random.uniform(density_key, cell_shape)
    spread = jnp.clip(0.12 * jax.random.normal(noise_key, (NF_TOT, 19, CELLS)), -0.35, 0.35)
    speed_all = 0.06 * jax.random.uniform(speed_key, (NF_TOT, 3, CELLS), minval=-1.0, maxval=1.0)
    speed_all = speed_all + jnp.asarray([0.05, 0.0, 0.0], jnp.float32).reshape(1, 3, 1)
    lattice = jnp.asarray(VELOCITY, jnp.float32)
    projected = speed_all[:, 0:1] * lattice[:, 0][None, :, None] + speed_all[:, 1:2] * lattice[:, 1][None, :, None] + speed_all[:, 2:3] * lattice[:, 2][None, :, None]
    square = jnp.sum(speed_all * speed_all, axis=1, keepdims=True)
    return (density * (1.0 + 3.0 * projected + 4.5 * projected * projected - 1.5 * square) * (1.0 + spread)).astype(jnp.float32)


def draw_heat_pop(key, part):
    key = jax.random.fold_in(key, 12)
    warm_key, noise_key = jax.random.split(key, 2)
    warmth = 0.3 + 0.6 * jax.random.uniform(warm_key, (NF_TOT, 1, CELLS))
    spread = 0.3 * jax.random.uniform(noise_key, (NF_TOT, 7, CELLS), minval=-1.0, maxval=1.0)
    return (warmth * (1.0 + spread)).astype(jnp.float32)


def draw_solid_temp(key, part):
    key = jax.random.fold_in(key, 13)
    rough = jax.random.uniform(key, (NS_TOT, CELLS))
    return (0.8 + 0.8 * rough).astype(jnp.float32)


def plant(values, rng, low, high):
    dims = values.shape
    spot = [jax.random.randint(jax.random.fold_in(rng, axis), (), 0, dims[axis]) for axis in range(len(dims))]
    values = values.at[tuple(spot)].set(low)
    longest = dims.index(max(dims))
    spot[longest] = (spot[longest] + 1) % dims[longest]
    return values.at[tuple(spot)].set(high)


def setup_inputs(seed: int = 0) -> dict:
    key_list = jax.random.split(jax.random.key(seed), 10)
    return {
        "fluid_pop": draw_fluid_pop(jax.random.fold_in(key_list[9], 71), 0),
        "heat_pop": draw_heat_pop(jax.random.fold_in(key_list[9], 71), 0),
        "solid_temp": draw_solid_temp(jax.random.fold_in(key_list[9], 71), 0),
        "material": plant(jax.random.randint(key_list[3], (NS_TOT, CELLS), 0, NMAT), jax.random.fold_in(key_list[3], 1), 0, NMAT - 1).astype(jnp.int32),
        "conductivity": jnp.clip(jnp.exp(jax.random.uniform(key_list[4], (NMAT,), jnp.float32, math.log(0.1), math.log(2.0))), 0.1, 2.0),
        "fluid_nbr": draw_fluid_nbr(jax.random.fold_in(key_list[9], 71), 0),
        "solid_face": draw_solid_face(jax.random.fold_in(key_list[9], 71), 0),
        "solid_nbr": draw_solid_nbr(jax.random.fold_in(key_list[9], 71), 0),
        "solid_fluid": draw_solid_fluid(jax.random.fold_in(key_list[9], 71), 0),
    }


VELOCITY = np.array([[0, 0, 0], [1, 0, 0], [-1, 0, 0], [0, 1, 0], [0, -1, 0], [0, 0, 1], [0, 0, -1],
                     [1, 1, 0], [-1, -1, 0], [1, -1, 0], [-1, 1, 0], [1, 0, 1], [-1, 0, -1],
                     [1, 0, -1], [-1, 0, 1], [0, 1, 1], [0, -1, -1], [0, 1, -1], [0, -1, 1]])
REVERSE = [0, 2, 1, 4, 3, 6, 5, 8, 7, 10, 9, 12, 11, 14, 13, 16, 15, 18, 17]
WEIGHT_FLOW = [1.0 / 3.0] + [1.0 / 18.0] * 6 + [1.0 / 36.0] * 12
WEIGHT_HEAT = [0.25] + [0.125] * 6
RELAX_FLOW = 1.25
RELAX_HEAT = 1.1
HEAT_CAPACITY = 1.0
FLUX_GAIN = 4.0


def face_plane(field_data, face_index, edge_cells):
    position = edge_cells - 1 if face_index % 2 == 0 else 0
    return jnp.take(field_data, position, axis=field_data.ndim - 3 + face_index // 2)


def all_faces(field_data, edge_cells):
    return jnp.stack([face_plane(field_data, face_index, edge_cells) for face_index in range(6)], axis=field_data.ndim - 3)


def padded(field_data):
    return jnp.pad(field_data, ((0, 0), (1, 1), (1, 1), (1, 1)))


def put_face(target, axis_index, position, values, edge_cells):
    index_list = [slice(None), slice(1, edge_cells + 1), slice(1, edge_cells + 1), slice(1, edge_cells + 1)]
    index_list[axis_index + 1] = position
    return target.at[tuple(index_list)].set(values)


def put_line(target, first_axis, first_at, second_axis, second_at, values, edge_cells):
    index_list = [slice(None), slice(1, edge_cells + 1), slice(1, edge_cells + 1), slice(1, edge_cells + 1)]
    index_list[first_axis + 1] = first_at
    index_list[second_axis + 1] = second_at
    return target.at[tuple(index_list)].set(values)


def moved(target, offsets, edge_cells):
    index_list = [slice(None)] + [slice(1 + int(offsets[axis_index]), 1 + int(offsets[axis_index]) + edge_cells) for axis_index in range(3)]
    return target[tuple(index_list)]


def collide(fluid_pop, heat_pop):
    flow_weight = jnp.asarray(WEIGHT_FLOW, fluid_pop.dtype)[:, None]
    heat_weight = jnp.asarray(WEIGHT_HEAT, heat_pop.dtype)[:, None]
    lattice = jnp.asarray(VELOCITY, fluid_pop.dtype)
    flow_part = fluid_pop * flow_weight
    heat_part = heat_pop * heat_weight
    density = jnp.sum(flow_part, axis=1, keepdims=True)
    speed_list = [jnp.sum(flow_part * lattice[:, axis_index][:, None], axis=1, keepdims=True) / density for axis_index in range(3)]
    projected = speed_list[0] * lattice[:, 0][:, None] + speed_list[1] * lattice[:, 1][:, None] + speed_list[2] * lattice[:, 2][:, None]
    square = speed_list[0] * speed_list[0] + speed_list[1] * speed_list[1] + speed_list[2] * speed_list[2]
    balance = flow_weight * density * (1.0 + 3.0 * projected + 4.5 * projected * projected - 1.5 * square)
    flow_star = flow_part - RELAX_FLOW * (flow_part - balance)
    warmth = jnp.sum(heat_part, axis=1, keepdims=True)
    heat_balance = heat_weight * warmth * (1.0 + 4.0 * projected[:, :7])
    heat_star = heat_part - RELAX_HEAT * (heat_part - heat_balance)
    return flow_star, heat_star


def stream_flow(flow_star, fetch_face, usable, edge_cells):
    result = [flow_star[:, 0]]
    for velocity_index in range(1, 19):
        offsets = VELOCITY[velocity_index]
        values = padded(flow_star[:, velocity_index])
        alive_mask = padded(jnp.ones_like(flow_star[:, 0]))
        moving = [axis_index for axis_index in range(3) if offsets[axis_index] != 0]
        for axis_index in moving:
            toward = 2 * axis_index + (0 if offsets[axis_index] > 0 else 1)
            source = toward ^ 1
            position = 0 if offsets[axis_index] > 0 else edge_cells + 1
            weight_in = usable[:, source][:, None, None]
            values = put_face(values, axis_index, position, fetch_face(source, toward, velocity_index) * weight_in, edge_cells)
            alive_mask = put_face(alive_mask, axis_index, position, weight_in, edge_cells)
        if len(moving) == 2:
            first_axis, second_axis = moving
            toward = 2 * first_axis + (0 if offsets[first_axis] > 0 else 1)
            source = REVERSE[velocity_index] - 1
            weight_in = usable[:, source][:, None]
            face_sheet = fetch_face(source, toward, velocity_index)
            row_at = edge_cells - 1 if offsets[second_axis] > 0 else 0
            if first_axis == 0 and second_axis == 1:
                edge_line = face_sheet[:, row_at, :]
            else:
                edge_line = face_sheet[:, :, row_at]
            first_at = 0 if offsets[first_axis] > 0 else edge_cells + 1
            second_at = 0 if offsets[second_axis] > 0 else edge_cells + 1
            values = put_line(values, first_axis, first_at, second_axis, second_at, edge_line * weight_in, edge_cells)
            alive_mask = put_line(alive_mask, first_axis, first_at, second_axis, second_at, weight_in, edge_cells)
        result.append(jnp.where(moved(alive_mask, -offsets, edge_cells) > 0.5, moved(values, -offsets, edge_cells),
                                flow_star[:, REVERSE[velocity_index]]))
    return jnp.stack(result, axis=1)


def stream_heat(heat_star, fetch_face, fluid_usable, solid_fetch, solid_usable, edge_cells):
    result = [heat_star[:, 0]]
    for velocity_index in range(1, 7):
        offsets = VELOCITY[velocity_index]
        axis_index = (velocity_index - 1) // 2
        toward = velocity_index - 1
        source = toward ^ 1
        position = 0 if offsets[axis_index] > 0 else edge_cells + 1
        fluid_in = fluid_usable[:, source][:, None, None]
        solid_in = solid_usable[:, source][:, None, None]
        empty_field = padded(jnp.zeros_like(heat_star[:, 0]))
        values = put_face(padded(heat_star[:, velocity_index]), axis_index, position, fetch_face(source, toward, velocity_index) * fluid_in, edge_cells)
        alive_mask = put_face(padded(jnp.ones_like(heat_star[:, 0])), axis_index, position, fluid_in, edge_cells)
        wall_heat = put_face(empty_field, axis_index, position, solid_fetch(source, toward) * solid_in, edge_cells)
        wall_mask = put_face(empty_field, axis_index, position, solid_in, edge_cells)
        bounced = heat_star[:, REVERSE[velocity_index]]
        shift = -offsets
        result.append(jnp.where(moved(alive_mask, shift, edge_cells) > 0.5, moved(values, shift, edge_cells),
                                jnp.where(moved(wall_mask, shift, edge_cells) > 0.5,
                                          2.0 * WEIGHT_HEAT[velocity_index] * moved(wall_heat, shift, edge_cells) - bounced, bounced)))
    return jnp.stack(result, axis=1)


def flux_planes(heat_star, solid_fetch, solid_usable, edge_cells):
    result = []
    for face_index in range(6):
        leaving_part = face_plane(heat_star[:, face_index + 1], face_index, edge_cells)
        temp_part = solid_fetch(face_index, face_index ^ 1)
        result.append(jnp.where(solid_usable[:, face_index][:, None, None] > 0.5,
                                2.0 * leaving_part - 2.0 * WEIGHT_HEAT[face_index + 1] * temp_part, 0.0))
    return jnp.stack(result, axis=1)


def heat_source(inflow, usable, solid_field, edge_cells):
    summed = jnp.zeros_like(solid_field)
    for face_index in range(6):
        index_list = [slice(None)] * 4
        index_list[face_index // 2 + 1] = edge_cells - 1 if face_index % 2 == 0 else 0
        summed = summed.at[tuple(index_list)].add(inflow(face_index) * usable[:, face_index][:, None, None])
    return summed


def conductances(solid_cond, ghost_of, edge_cells):
    widened = padded(solid_cond)
    for face_index in range(6):
        widened = put_face(widened, face_index // 2, edge_cells + 1 if face_index % 2 == 0 else 0, ghost_of(face_index), edge_cells)
    result = []
    for face_index in range(6):
        beside = moved(widened, VELOCITY[face_index + 1], edge_cells)
        result.append(2.0 * solid_cond * beside / (solid_cond + beside))
    return result


def operate(field_data, ghost_of, face_links, edge_cells):
    widened = padded(field_data)
    for face_index in range(6):
        widened = put_face(widened, face_index // 2, edge_cells + 1 if face_index % 2 == 0 else 0, ghost_of(face_index), edge_cells)
    summed = HEAT_CAPACITY * field_data
    for face_index in range(6):
        summed = summed + face_links[face_index] * (field_data - moved(widened, VELOCITY[face_index + 1], edge_cells))
    return summed


def chebyshev(start_field, source, face_links, first_ghost, share_faces, conductivity, edge_cells):
    largest = jnp.max(conductivity)
    center = HEAT_CAPACITY + 6.0 * largest
    radius = 6.0 * largest
    sigma_ratio = center / radius
    right_side = HEAT_CAPACITY * start_field + FLUX_GAIN * source
    residual = right_side - operate(start_field, first_ghost, face_links, edge_cells)
    update = residual / center
    factor = 1.0 / sigma_ratio
    result = start_field
    for sweep_index in range(ITERS):
        result = result + update
        if sweep_index + 1 < ITERS:
            residual = residual - operate(update, share_faces(update), face_links, edge_cells)
            factor_next = 1.0 / (2.0 * sigma_ratio - factor)
            update = factor_next * factor * update + (2.0 * factor_next / radius) * residual
            factor = factor_next
    return result


def ghost_from(pool_faces, slot_rows, usable):
    def ghost_of(face_index):
        return jnp.take(pool_faces[:, face_index ^ 1], slot_rows[:, face_index], axis=0) * usable[:, face_index][:, None, None]
    return ghost_of


def reference(fluid_pop, heat_pop, solid_temp, material, conductivity, fluid_nbr, solid_face, solid_nbr, solid_fluid):
    edge_cells = BLK
    fluid_count = fluid_pop.shape[0]
    solid_count = solid_temp.shape[0]
    cube = (edge_cells, edge_cells, edge_cells)
    flow_star, heat_star = collide(fluid_pop, heat_pop)
    flow_star = flow_star.reshape((fluid_count, 19) + cube)
    heat_star = heat_star.reshape((fluid_count, 7) + cube)
    solid_field = solid_temp.reshape((solid_count,) + cube)
    solid_cond = conductivity[material].reshape((solid_count,) + cube)

    def slots(id_table):
        return jnp.maximum(id_table, 0).astype(jnp.int32), (id_table >= 0).astype(fluid_pop.dtype)

    fluid_slot, fluid_usable = slots(fluid_nbr)
    wall_slot, wall_usable = slots(solid_face)
    solid_slot, solid_usable = slots(solid_nbr)
    across_slot, across_usable = slots(solid_fluid)
    flow_pool = all_faces(flow_star, edge_cells)
    heat_pool = all_faces(heat_star, edge_cells)
    temp_pool = all_faces(solid_field, edge_cells)
    cond_pool = all_faces(solid_cond, edge_cells)

    def solid_pick(neighbor, face_index):
        return jnp.take(temp_pool[:, face_index], wall_slot[:, neighbor], axis=0)

    flow_new = stream_flow(flow_star, lambda neighbor, face_index, velocity_index: jnp.take(
        flow_pool[:, velocity_index, face_index], fluid_slot[:, neighbor], axis=0), fluid_usable, edge_cells)
    heat_new = stream_heat(heat_star, lambda neighbor, face_index, velocity_index: jnp.take(
        heat_pool[:, velocity_index, face_index], fluid_slot[:, neighbor], axis=0), fluid_usable, solid_pick, wall_usable, edge_cells)
    flux_pool = flux_planes(heat_star, solid_pick, wall_usable, edge_cells)

    def inflow(face_index):
        return jnp.take(flux_pool[:, face_index ^ 1], across_slot[:, face_index], axis=0)

    source = heat_source(inflow, across_usable, solid_field, edge_cells)
    face_links = conductances(solid_cond, ghost_from(cond_pool, solid_slot, solid_usable), edge_cells)

    def share_faces(field_data):
        return ghost_from(all_faces(field_data, edge_cells), solid_slot, solid_usable)

    solid_new = chebyshev(solid_field, source, face_links, ghost_from(temp_pool, solid_slot, solid_usable),
                          share_faces, conductivity, edge_cells)
    flow_weight = jnp.asarray(WEIGHT_FLOW, fluid_pop.dtype)[:, None]
    heat_weight = jnp.asarray(WEIGHT_HEAT, heat_pop.dtype)[:, None]
    fluid_out = flow_new.reshape(fluid_count, 19, -1) / flow_weight
    heat_out = heat_new.reshape(fluid_count, 7, -1) / heat_weight
    return fluid_out, heat_out, solid_new.reshape(solid_count, -1)
```

```python
import functools

import jax
import jax.numpy as jnp
from jax import lax
from jax.experimental import pallas as pl
from jax.experimental.pallas import tpu as pltpu
from jax.sharding import PartitionSpec as P

MESH = pl.DeviceIdType.MESH
F32 = jnp.float32
E = 16
W = 256
H = 128
FB = 3
SB = 2
C = [
    (0, 0, 0),
    (1, 0, 0),
    (-1, 0, 0),
    (0, 1, 0),
    (0, -1, 0),
    (0, 0, 1),
    (0, 0, -1),
    (1, 1, 0),
    (-1, -1, 0),
    (1, -1, 0),
    (-1, 1, 0),
    (1, 0, 1),
    (-1, 0, -1),
    (1, 0, -1),
    (-1, 0, 1),
    (0, 1, 1),
    (0, -1, -1),
    (0, 1, -1),
    (0, -1, 1),
]
OPP = [0, 2, 1, 4, 3, 6, 5, 8, 7, 10, 9, 12, 11, 14, 13, 16, 15, 18, 17]
PX = ([1, 7, 9, 11, 13], [2, 8, 10, 12, 14])
PY = ([3, 7, 10, 15, 17], [4, 8, 9, 16, 18])
HEAT = 5
SIDES = [(1, 0), (-1, 0), (0, 1), (0, -1)]
CORNERS = [(1, 1), (1, -1), (-1, -1), (-1, 1)]
PEERS = SIDES + CORNERS
CORNER_SRC = [(0, 1, 1), (0, 2, 0), (1, 1, 0), (1, 2, 1)]
CORNER_OF = {7: 0, 9: 1, 8: 2, 10: 3}
N_COPY = 20


def lroll(v, s):
    n = v.shape[1]
    s = s % n
    return v if s == 0 else pltpu.roll(v, s, axis=1)


def rroll(v, s):
    n = v.shape[0]
    s = s % n
    return v if s == 0 else pltpu.roll(v, s, axis=0)


def lanes(shape):
    return lax.broadcasted_iota(jnp.int32, shape, 1)


def rows(shape):
    return lax.broadcasted_iota(jnp.int32, shape, 0)


def collide_tile(G, Q, b, rs, ls):
    def ld(p):
        return G[b, p, rs, ls]

    f = [ld(p) for p in range(19)]
    d = [None] * 19
    for p in (1, 3, 5, 7, 9, 11, 13, 15, 17):
        d[p] = f[p] - f[p + 1]
    s1 = ((f[1] + f[2]) + (f[3] + f[4])) + (f[5] + f[6])
    s2 = (((f[7] + f[8]) + (f[9] + f[10])) + ((f[11] + f[12]) + (f[13] + f[14]))) + (
        (f[15] + f[16]) + (f[17] + f[18])
    )
    rho = f[0] * (1.0 / 3.0) + s1 * (1.0 / 18.0) + s2 * (1.0 / 36.0)
    jx = d[1] * (1.0 / 18.0) + ((d[7] + d[9]) + (d[11] + d[13])) * (1.0 / 36.0)
    jy = d[3] * (1.0 / 18.0) + ((d[7] - d[9]) + (d[15] + d[17])) * (1.0 / 36.0)
    jz = d[5] * (1.0 / 18.0) + ((d[11] - d[13]) + (d[15] - d[17])) * (1.0 / 36.0)
    inv = 1.0 / rho
    u = (jx * inv, jy * inv, jz * inv)
    j = (jx, jy, jz)
    base = 1.25 * rho - 1.875 * (jx * u[0] + jy * u[1] + jz * u[2])
    G[b, 0, rs, ls] = base - 0.25 * f[0]
    cus = {}
    for p in (1, 3, 5, 7, 9, 11, 13, 15, 17):
        cj = None
        cu = None
        for a in range(3):
            s = C[p][a]
            if s == 0:
                continue
            if cj is None:
                cj, cu = j[a], u[a]
            elif s > 0:
                cj, cu = cj + j[a], cu + u[a]
            else:
                cj, cu = cj - j[a], cu - u[a]
        even = base + 5.625 * (cj * cu)
        odd = 3.75 * cj
        G[b, p, rs, ls] = (even + odd) - 0.25 * f[p]
        G[b, p + 1, rs, ls] = (even - odd) - 0.25 * f[p + 1]
        cus[p] = cu
    h = [Q[b, k, rs, ls] for k in range(7)]
    hs = ((h[1] + h[2]) + (h[3] + h[4])) + (h[5] + h[6])
    t11 = (h[0] * 0.25 + hs * 0.125) * 1.1
    t44 = 4.0 * t11
    Q[b, 0, rs, ls] = t11 - 0.1 * h[0]
    for k in (1, 3, 5):
        o = t44 * cus[k]
        Q[b, k, rs, ls] = (t11 + o) - 0.1 * h[k]
        Q[b, k + 1, rs, ls] = (t11 - o) - 0.1 * h[k + 1]


def kernel(
    nf,
    nc,
    fluid_in,
    heat_in,
    temp_in,
    mat_in,
    cond,
    nbr,
    wall,
    snbr,
    sflu,
    fluid_out,
    heat_out,
    solid_out,
    G,
    Q,
    GO,
    QO,
    T,
    M,
    KAP,
    TO,
    XS,
    XR,
    YS,
    YR,
    CR,
    XTS,
    XTR,
    YTS,
    YTR,
    DXS,
    DXR,
    DYS,
    DYR,
    in_sem,
    out_sem,
    send_sem,
    recv_sem,
):
    fl = lax.axis_index("flow")
    cr = lax.axis_index("cross")

    def peer(df, dc):
        return (lax.rem(fl + (df + nf), nf), lax.rem(cr + (dc + nc), nc))

    barrier = pltpu.get_barrier_semaphore()
    for df, dc in PEERS:
        pl.semaphore_signal(barrier, inc=1, device_id=peer(df, dc), device_id_type=MESH)

    def load(src, dst, sem):
        for x in range(E):
            pltpu.make_async_copy(
                src.at[..., pl.ds(W * x, W)], dst.at[..., x, :], sem
            ).start()

    def all_of(ref, sem):
        return pltpu.make_async_copy(ref, ref, sem)

    load(temp_in, T, in_sem.at[0])
    load(mat_in, M, in_sem.at[1])
    for b in range(FB):
        load(fluid_in.at[b], G.at[b], in_sem.at[2 + 2 * b])
        load(heat_in.at[b], Q.at[b], in_sem.at[3 + 2 * b])

    copies = {}

    def send(i, src, dst, df, dc):
        copies[i] = pltpu.make_async_remote_copy(
            src_ref=src,
            dst_ref=dst,
            send_sem=send_sem.at[i],
            recv_sem=recv_sem.at[i],
            device_id=peer(df, dc),
            device_id_type=MESH,
        )
        copies[i].start()

    wide = (E, W)
    lw = lanes(wide)
    rw = rows(wide)
    zw = jnp.bitwise_and(lw, E - 1)
    lh = lanes((E, H))
    group = jnp.right_shift(lh, 4)

    def base_of(df, dc):
        return (fl + df) * nc + (cr + dc)

    all_of(T, in_sem.at[0]).wait()
    all_of(M, in_sem.at[1]).wait()
    for s in range(SB):
        m = M[s]
        k = jnp.full(wide, cond[0], F32)
        for i in range(1, 8):
            k = jnp.where(m == i, cond[i], k)
        KAP[s] = k

    def pack_y(pieces, side):
        acc = None
        for g, v in enumerate(pieces):
            if side == 0:
                r = lroll(v[:, H:], E * g - (H - E))
            else:
                r = lroll(v[:, :H], E * g)
            acc = r if acc is None else jnp.where(group == g, r, acc)
        return acc

    for side in range(2):
        x = E - 1 if side == 0 else 0
        for s in range(SB):
            XTS[side, s, 0:1, :] = T[s, x : x + 1, :]
            XTS[side, s, 1:2, :] = KAP[s, x : x + 1, :]
        YTS[side] = pack_y([T[0], KAP[0], T[1], KAP[1]], side)

    pl.semaphore_wait(barrier, len(PEERS))
    for i, (df, dc) in enumerate(SIDES):
        side = i % 2
        if i < 2:
            send(i, XTS.at[side], XTR.at[side], df, dc)
        else:
            send(i, YTS.at[side], YTR.at[side], df, dc)

    for b in range(FB):
        all_of(G.at[b], in_sem.at[2 + 2 * b]).wait()
        all_of(Q.at[b], in_sem.at[3 + 2 * b]).wait()
        for xh in range(2):
            for yh in range(2):
                collide_tile(G, Q, b, pl.ds(8 * xh, 8), pl.ds(H * yh, H))
        for side in range(2):
            x = E - 1 if side == 0 else 0
            for r in range(5):
                XS[side, b, r : r + 1, :] = G[b, PX[side][r], x : x + 1, :]
            XS[side, b, HEAT : HEAT + 1, :] = Q[b, 1 + side, x : x + 1, :]
            YS[side, b] = pack_y(
                [G[b, PY[side][r]] for r in range(5)] + [Q[b, 3 + side]], side
            )

    for i, (df, dc) in enumerate(SIDES):
        side = i % 2
        if i < 2:
            send(4 + i, XS.at[side], XR.at[side], df, dc)
        else:
            send(4 + i, YS.at[side], YR.at[side], df, dc)
    for i, (df, dc) in enumerate(CORNERS):
        side, r, half = CORNER_SRC[i]
        send(
            8 + i,
            XS.at[side, :, pl.ds(r, 1), pl.ds(H * half, H)],
            CR.at[i],
            df,
            dc,
        )

    def slot(idv, base, n):
        return jnp.clip(idv - base * n, 0, n - 1)

    def unpack_group(v, g, lo):
        return lroll(v, -E * g) if lo else lroll(v, (H - E) - E * g)

    def widen(v, lo):
        return jnp.concatenate([v, v], axis=1)

    def pick(sel, a, b_):
        return jnp.where(jnp.full(a.shape, sel) == 0, a, b_)

    edges = [rw == E - 1, rw == 0, lw >= W - E, lw < E, zw == E - 1, zw == 0]

    def shifted(v, k):
        return [
            lambda: rroll(v, -1),
            lambda: rroll(v, 1),
            lambda: lroll(v, -E),
            lambda: lroll(v, E),
            lambda: lroll(v, -1),
            lambda: lroll(v, 1),
        ][k]()

    def step_base(k):
        return base_of(C[k + 1][0], C[k + 1][1])

    def z_ghost(v, k):
        return lroll(v, E - 1) if k == 4 else lroll(v, 1 - E)

    def solid_ghost(k, s, sl, q, field):
        if k < 2:
            return XTR[1 - k, sl, q : q + 1, :]
        if k < 4:
            v = YTR[1 - (k - 2)]
            lo = k == 3
            return widen(pick(sl, unpack_group(v, q, lo), unpack_group(v, 2 + q, lo)), lo)
        return z_ghost(field[1 - s], k)

    def heat_ghost(k, fsl):
        if k < 2:
            return XR[1 - k, fsl, HEAT : HEAT + 1, :]
        if k < 4:
            lo = k == 3
            return widen(unpack_group(YR[1 - (k - 2), fsl], HEAT, lo), lo)
        return z_ghost(Q[fsl, 6 if k == 4 else 5], k)

    for i in range(12):
        copies[i].wait_recv()

    kmax = cond[0]
    for i in range(1, 8):
        kmax = jnp.maximum(kmax, cond[i])
    radius = jnp.full((8, H), kmax * 6.0, F32)
    center = radius + 1.0
    sigma = center / radius

    def grow(v):
        v = jnp.concatenate([v, v], axis=0)
        return jnp.concatenate([v, v], axis=1)

    inv_center = grow(1.0 / center)
    rho0 = 1.0 / sigma
    rho1 = 1.0 / (2.0 * sigma - rho0)
    rho2 = 1.0 / (2.0 * sigma - rho1)
    coef = [
        (grow(rho1 * rho0), grow(2.0 * rho1 / radius)),
        (grow(rho2 * rho1), grow(2.0 * rho2 / radius)),
    ]

    sid = [[snbr[s, k] for k in range(6)] for s in range(SB)]
    fid = [[sflu[s, k] for k in range(6)] for s in range(SB)]
    ssl = [[slot(sid[s][k], step_base(k), SB) for k in range(6)] for s in range(SB)]
    links = []
    resid = []
    upd = []
    sol = []
    for s in range(SB):
        t = T[s]
        kap = KAP[s]
        acc = jnp.zeros(wide, F32)
        row = []
        for k in range(6):
            sl = ssl[s][k]
            live = jnp.full(wide, sid[s][k]) >= 0
            wet = jnp.full(wide, fid[s][k]) >= 0
            kb = jnp.where(edges[k], solid_ghost(k, s, sl, 1, KAP), shifted(kap, k))
            link = (2.0 * kap * kb) / (kap + kb)
            link = jnp.where(edges[k] & ~live, 0.0, link)
            row.append(link)
            tb = jnp.where(edges[k], solid_ghost(k, s, sl, 0, T), shifted(t, k))
            hb = heat_ghost(k, slot(fid[s][k], step_base(k), FB))
            wet_edge = edges[k] & wet
            acc = acc + jnp.where(wet_edge, 1.0, link) * (jnp.where(wet_edge, hb, tb) - t)
        links.append(row)
        d = acc * inv_center
        resid.append(acc)
        upd.append(d)
        sol.append(t + d)

    def share(n):
        for side in range(2):
            x = E - 1 if side == 0 else 0
            for s in range(SB):
                DXS[n, side, s : s + 1, :] = upd[s][x : x + 1, :]
            DYS[n, side] = pack_y(upd, side)
        for i, (df, dc) in enumerate(SIDES):
            side = i % 2
            if i < 2:
                send(12 + 4 * n + i, DXS.at[n, side], DXR.at[n, side], df, dc)
            else:
                send(12 + 4 * n + i, DYS.at[n, side], DYR.at[n, side], df, dc)

    def update_ghost(n, k, s, sl):
        if k < 2:
            v = DXR[n, 1 - k]
            return pick(sl, v[0:1], v[1:2])
        if k < 4:
            v = DYR[n, 1 - (k - 2)]
            lo = k == 3
            return widen(pick(sl, unpack_group(v, 0, lo), unpack_group(v, 1, lo)), lo)
        return z_ghost(upd[1 - s], k)

    def sweep(n):
        for i in range(4):
            copies[12 + 4 * n + i].wait_recv()
        fresh = []
        for s in range(SB):
            d = upd[s]
            acc = d
            for k in range(6):
                db = jnp.where(edges[k], update_ghost(n, k, s, ssl[s][k]), shifted(d, k))
                acc = acc + links[s][k] * (d - db)
            resid[s] = resid[s] - acc
            nd = coef[n][0] * d + coef[n][1] * resid[s]
            fresh.append(nd)
            sol[s] = sol[s] + nd
        for s in range(SB):
            upd[s] = fresh[s]

    share(0)

    def x_face(b, side):
        shape = (8, W)
        r8 = rows(shape)
        l8 = lanes(shape)
        z8 = jnp.bitwise_and(l8, E - 1)
        df = -1 if side == 0 else 1
        dirn = 2 if side == 0 else 1
        bf = base_of(df, 0)
        main_id = nbr[b, dirn - 1]
        a = XR[side, slot(main_id, bf, FB)]
        val = a
        ids = jnp.full(shape, main_id)
        for r, p in enumerate(PX[side]):
            _, cy, cz = C[p]
            if r == 0:
                continue
            src = OPP[p]
            cid = nbr[b, src - 1]
            if cy:
                corner = CR[CORNER_OF[p], slot(cid, base_of(df, -cy), FB)]
                corner = jnp.broadcast_to(corner, (8, H))
                corner = lroll(corner, E * cy)
                corner = jnp.concatenate([corner, corner], axis=1)
                edge = l8 < E if cy > 0 else l8 >= W - E
                cand = jnp.where(edge, corner, lroll(a, E * cy))
            else:
                other = XR[side, slot(cid, bf, FB)]
                edge = z8 == 0 if cz > 0 else z8 == E - 1
                cand = jnp.where(edge, lroll(other, -(E - 1) * cz), lroll(a, cz))
            val = jnp.where(r8 == r, cand, val)
            ids = jnp.where((r8 == r) & edge, jnp.full(shape, cid), ids)
        fall = XS[1 - side, b]
        wid = wall[b, dirn - 1]
        tw = XTR[side, slot(wid, bf, SB), 0:1, :]
        hot = (r8 == HEAT) & (jnp.full(shape, wid) >= 0)
        fall = jnp.where(hot, 2.0 * tw - fall, fall)
        return jnp.where(ids >= 0, val, fall)

    def y_face(b, side):
        shape = (E, H)
        zh = jnp.bitwise_and(lh, E - 1)
        dc = -1 if side == 0 else 1
        dirn = 4 if side == 0 else 3
        bf = base_of(0, dc)
        main_id = nbr[b, dirn - 1]
        a = YR[side, slot(main_id, bf, FB)]
        val = a
        ids = jnp.full(shape, main_id)
        for r, p in enumerate(PY[side]):
            cx, _, cz = C[p]
            if r == 0:
                continue
            if cx:
                val = jnp.where(group == r, rroll(a, cx), val)
                continue
            cid = nbr[b, OPP[p] - 1]
            other = YR[side, slot(cid, bf, FB)]
            edge = zh == 0 if cz > 0 else zh == E - 1
            cand = jnp.where(edge, lroll(other, -(E - 1) * cz), lroll(a, cz))
            val = jnp.where(group == r, cand, val)
            ids = jnp.where((group == r) & edge, jnp.full(shape, cid), ids)
        fall = YS[1 - side, b]
        wid = wall[b, dirn - 1]
        wsl = slot(wid, bf, SB)
        tv = YTR[side]
        tw = pick(wsl, lroll(tv, E * HEAT), lroll(tv, E * (HEAT - 2)))
        hot = (group == HEAT) & (jnp.full(shape, wid) >= 0)
        fall = jnp.where(hot, 2.0 * tw - fall, fall)
        return jnp.where(ids >= 0, val, fall)

    def stream(b):
        yf = [y_face(b, 0), y_face(b, 1)]

        def main(ref, p, q):
            cx, cy, cz = C[p]
            s = E * cy + cz
            out = lroll(rroll(ref[b, p], cx), s)
            if cz:
                back = ref[b, OPP[p]]
                adj = (b - cz) % FB
                if 0 <= b - cz < FB:
                    other = lroll(rroll(ref[adj, p], cx), E * cy - (E - 1) * cz)
                    zid = nbr[b, (6 if cz > 0 else 5) - 1]
                else:
                    other = None
                if ref is Q:
                    wid = wall[b, (6 if cz > 0 else 5) - 1]
                    tw = lroll(T[slot(wid, base_of(0, 0), SB)], -(E - 1) * cz)
                    back = jnp.where(jnp.full(wide, wid) >= 0, 2.0 * tw - back, back)
                if other is not None:
                    back = jnp.where(jnp.full(wide, zid) >= 0, other, back)
                edge = zw == 0 if cz > 0 else zw == E - 1
                out = jnp.where(edge, back, out)
            if cy:
                lo = cy > 0
                v = unpack_group(yf[0 if lo else 1], q, lo)
                if lo:
                    out = jnp.concatenate(
                        [jnp.where(lh < E, v, out[:, :H]), out[:, H:]], axis=1
                    )
                else:
                    out = jnp.concatenate(
                        [out[:, :H], jnp.where(lh >= H - E, v, out[:, H:])], axis=1
                    )
            return out

        GO[b, 0] = G[b, 0]
        QO[b, 0] = Q[b, 0]
        for p in range(1, 19):
            cy = C[p][1]
            q = PY[0 if cy > 0 else 1].index(p) if cy else None
            GO[b, p] = main(G, p, q)
        for p in range(1, 7):
            QO[b, p] = main(Q, p, HEAT)
        for side in range(2):
            xf = x_face(b, side)
            x = 0 if side == 0 else E - 1
            for r, p in enumerate(PX[side]):
                GO[b, p, x : x + 1, :] = xf[r : r + 1]
            QO[b, 1 + side, x : x + 1, :] = xf[HEAT : HEAT + 1]

    def put(src, dst, sem):
        for x in range(E):
            pltpu.make_async_copy(
                src.at[..., x, :], dst.at[..., pl.ds(W * x, W)], sem
            ).start()

    def finish(b):
        stream(b)
        put(GO.at[b], fluid_out.at[b], out_sem.at[2 * b])
        put(QO.at[b], heat_out.at[b], out_sem.at[2 * b + 1])

    finish(0)
    sweep(0)
    share(1)
    finish(1)
    sweep(1)
    for s in range(SB):
        TO[s] = sol[s]
    put(TO, solid_out, out_sem.at[6])
    finish(2)

    for b in range(FB):
        all_of(GO.at[b], out_sem.at[2 * b]).wait()
        all_of(QO.at[b], out_sem.at[2 * b + 1]).wait()
    all_of(TO, out_sem.at[6]).wait()
    for i in range(N_COPY):
        copies[i].wait_send()


def body(nf, nc, fluid_pop, heat_pop, solid_temp, material, cond, nbr, wall, snbr, sflu):
    hbm = pl.BlockSpec(memory_space=pl.ANY)
    smem = pl.BlockSpec(memory_space=pltpu.SMEM)

    def vm(*shape):
        return pltpu.VMEM(shape, F32)

    return pl.pallas_call(
        functools.partial(kernel, nf, nc),
        out_shape=(
            jax.ShapeDtypeStruct(fluid_pop.shape, F32),
            jax.ShapeDtypeStruct(heat_pop.shape, F32),
            jax.ShapeDtypeStruct(solid_temp.shape, F32),
        ),
        in_specs=[hbm] * 4 + [smem] * 5,
        out_specs=(hbm, hbm, hbm),
        scratch_shapes=[
            vm(FB, 19, E, W),
            vm(FB, 7, E, W),
            vm(FB, 19, E, W),
            vm(FB, 7, E, W),
            vm(SB, E, W),
            pltpu.VMEM((SB, E, W), jnp.int32),
            vm(SB, E, W),
            vm(SB, E, W),
            vm(2, FB, 8, W),
            vm(2, FB, 8, W),
            vm(2, FB, E, H),
            vm(2, FB, E, H),
            vm(4, FB, 1, H),
            vm(2, SB, 2, W),
            vm(2, SB, 2, W),
            vm(2, E, H),
            vm(2, E, H),
            vm(2, 2, SB, W),
            vm(2, 2, SB, W),
            vm(2, 2, E, H),
            vm(2, 2, E, H),
            pltpu.SemaphoreType.DMA((8,)),
            pltpu.SemaphoreType.DMA((7,)),
            pltpu.SemaphoreType.DMA((N_COPY,)),
            pltpu.SemaphoreType.DMA((N_COPY,)),
        ],
        compiler_params=pltpu.CompilerParams(
            collective_id=0, has_side_effects=True, vmem_limit_bytes=32 * 1024 * 1024
        ),
    )(fluid_pop, heat_pop, solid_temp, material, cond, nbr, wall, snbr, sflu)


def solution(mesh):
    both = ("flow", "cross")
    in_specs = (
        P(both, None, None),
        P(both, None, None),
        P(both, None),
        P(both, None),
        P(),
        P(both, None),
        P(both, None),
        P(both, None),
        P(both, None),
    )
    out_specs = (P(both, None, None), P(both, None, None), P(both, None))
    return jax.shard_map(
        functools.partial(body, mesh.shape["flow"], mesh.shape["cross"]),
        mesh=mesh,
        in_specs=in_specs,
        out_specs=out_specs,
        check_vma=False,
    )
```

```python
import functools

import jax
import jax.numpy as jnp
from jax import lax
from jax.experimental import pallas as pl
from jax.experimental.pallas import tpu as pltpu
from jax.sharding import PartitionSpec as P

MESH = pl.DeviceIdType.MESH
F32 = jnp.float32
E = 16
W = 256
H = 128
FB = 3
SB = 2
C = [
    (0, 0, 0),
    (1, 0, 0),
    (-1, 0, 0),
    (0, 1, 0),
    (0, -1, 0),
    (0, 0, 1),
    (0, 0, -1),
    (1, 1, 0),
    (-1, -1, 0),
    (1, -1, 0),
    (-1, 1, 0),
    (1, 0, 1),
    (-1, 0, -1),
    (1, 0, -1),
    (-1, 0, 1),
    (0, 1, 1),
    (0, -1, -1),
    (0, 1, -1),
    (0, -1, 1),
]
OPP = [0, 2, 1, 4, 3, 6, 5, 8, 7, 10, 9, 12, 11, 14, 13, 16, 15, 18, 17]
PX = ([1, 7, 9, 11, 13], [2, 8, 10, 12, 14])
PY = ([3, 7, 10, 15, 17], [4, 8, 9, 16, 18])
HEAT = 5
SIDES = [(1, 0), (-1, 0), (0, 1), (0, -1)]
CORNERS = [(1, 1), (1, -1), (-1, -1), (-1, 1)]
PEERS = SIDES + CORNERS
CORNER_SRC = [(0, 1, 1), (0, 2, 0), (1, 1, 0), (1, 2, 1)]
CORNER_OF = {7: 0, 9: 1, 8: 2, 10: 3}
N_COPY = 20


def lroll(v, s):
    n = v.shape[1]
    s = s % n
    return v if s == 0 else pltpu.roll(v, s, axis=1)


def rroll(v, s):
    n = v.shape[0]
    s = s % n
    return v if s == 0 else pltpu.roll(v, s, axis=0)


def lanes(shape):
    return lax.broadcasted_iota(jnp.int32, shape, 1)


def rows(shape):
    return lax.broadcasted_iota(jnp.int32, shape, 0)


def collide_tile(G, Q, b, rs, ls):
    def ld(p):
        return G[b, p, rs, ls]

    f = [ld(p) for p in range(19)]
    d = [None] * 19
    for p in (1, 3, 5, 7, 9, 11, 13, 15, 17):
        d[p] = f[p] - f[p + 1]
    s1 = ((f[1] + f[2]) + (f[3] + f[4])) + (f[5] + f[6])
    s2 = (((f[7] + f[8]) + (f[9] + f[10])) + ((f[11] + f[12]) + (f[13] + f[14]))) + (
        (f[15] + f[16]) + (f[17] + f[18])
    )
    rho = f[0] * (1.0 / 3.0) + s1 * (1.0 / 18.0) + s2 * (1.0 / 36.0)
    jx = d[1] * (1.0 / 18.0) + ((d[7] + d[9]) + (d[11] + d[13])) * (1.0 / 36.0)
    jy = d[3] * (1.0 / 18.0) + ((d[7] - d[9]) + (d[15] + d[17])) * (1.0 / 36.0)
    jz = d[5] * (1.0 / 18.0) + ((d[11] - d[13]) + (d[15] - d[17])) * (1.0 / 36.0)
    inv = 1.0 / rho
    u = (jx * inv, jy * inv, jz * inv)
    j = (jx, jy, jz)
    base = 1.25 * rho - 1.875 * (jx * u[0] + jy * u[1] + jz * u[2])
    G[b, 0, rs, ls] = base - 0.25 * f[0]
    cus = {}
    for p in (1, 3, 5, 7, 9, 11, 13, 15, 17):
        cj = None
        cu = None
        for a in range(3):
            s = C[p][a]
            if s == 0:
                continue
            if cj is None:
                cj, cu = j[a], u[a]
            elif s > 0:
                cj, cu = cj + j[a], cu + u[a]
            else:
                cj, cu = cj - j[a], cu - u[a]
        even = base + 5.625 * (cj * cu)
        odd = 3.75 * cj
        G[b, p, rs, ls] = (even + odd) - 0.25 * f[p]
        G[b, p + 1, rs, ls] = (even - odd) - 0.25 * f[p + 1]
        cus[p] = cu
    h = [Q[b, k, rs, ls] for k in range(7)]
    hs = ((h[1] + h[2]) + (h[3] + h[4])) + (h[5] + h[6])
    t11 = (h[0] * 0.25 + hs * 0.125) * 1.1
    t44 = 4.0 * t11
    Q[b, 0, rs, ls] = t11 - 0.1 * h[0]
    for k in (1, 3, 5):
        o = t44 * cus[k]
        Q[b, k, rs, ls] = (t11 + o) - 0.1 * h[k]
        Q[b, k + 1, rs, ls] = (t11 - o) - 0.1 * h[k + 1]


def kernel(
    nf,
    nc,
    fluid_in,
    heat_in,
    temp_in,
    mat_in,
    cond_in,
    nbr_in,
    wall_in,
    snbr_in,
    sflu_in,
    fluid_out,
    heat_out,
    solid_out,
    G,
    Q,
    GO,
    QO,
    T,
    M,
    KAP,
    TO,
    XS,
    XR,
    YS,
    YR,
    CR,
    XTS,
    XTR,
    YTS,
    YTR,
    DXS,
    DXR,
    DYS,
    DYR,
    cond,
    nbr,
    wall,
    snbr,
    sflu,
    in_sem,
    out_sem,
    send_sem,
    recv_sem,
):
    fl = lax.axis_index("flow")
    cr = lax.axis_index("cross")

    inside = {-1: (fl > 0, cr > 0), 0: (True, True), 1: (fl < nf - 1, cr < nc - 1)}

    def near(df, dc):
        a, b = inside[df][0], inside[dc][1]
        if df == 0:
            return b
        return a if dc == 0 else jnp.logical_and(a, b)

    barrier = pltpu.get_barrier_semaphore()
    for df, dc in PEERS:

        @pl.when(near(df, dc))
        def _():
            pl.semaphore_signal(
                barrier, inc=1, device_id=(fl + df, cr + dc), device_id_type=MESH
            )

    nx = 2 - (fl == 0).astype(jnp.int32) - (fl == nf - 1).astype(jnp.int32)
    ny = 2 - (cr == 0).astype(jnp.int32) - (cr == nc - 1).astype(jnp.int32)
    n_peers = nx + ny + nx * ny

    def load(src, dst, sem):
        for x in range(E):
            pltpu.make_async_copy(
                src.at[..., pl.ds(W * x, W)], dst.at[..., x, :], sem
            ).start()

    def all_of(ref, sem):
        return pltpu.make_async_copy(ref, ref, sem)

    tables = [
        (cond_in, cond, 8),
        (nbr_in, nbr, 9),
        (wall_in, wall, 10),
        (snbr_in, snbr, 11),
        (sflu_in, sflu, 12),
    ]
    tables = [pltpu.make_async_copy(a, b, in_sem.at[i]) for a, b, i in tables]
    for c in tables:
        c.start()
    load(temp_in, T, in_sem.at[0])
    load(mat_in, M, in_sem.at[1])
    for b in range(FB):
        load(fluid_in.at[b], G.at[b], in_sem.at[2 + 2 * b])
        load(heat_in.at[b], Q.at[b], in_sem.at[3 + 2 * b])

    copies = {}
    steps = {}

    def send(i, src, dst, df, dc):
        copies[i] = pltpu.make_async_remote_copy(
            src_ref=src,
            dst_ref=dst,
            send_sem=send_sem.at[i],
            recv_sem=recv_sem.at[i],
            device_id=(fl + df, cr + dc),
            device_id_type=MESH,
        )
        steps[i] = (df, dc)

        @pl.when(near(df, dc))
        def _():
            copies[i].start()

    def received(i):
        @pl.when(near(-steps[i][0], -steps[i][1]))
        def _():
            copies[i].wait_recv()

    wide = (E, W)
    lw = lanes(wide)
    rw = rows(wide)
    zw = jnp.bitwise_and(lw, E - 1)
    lh = lanes((E, H))
    group = jnp.right_shift(lh, 4)

    def base_of(df, dc):
        return (fl + df) * nc + (cr + dc)

    with jax.named_scope("wait_solid"):
        for c in tables:
            c.wait()
        all_of(T, in_sem.at[0]).wait()
        all_of(M, in_sem.at[1]).wait()
    for s in range(SB):
        m = M[s]
        k = jnp.full(wide, cond[0], F32)
        for i in range(1, 8):
            k = jnp.where(m == i, cond[i], k)
        KAP[s] = k

    def pack_y(pieces, side):
        acc = None
        for g, v in enumerate(pieces):
            if side == 0:
                r = lroll(v[:, H:], E * g - (H - E))
            else:
                r = lroll(v[:, :H], E * g)
            acc = r if acc is None else jnp.where(group == g, r, acc)
        return acc

    for side in range(2):
        x = E - 1 if side == 0 else 0
        for s in range(SB):
            XTS[side, s, 0:1, :] = T[s, x : x + 1, :]
            XTS[side, s, 1:2, :] = KAP[s, x : x + 1, :]
        YTS[side] = pack_y([T[0], KAP[0], T[1], KAP[1]], side)

    with jax.named_scope("entry_barrier"):
        pl.semaphore_wait(barrier, n_peers)
    for i, (df, dc) in enumerate(SIDES):
        side = i % 2
        if i < 2:
            send(i, XTS.at[side], XTR.at[side], df, dc)
        else:
            send(i, YTS.at[side], YTR.at[side], df, dc)

    for b in range(FB):
        with jax.named_scope("wait_pops"):
            all_of(G.at[b], in_sem.at[2 + 2 * b]).wait()
            all_of(Q.at[b], in_sem.at[3 + 2 * b]).wait()
        with jax.named_scope("collide"):
            for xh in range(2):
                for yh in range(2):
                    collide_tile(G, Q, b, pl.ds(8 * xh, 8), pl.ds(H * yh, H))
        for side in range(2):
            x = E - 1 if side == 0 else 0
            for r in range(5):
                XS[side, b, r : r + 1, :] = G[b, PX[side][r], x : x + 1, :]
            XS[side, b, HEAT : HEAT + 1, :] = Q[b, 1 + side, x : x + 1, :]
            YS[side, b] = pack_y(
                [G[b, PY[side][r]] for r in range(5)] + [Q[b, 3 + side]], side
            )

    for i, (df, dc) in enumerate(SIDES):
        side = i % 2
        if i < 2:
            send(4 + i, XS.at[side], XR.at[side], df, dc)
        else:
            send(4 + i, YS.at[side], YR.at[side], df, dc)
    for i, (df, dc) in enumerate(CORNERS):
        side, r, half = CORNER_SRC[i]
        send(
            8 + i,
            XS.at[side, :, pl.ds(r, 1), pl.ds(H * half, H)],
            CR.at[i],
            df,
            dc,
        )

    def slot(idv, base, n):
        return jnp.clip(idv - base * n, 0, n - 1)

    def unpack_group(v, g, lo):
        return lroll(v, -E * g) if lo else lroll(v, (H - E) - E * g)

    def widen(v, lo):
        return jnp.concatenate([v, v], axis=1)

    def pick(sel, a, b_):
        return jnp.where(jnp.full(a.shape, sel) == 0, a, b_)

    edges = [rw == E - 1, rw == 0, lw >= W - E, lw < E, zw == E - 1, zw == 0]

    def shifted(v, k):
        return [
            lambda: rroll(v, -1),
            lambda: rroll(v, 1),
            lambda: lroll(v, -E),
            lambda: lroll(v, E),
            lambda: lroll(v, -1),
            lambda: lroll(v, 1),
        ][k]()

    def step_base(k):
        return base_of(C[k + 1][0], C[k + 1][1])

    def z_ghost(v, k):
        return lroll(v, E - 1) if k == 4 else lroll(v, 1 - E)

    def solid_ghost(k, s, sl, q, field):
        if k < 2:
            return XTR[1 - k, sl, q : q + 1, :]
        if k < 4:
            v = YTR[1 - (k - 2)]
            lo = k == 3
            return widen(pick(sl, unpack_group(v, q, lo), unpack_group(v, 2 + q, lo)), lo)
        return z_ghost(field[1 - s], k)

    def heat_ghost(k, fsl):
        if k < 2:
            return XR[1 - k, fsl, HEAT : HEAT + 1, :]
        if k < 4:
            lo = k == 3
            return widen(unpack_group(YR[1 - (k - 2), fsl], HEAT, lo), lo)
        return z_ghost(Q[fsl, 6 if k == 4 else 5], k)

    with jax.named_scope("wait_faces"):
        for i in range(12):
            received(i)

    kmax = cond[0]
    for i in range(1, 8):
        kmax = jnp.maximum(kmax, cond[i])
    radius = jnp.full((8, H), kmax * 6.0, F32)
    center = radius + 1.0
    sigma = center / radius

    def grow(v):
        v = jnp.concatenate([v, v], axis=0)
        return jnp.concatenate([v, v], axis=1)

    inv_center = grow(1.0 / center)
    rho0 = 1.0 / sigma
    rho1 = 1.0 / (2.0 * sigma - rho0)
    rho2 = 1.0 / (2.0 * sigma - rho1)
    coef = [
        (grow(rho1 * rho0), grow(2.0 * rho1 / radius)),
        (grow(rho2 * rho1), grow(2.0 * rho2 / radius)),
    ]

    sid = [[snbr[s, k] for k in range(6)] for s in range(SB)]
    fid = [[sflu[s, k] for k in range(6)] for s in range(SB)]
    ssl = [[slot(sid[s][k], step_base(k), SB) for k in range(6)] for s in range(SB)]
    links = []
    resid = []
    upd = []
    sol = []
    for s in range(SB):
        t = T[s]
        kap = KAP[s]
        acc = jnp.zeros(wide, F32)
        row = []
        for k in range(6):
            sl = ssl[s][k]
            live = jnp.full(wide, sid[s][k]) >= 0
            wet = jnp.full(wide, fid[s][k]) >= 0
            kb = jnp.where(edges[k], solid_ghost(k, s, sl, 1, KAP), shifted(kap, k))
            link = (2.0 * kap * kb) / (kap + kb)
            link = jnp.where(edges[k] & ~live, 0.0, link)
            row.append(link)
            tb = jnp.where(edges[k], solid_ghost(k, s, sl, 0, T), shifted(t, k))
            hb = heat_ghost(k, slot(fid[s][k], step_base(k), FB))
            tb = jnp.where(edges[k] & ~live, t, tb)
            wet_edge = edges[k] & wet
            acc = acc + jnp.where(wet_edge, 1.0, link) * (jnp.where(wet_edge, hb, tb) - t)
        links.append(row)
        d = acc * inv_center
        resid.append(acc)
        upd.append(d)
        sol.append(t + d)

    def share(n):
        for side in range(2):
            x = E - 1 if side == 0 else 0
            for s in range(SB):
                DXS[n, side, s : s + 1, :] = upd[s][x : x + 1, :]
            DYS[n, side] = pack_y(upd, side)
        for i, (df, dc) in enumerate(SIDES):
            side = i % 2
            if i < 2:
                send(12 + 4 * n + i, DXS.at[n, side], DXR.at[n, side], df, dc)
            else:
                send(12 + 4 * n + i, DYS.at[n, side], DYR.at[n, side], df, dc)

    def update_ghost(n, k, s, sl):
        if k < 2:
            v = DXR[n, 1 - k]
            return pick(sl, v[0:1], v[1:2])
        if k < 4:
            v = DYR[n, 1 - (k - 2)]
            lo = k == 3
            return widen(pick(sl, unpack_group(v, 0, lo), unpack_group(v, 1, lo)), lo)
        return z_ghost(upd[1 - s], k)

    def sweep(n):
        with jax.named_scope("wait_updates"):
            for i in range(4):
                received(12 + 4 * n + i)
        fresh = []
        for s in range(SB):
            d = upd[s]
            acc = d
            for k in range(6):
                ghost = update_ghost(n, k, s, ssl[s][k])
                ghost = jnp.where(jnp.full(ghost.shape, sid[s][k]) >= 0, ghost, 0.0)
                db = jnp.where(edges[k], ghost, shifted(d, k))
                acc = acc + links[s][k] * (d - db)
            resid[s] = resid[s] - acc
            nd = coef[n][0] * d + coef[n][1] * resid[s]
            fresh.append(nd)
            sol[s] = sol[s] + nd
        for s in range(SB):
            upd[s] = fresh[s]

    share(0)

    def x_face(b, side):
        shape = (8, W)
        r8 = rows(shape)
        l8 = lanes(shape)
        z8 = jnp.bitwise_and(l8, E - 1)
        df = -1 if side == 0 else 1
        dirn = 2 if side == 0 else 1
        bf = base_of(df, 0)
        main_id = nbr[b, dirn - 1]
        a = XR[side, slot(main_id, bf, FB)]
        val = a
        ids = jnp.full(shape, main_id)
        for r, p in enumerate(PX[side]):
            _, cy, cz = C[p]
            if r == 0:
                continue
            src = OPP[p]
            cid = nbr[b, src - 1]
            if cy:
                corner = CR[CORNER_OF[p], slot(cid, base_of(df, -cy), FB)]
                corner = jnp.broadcast_to(corner, (8, H))
                corner = lroll(corner, E * cy)
                corner = jnp.concatenate([corner, corner], axis=1)
                edge = l8 < E if cy > 0 else l8 >= W - E
                cand = jnp.where(edge, corner, lroll(a, E * cy))
            else:
                other = XR[side, slot(cid, bf, FB)]
                edge = z8 == 0 if cz > 0 else z8 == E - 1
                cand = jnp.where(edge, lroll(other, -(E - 1) * cz), lroll(a, cz))
            val = jnp.where(r8 == r, cand, val)
            ids = jnp.where((r8 == r) & edge, jnp.full(shape, cid), ids)
        fall = XS[1 - side, b]
        wid = wall[b, dirn - 1]
        tw = XTR[side, slot(wid, bf, SB), 0:1, :]
        hot = (r8 == HEAT) & (jnp.full(shape, wid) >= 0)
        fall = jnp.where(hot, 2.0 * tw - fall, fall)
        return jnp.where(ids >= 0, val, fall)

    def y_face(b, side):
        shape = (E, H)
        zh = jnp.bitwise_and(lh, E - 1)
        dc = -1 if side == 0 else 1
        dirn = 4 if side == 0 else 3
        bf = base_of(0, dc)
        main_id = nbr[b, dirn - 1]
        a = YR[side, slot(main_id, bf, FB)]
        val = a
        ids = jnp.full(shape, main_id)
        for r, p in enumerate(PY[side]):
            cx, _, cz = C[p]
            if r == 0:
                continue
            if cx:
                val = jnp.where(group == r, rroll(a, cx), val)
                continue
            cid = nbr[b, OPP[p] - 1]
            other = YR[side, slot(cid, bf, FB)]
            edge = zh == 0 if cz > 0 else zh == E - 1
            cand = jnp.where(edge, lroll(other, -(E - 1) * cz), lroll(a, cz))
            val = jnp.where(group == r, cand, val)
            ids = jnp.where((group == r) & edge, jnp.full(shape, cid), ids)
        fall = YS[1 - side, b]
        wid = wall[b, dirn - 1]
        wsl = slot(wid, bf, SB)
        tv = YTR[side]
        tw = pick(wsl, lroll(tv, E * HEAT), lroll(tv, E * (HEAT - 2)))
        hot = (group == HEAT) & (jnp.full(shape, wid) >= 0)
        fall = jnp.where(hot, 2.0 * tw - fall, fall)
        return jnp.where(ids >= 0, val, fall)

    def stream(b):
        yf = [y_face(b, 0), y_face(b, 1)]

        def main(ref, p, q):
            cx, cy, cz = C[p]
            s = E * cy + cz
            out = lroll(rroll(ref[b, p], cx), s)
            if cz:
                back = ref[b, OPP[p]]
                adj = (b - cz) % FB
                if 0 <= b - cz < FB:
                    other = lroll(rroll(ref[adj, p], cx), E * cy - (E - 1) * cz)
                    zid = nbr[b, (6 if cz > 0 else 5) - 1]
                else:
                    other = None
                if ref is Q:
                    wid = wall[b, (6 if cz > 0 else 5) - 1]
                    tw = lroll(T[slot(wid, base_of(0, 0), SB)], -(E - 1) * cz)
                    back = jnp.where(jnp.full(wide, wid) >= 0, 2.0 * tw - back, back)
                if other is not None:
                    back = jnp.where(jnp.full(wide, zid) >= 0, other, back)
                edge = zw == 0 if cz > 0 else zw == E - 1
                out = jnp.where(edge, back, out)
            if cy:
                lo = cy > 0
                v = unpack_group(yf[0 if lo else 1], q, lo)
                if lo:
                    out = jnp.concatenate(
                        [jnp.where(lh < E, v, out[:, :H]), out[:, H:]], axis=1
                    )
                else:
                    out = jnp.concatenate(
                        [out[:, :H], jnp.where(lh >= H - E, v, out[:, H:])], axis=1
                    )
            return out

        GO[b, 0] = G[b, 0]
        QO[b, 0] = Q[b, 0]
        for p in range(1, 19):
            cy = C[p][1]
            q = PY[0 if cy > 0 else 1].index(p) if cy else None
            GO[b, p] = main(G, p, q)
        for p in range(1, 7):
            QO[b, p] = main(Q, p, HEAT)
        for side in range(2):
            xf = x_face(b, side)
            x = 0 if side == 0 else E - 1
            for r, p in enumerate(PX[side]):
                GO[b, p, x : x + 1, :] = xf[r : r + 1]
            QO[b, 1 + side, x : x + 1, :] = xf[HEAT : HEAT + 1]

    def put(src, dst, sem):
        for x in range(E):
            pltpu.make_async_copy(
                src.at[..., x, :], dst.at[..., pl.ds(W * x, W)], sem
            ).start()

    def finish(b):
        with jax.named_scope("stream"):
            stream(b)
        put(GO.at[b], fluid_out.at[b], out_sem.at[2 * b])
        put(QO.at[b], heat_out.at[b], out_sem.at[2 * b + 1])

    finish(0)
    sweep(0)
    share(1)
    finish(1)
    sweep(1)
    for s in range(SB):
        TO[s] = sol[s]
    put(TO, solid_out, out_sem.at[6])
    finish(2)

    with jax.named_scope("wait_stores"):
        for b in range(FB):
            all_of(GO.at[b], out_sem.at[2 * b]).wait()
            all_of(QO.at[b], out_sem.at[2 * b + 1]).wait()
        all_of(TO, out_sem.at[6]).wait()
    for i in range(N_COPY):

        @pl.when(near(*steps[i]))
        def _():
            copies[i].wait_send()


def body(nf, nc, fluid_pop, heat_pop, solid_temp, material, cond, nbr, wall, snbr, sflu):
    hbm = pl.BlockSpec(memory_space=pltpu.HBM)

    def vm(*shape):
        return pltpu.VMEM(shape, F32)

    return pl.pallas_call(
        functools.partial(kernel, nf, nc),
        out_shape=(
            jax.ShapeDtypeStruct(fluid_pop.shape, F32),
            jax.ShapeDtypeStruct(heat_pop.shape, F32),
            jax.ShapeDtypeStruct(solid_temp.shape, F32),
        ),
        in_specs=[hbm] * 9,
        out_specs=(hbm, hbm, hbm),
        scratch_shapes=[
            vm(FB, 19, E, W),
            vm(FB, 7, E, W),
            vm(FB, 19, E, W),
            vm(FB, 7, E, W),
            vm(SB, E, W),
            pltpu.VMEM((SB, E, W), jnp.int32),
            vm(SB, E, W),
            vm(SB, E, W),
            vm(2, FB, 8, W),
            vm(2, FB, 8, W),
            vm(2, FB, E, H),
            vm(2, FB, E, H),
            vm(4, FB, 1, H),
            vm(2, SB, 2, W),
            vm(2, SB, 2, W),
            vm(2, E, H),
            vm(2, E, H),
            vm(2, 2, SB, W),
            vm(2, 2, SB, W),
            vm(2, 2, E, H),
            vm(2, 2, E, H),
            pltpu.SMEM(cond.shape, F32),
            pltpu.SMEM(nbr.shape, jnp.int32),
            pltpu.SMEM(wall.shape, jnp.int32),
            pltpu.SMEM(snbr.shape, jnp.int32),
            pltpu.SMEM(sflu.shape, jnp.int32),
            pltpu.SemaphoreType.DMA((13,)),
            pltpu.SemaphoreType.DMA((7,)),
            pltpu.SemaphoreType.DMA((N_COPY,)),
            pltpu.SemaphoreType.DMA((N_COPY,)),
        ],
        compiler_params=pltpu.CompilerParams(
            collective_id=0, has_side_effects=True, vmem_limit_bytes=60 * 1024 * 1024
        ),
    )(fluid_pop, heat_pop, solid_temp, material, cond, nbr, wall, snbr, sflu)


def solution(mesh):
    both = ("flow", "cross")
    in_specs = (
        P(both, None, None),
        P(both, None, None),
        P(both, None),
        P(both, None),
        P(),
        P(both, None),
        P(both, None),
        P(both, None),
        P(both, None),
    )
    out_specs = (P(both, None, None), P(both, None, None), P(both, None))
    return jax.shard_map(
        functools.partial(body, mesh.shape["flow"], mesh.shape["cross"]),
        mesh=mesh,
        in_specs=in_specs,
        out_specs=out_specs,
        check_vma=False,
    )
```

```python
import functools

import jax
import jax.numpy as jnp
from jax import lax
from jax.experimental import pallas as pl
from jax.experimental.pallas import tpu as pltpu
from jax.sharding import PartitionSpec as P

MESH = pl.DeviceIdType.MESH
F32 = jnp.float32
E = 16
W = 256
H = 128
FB = 3
SB = 2
C = [
    (0, 0, 0),
    (1, 0, 0),
    (-1, 0, 0),
    (0, 1, 0),
    (0, -1, 0),
    (0, 0, 1),
    (0, 0, -1),
    (1, 1, 0),
    (-1, -1, 0),
    (1, -1, 0),
    (-1, 1, 0),
    (1, 0, 1),
    (-1, 0, -1),
    (1, 0, -1),
    (-1, 0, 1),
    (0, 1, 1),
    (0, -1, -1),
    (0, 1, -1),
    (0, -1, 1),
]
OPP = [0, 2, 1, 4, 3, 6, 5, 8, 7, 10, 9, 12, 11, 14, 13, 16, 15, 18, 17]
PX = ([1, 7, 9, 11, 13], [2, 8, 10, 12, 14])
PY = ([3, 7, 10, 15, 17], [4, 8, 9, 16, 18])
HEAT = 5
SIDES = [(1, 0), (-1, 0), (0, 1), (0, -1)]
CORNERS = [(1, 1), (1, -1), (-1, -1), (-1, 1)]
PEERS = SIDES + CORNERS
CORNER_SRC = [(0, 1, 1), (0, 2, 0), (1, 1, 0), (1, 2, 1)]
CORNER_OF = {7: 0, 9: 1, 8: 2, 10: 3}
N_COPY = 20
LIMIT = 60 * 1024 * 1024


def lroll(v, s):
    n = v.shape[1]
    s = s % n
    return v if s == 0 else pltpu.roll(v, s, axis=1)


def rroll(v, s):
    n = v.shape[0]
    s = s % n
    return v if s == 0 else pltpu.roll(v, s, axis=0)


def lanes(shape):
    return lax.broadcasted_iota(jnp.int32, shape, 1)


def rows(shape):
    return lax.broadcasted_iota(jnp.int32, shape, 0)


def collide_tile(G, Q, b, rs, ls):
    def ld(p):
        return G[b, p, rs, ls]

    f = [ld(p) for p in range(19)]
    d = [None] * 19
    for p in (1, 3, 5, 7, 9, 11, 13, 15, 17):
        d[p] = f[p] - f[p + 1]
    s1 = ((f[1] + f[2]) + (f[3] + f[4])) + (f[5] + f[6])
    s2 = (((f[7] + f[8]) + (f[9] + f[10])) + ((f[11] + f[12]) + (f[13] + f[14]))) + (
        (f[15] + f[16]) + (f[17] + f[18])
    )
    rho = f[0] * (1.0 / 3.0) + s1 * (1.0 / 18.0) + s2 * (1.0 / 36.0)
    jx = d[1] * (1.0 / 18.0) + ((d[7] + d[9]) + (d[11] + d[13])) * (1.0 / 36.0)
    jy = d[3] * (1.0 / 18.0) + ((d[7] - d[9]) + (d[15] + d[17])) * (1.0 / 36.0)
    jz = d[5] * (1.0 / 18.0) + ((d[11] - d[13]) + (d[15] - d[17])) * (1.0 / 36.0)
    inv = 1.0 / rho
    u = (jx * inv, jy * inv, jz * inv)
    j = (jx, jy, jz)
    base = 1.25 * rho - 1.875 * (jx * u[0] + jy * u[1] + jz * u[2])
    G[b, 0, rs, ls] = base - 0.25 * f[0]
    cus = {}
    for p in (1, 3, 5, 7, 9, 11, 13, 15, 17):
        cj = None
        cu = None
        for a in range(3):
            s = C[p][a]
            if s == 0:
                continue
            if cj is None:
                cj, cu = j[a], u[a]
            elif s > 0:
                cj, cu = cj + j[a], cu + u[a]
            else:
                cj, cu = cj - j[a], cu - u[a]
        even = base + 5.625 * (cj * cu)
        odd = 3.75 * cj
        G[b, p, rs, ls] = (even + odd) - 0.25 * f[p]
        G[b, p + 1, rs, ls] = (even - odd) - 0.25 * f[p + 1]
        cus[p] = cu
    h = [Q[b, k, rs, ls] for k in range(7)]
    hs = ((h[1] + h[2]) + (h[3] + h[4])) + (h[5] + h[6])
    t11 = (h[0] * 0.25 + hs * 0.125) * 1.1
    t44 = 4.0 * t11
    Q[b, 0, rs, ls] = t11 - 0.1 * h[0]
    for k in (1, 3, 5):
        o = t44 * cus[k]
        Q[b, k, rs, ls] = (t11 + o) - 0.1 * h[k]
        Q[b, k + 1, rs, ls] = (t11 - o) - 0.1 * h[k + 1]


def kernel(
    nf,
    nc,
    fluid_in,
    heat_in,
    temp_in,
    mat_in,
    cond_in,
    nbr_in,
    wall_in,
    snbr_in,
    sflu_in,
    GO,
    QO,
    TO,
    G,
    Q,
    T,
    M,
    KAP,
    XS,
    XR,
    YS,
    YR,
    CR,
    XTS,
    XTR,
    YTS,
    YTR,
    DXS,
    DXR,
    DYS,
    DYR,
    cond,
    nbr,
    wall,
    snbr,
    sflu,
    in_sem,
    send_sem,
    recv_sem,
):
    fl = lax.axis_index("flow")
    cr = lax.axis_index("cross")

    inside = {-1: (fl > 0, cr > 0), 0: (True, True), 1: (fl < nf - 1, cr < nc - 1)}

    def near(df, dc):
        a, b = inside[df][0], inside[dc][1]
        if df == 0:
            return b
        return a if dc == 0 else jnp.logical_and(a, b)

    barrier = pltpu.get_barrier_semaphore()
    for df, dc in PEERS:

        @pl.when(near(df, dc))
        def _():
            pl.semaphore_signal(
                barrier, inc=1, device_id=(fl + df, cr + dc), device_id_type=MESH
            )

    nx = 2 - (fl == 0).astype(jnp.int32) - (fl == nf - 1).astype(jnp.int32)
    ny = 2 - (cr == 0).astype(jnp.int32) - (cr == nc - 1).astype(jnp.int32)
    n_peers = nx + ny + nx * ny

    def load(src, dst, sem):
        for x in range(E):
            pltpu.make_async_copy(
                src.at[..., pl.ds(W * x, W)], dst.at[..., x, :], sem
            ).start()

    def all_of(ref, sem):
        return pltpu.make_async_copy(ref, ref, sem)

    tables = [
        (cond_in, cond, 8),
        (nbr_in, nbr, 9),
        (wall_in, wall, 10),
        (snbr_in, snbr, 11),
        (sflu_in, sflu, 12),
    ]
    tables = [pltpu.make_async_copy(a, b, in_sem.at[i]) for a, b, i in tables]
    for c in tables:
        c.start()
    load(temp_in, T, in_sem.at[0])
    load(mat_in, M, in_sem.at[1])
    for b in range(FB):
        load(fluid_in.at[b], G.at[b], in_sem.at[2 + 2 * b])
        load(heat_in.at[b], Q.at[b], in_sem.at[3 + 2 * b])

    copies = {}
    steps = {}

    def send(i, src, dst, df, dc):
        copies[i] = pltpu.make_async_remote_copy(
            src_ref=src,
            dst_ref=dst,
            send_sem=send_sem.at[i],
            recv_sem=recv_sem.at[i],
            device_id=(fl + df, cr + dc),
            device_id_type=MESH,
        )
        steps[i] = (df, dc)

        @pl.when(near(df, dc))
        def _():
            copies[i].start()

    def received(i):
        @pl.when(near(-steps[i][0], -steps[i][1]))
        def _():
            copies[i].wait_recv()

    wide = (E, W)
    lw = lanes(wide)
    rw = rows(wide)
    zw = jnp.bitwise_and(lw, E - 1)
    lh = lanes((E, H))
    group = jnp.right_shift(lh, 4)

    def base_of(df, dc):
        return (fl + df) * nc + (cr + dc)

    with jax.named_scope("wait_solid"):
        for c in tables:
            c.wait()
        all_of(T, in_sem.at[0]).wait()
        all_of(M, in_sem.at[1]).wait()
    for s in range(SB):
        m = M[s]
        k = jnp.full(wide, cond[0], F32)
        for i in range(1, 8):
            k = jnp.where(m == i, cond[i], k)
        KAP[s] = k

    def pack_y(pieces, side):
        acc = None
        for g, v in enumerate(pieces):
            if side == 0:
                r = lroll(v[:, H:], E * g - (H - E))
            else:
                r = lroll(v[:, :H], E * g)
            acc = r if acc is None else jnp.where(group == g, r, acc)
        return acc

    for side in range(2):
        x = E - 1 if side == 0 else 0
        for s in range(SB):
            XTS[side, s, 0:1, :] = T[s, x : x + 1, :]
            XTS[side, s, 1:2, :] = KAP[s, x : x + 1, :]
        YTS[side] = pack_y([T[0], KAP[0], T[1], KAP[1]], side)

    with jax.named_scope("entry_barrier"):
        pl.semaphore_wait(barrier, n_peers)
    for i, (df, dc) in enumerate(SIDES):
        side = i % 2
        if i < 2:
            send(i, XTS.at[side], XTR.at[side], df, dc)
        else:
            send(i, YTS.at[side], YTR.at[side], df, dc)

    for b in range(FB):
        with jax.named_scope("wait_pops"):
            all_of(G.at[b], in_sem.at[2 + 2 * b]).wait()
            all_of(Q.at[b], in_sem.at[3 + 2 * b]).wait()
        with jax.named_scope("collide"):
            for xh in range(2):
                for yh in range(2):
                    collide_tile(G, Q, b, pl.ds(8 * xh, 8), pl.ds(H * yh, H))
        for side in range(2):
            x = E - 1 if side == 0 else 0
            for r in range(5):
                XS[side, b, r : r + 1, :] = G[b, PX[side][r], x : x + 1, :]
            XS[side, b, HEAT : HEAT + 1, :] = Q[b, 1 + side, x : x + 1, :]
            YS[side, b] = pack_y(
                [G[b, PY[side][r]] for r in range(5)] + [Q[b, 3 + side]], side
            )

    for i, (df, dc) in enumerate(SIDES):
        side = i % 2
        if i < 2:
            send(4 + i, XS.at[side], XR.at[side], df, dc)
        else:
            send(4 + i, YS.at[side], YR.at[side], df, dc)
    for i, (df, dc) in enumerate(CORNERS):
        side, r, half = CORNER_SRC[i]
        send(
            8 + i,
            XS.at[side, :, pl.ds(r, 1), pl.ds(H * half, H)],
            CR.at[i],
            df,
            dc,
        )

    def slot(idv, base, n):
        return jnp.clip(idv - base * n, 0, n - 1)

    def unpack_group(v, g, lo):
        return lroll(v, -E * g) if lo else lroll(v, (H - E) - E * g)

    def widen(v, lo):
        return jnp.concatenate([v, v], axis=1)

    def pick(sel, a, b_):
        return jnp.where(jnp.full(a.shape, sel) == 0, a, b_)

    edges = [rw == E - 1, rw == 0, lw >= W - E, lw < E, zw == E - 1, zw == 0]

    def shifted(v, k):
        return [
            lambda: rroll(v, -1),
            lambda: rroll(v, 1),
            lambda: lroll(v, -E),
            lambda: lroll(v, E),
            lambda: lroll(v, -1),
            lambda: lroll(v, 1),
        ][k]()

    def step_base(k):
        return base_of(C[k + 1][0], C[k + 1][1])

    def z_ghost(v, k):
        return lroll(v, E - 1) if k == 4 else lroll(v, 1 - E)

    def solid_ghost(k, s, sl, q, field):
        if k < 2:
            return XTR[1 - k, sl, q : q + 1, :]
        if k < 4:
            v = YTR[1 - (k - 2)]
            lo = k == 3
            return widen(pick(sl, unpack_group(v, q, lo), unpack_group(v, 2 + q, lo)), lo)
        return z_ghost(field[1 - s], k)

    def heat_ghost(k, fsl):
        if k < 2:
            return XR[1 - k, fsl, HEAT : HEAT + 1, :]
        if k < 4:
            lo = k == 3
            return widen(unpack_group(YR[1 - (k - 2), fsl], HEAT, lo), lo)
        return z_ghost(Q[fsl, 6 if k == 4 else 5], k)

    with jax.named_scope("wait_faces"):
        for i in range(12):
            received(i)

    kmax = cond[0]
    for i in range(1, 8):
        kmax = jnp.maximum(kmax, cond[i])
    radius = jnp.full((8, H), kmax * 6.0, F32)
    center = radius + 1.0
    sigma = center / radius

    def grow(v):
        v = jnp.concatenate([v, v], axis=0)
        return jnp.concatenate([v, v], axis=1)

    inv_center = grow(1.0 / center)
    rho0 = 1.0 / sigma
    rho1 = 1.0 / (2.0 * sigma - rho0)
    rho2 = 1.0 / (2.0 * sigma - rho1)
    coef = [
        (grow(rho1 * rho0), grow(2.0 * rho1 / radius)),
        (grow(rho2 * rho1), grow(2.0 * rho2 / radius)),
    ]

    sid = [[snbr[s, k] for k in range(6)] for s in range(SB)]
    fid = [[sflu[s, k] for k in range(6)] for s in range(SB)]
    ssl = [[slot(sid[s][k], step_base(k), SB) for k in range(6)] for s in range(SB)]
    links = []
    resid = []
    upd = []
    sol = []
    for s in range(SB):
        t = T[s]
        kap = KAP[s]
        acc = jnp.zeros(wide, F32)
        row = []
        for k in range(6):
            sl = ssl[s][k]
            live = jnp.full(wide, sid[s][k]) >= 0
            wet = jnp.full(wide, fid[s][k]) >= 0
            kb = jnp.where(edges[k], solid_ghost(k, s, sl, 1, KAP), shifted(kap, k))
            link = (2.0 * kap * kb) / (kap + kb)
            link = jnp.where(edges[k] & ~live, 0.0, link)
            row.append(link)
            tb = jnp.where(edges[k], solid_ghost(k, s, sl, 0, T), shifted(t, k))
            hb = heat_ghost(k, slot(fid[s][k], step_base(k), FB))
            tb = jnp.where(edges[k] & ~live, t, tb)
            wet_edge = edges[k] & wet
            acc = acc + jnp.where(wet_edge, 1.0, link) * (jnp.where(wet_edge, hb, tb) - t)
        links.append(row)
        d = acc * inv_center
        resid.append(acc)
        upd.append(d)
        sol.append(t + d)

    def share(n):
        for side in range(2):
            x = E - 1 if side == 0 else 0
            for s in range(SB):
                DXS[n, side, s : s + 1, :] = upd[s][x : x + 1, :]
            DYS[n, side] = pack_y(upd, side)
        for i, (df, dc) in enumerate(SIDES):
            side = i % 2
            if i < 2:
                send(12 + 4 * n + i, DXS.at[n, side], DXR.at[n, side], df, dc)
            else:
                send(12 + 4 * n + i, DYS.at[n, side], DYR.at[n, side], df, dc)

    def update_ghost(n, k, s, sl):
        if k < 2:
            v = DXR[n, 1 - k]
            return pick(sl, v[0:1], v[1:2])
        if k < 4:
            v = DYR[n, 1 - (k - 2)]
            lo = k == 3
            return widen(pick(sl, unpack_group(v, 0, lo), unpack_group(v, 1, lo)), lo)
        return z_ghost(upd[1 - s], k)

    def sweep(n):
        with jax.named_scope("wait_updates"):
            for i in range(4):
                received(12 + 4 * n + i)
        fresh = []
        for s in range(SB):
            d = upd[s]
            acc = d
            for k in range(6):
                ghost = update_ghost(n, k, s, ssl[s][k])
                ghost = jnp.where(jnp.full(ghost.shape, sid[s][k]) >= 0, ghost, 0.0)
                db = jnp.where(edges[k], ghost, shifted(d, k))
                acc = acc + links[s][k] * (d - db)
            resid[s] = resid[s] - acc
            nd = coef[n][0] * d + coef[n][1] * resid[s]
            fresh.append(nd)
            sol[s] = sol[s] + nd
        for s in range(SB):
            upd[s] = fresh[s]

    share(0)

    def x_face(b, side):
        shape = (8, W)
        r8 = rows(shape)
        l8 = lanes(shape)
        z8 = jnp.bitwise_and(l8, E - 1)
        df = -1 if side == 0 else 1
        dirn = 2 if side == 0 else 1
        bf = base_of(df, 0)
        main_id = nbr[b, dirn - 1]
        a = XR[side, slot(main_id, bf, FB)]
        val = a
        ids = jnp.full(shape, main_id)
        for r, p in enumerate(PX[side]):
            _, cy, cz = C[p]
            if r == 0:
                continue
            src = OPP[p]
            cid = nbr[b, src - 1]
            if cy:
                corner = CR[CORNER_OF[p], slot(cid, base_of(df, -cy), FB)]
                corner = jnp.broadcast_to(corner, (8, H))
                corner = lroll(corner, E * cy)
                corner = jnp.concatenate([corner, corner], axis=1)
                edge = l8 < E if cy > 0 else l8 >= W - E
                cand = jnp.where(edge, corner, lroll(a, E * cy))
            else:
                other = XR[side, slot(cid, bf, FB)]
                edge = z8 == 0 if cz > 0 else z8 == E - 1
                cand = jnp.where(edge, lroll(other, -(E - 1) * cz), lroll(a, cz))
            val = jnp.where(r8 == r, cand, val)
            ids = jnp.where((r8 == r) & edge, jnp.full(shape, cid), ids)
        fall = XS[1 - side, b]
        wid = wall[b, dirn - 1]
        tw = XTR[side, slot(wid, bf, SB), 0:1, :]
        hot = (r8 == HEAT) & (jnp.full(shape, wid) >= 0)
        fall = jnp.where(hot, 2.0 * tw - fall, fall)
        return jnp.where(ids >= 0, val, fall)

    def y_face(b, side):
        shape = (E, H)
        zh = jnp.bitwise_and(lh, E - 1)
        dc = -1 if side == 0 else 1
        dirn = 4 if side == 0 else 3
        bf = base_of(0, dc)
        main_id = nbr[b, dirn - 1]
        a = YR[side, slot(main_id, bf, FB)]
        val = a
        ids = jnp.full(shape, main_id)
        for r, p in enumerate(PY[side]):
            cx, _, cz = C[p]
            if r == 0:
                continue
            if cx:
                val = jnp.where(group == r, rroll(a, cx), val)
                continue
            cid = nbr[b, OPP[p] - 1]
            other = YR[side, slot(cid, bf, FB)]
            edge = zh == 0 if cz > 0 else zh == E - 1
            cand = jnp.where(edge, lroll(other, -(E - 1) * cz), lroll(a, cz))
            val = jnp.where(group == r, cand, val)
            ids = jnp.where((group == r) & edge, jnp.full(shape, cid), ids)
        fall = YS[1 - side, b]
        wid = wall[b, dirn - 1]
        wsl = slot(wid, bf, SB)
        tv = YTR[side]
        tw = pick(wsl, lroll(tv, E * HEAT), lroll(tv, E * (HEAT - 2)))
        hot = (group == HEAT) & (jnp.full(shape, wid) >= 0)
        fall = jnp.where(hot, 2.0 * tw - fall, fall)
        return jnp.where(ids >= 0, val, fall)

    def stream(b):
        yf = [y_face(b, 0), y_face(b, 1)]

        def main(ref, p, q):
            cx, cy, cz = C[p]
            s = E * cy + cz
            out = lroll(rroll(ref[b, p], cx), s)
            if cz:
                back = ref[b, OPP[p]]
                adj = (b - cz) % FB
                if 0 <= b - cz < FB:
                    other = lroll(rroll(ref[adj, p], cx), E * cy - (E - 1) * cz)
                    zid = nbr[b, (6 if cz > 0 else 5) - 1]
                else:
                    other = None
                if ref is Q:
                    wid = wall[b, (6 if cz > 0 else 5) - 1]
                    tw = lroll(T[slot(wid, base_of(0, 0), SB)], -(E - 1) * cz)
                    back = jnp.where(jnp.full(wide, wid) >= 0, 2.0 * tw - back, back)
                if other is not None:
                    back = jnp.where(jnp.full(wide, zid) >= 0, other, back)
                edge = zw == 0 if cz > 0 else zw == E - 1
                out = jnp.where(edge, back, out)
            if cy:
                lo = cy > 0
                v = unpack_group(yf[0 if lo else 1], q, lo)
                if lo:
                    out = jnp.concatenate(
                        [jnp.where(lh < E, v, out[:, :H]), out[:, H:]], axis=1
                    )
                else:
                    out = jnp.concatenate(
                        [out[:, :H], jnp.where(lh >= H - E, v, out[:, H:])], axis=1
                    )
            return out

        GO[b, 0] = G[b, 0]
        QO[b, 0] = Q[b, 0]
        for p in range(1, 19):
            cy = C[p][1]
            q = PY[0 if cy > 0 else 1].index(p) if cy else None
            GO[b, p] = main(G, p, q)
        for p in range(1, 7):
            QO[b, p] = main(Q, p, HEAT)
        for side in range(2):
            xf = x_face(b, side)
            x = 0 if side == 0 else E - 1
            for r, p in enumerate(PX[side]):
                GO[b, p, x : x + 1, :] = xf[r : r + 1]
            QO[b, 1 + side, x : x + 1, :] = xf[HEAT : HEAT + 1]

    with jax.named_scope("stream"):
        stream(0)
        stream(1)
    sweep(0)
    share(1)
    with jax.named_scope("stream"):
        stream(2)
    sweep(1)
    for s in range(SB):
        TO[s] = sol[s]

    for i in range(N_COPY):

        @pl.when(near(*steps[i]))
        def _():
            copies[i].wait_send()


def store_kernel(fluid, heat, solid, fluid_out, heat_out, solid_out, sem):
    pairs = [(fluid, fluid_out), (heat, heat_out), (solid, solid_out)]
    for i, (src, dst) in enumerate(pairs):
        for x in range(E):
            pltpu.make_async_copy(
                src.at[..., x, :], dst.at[..., pl.ds(W * x, W)], sem.at[i]
            ).start()
    for i, (src, dst) in enumerate(pairs):
        pltpu.make_async_copy(src, src, sem.at[i]).wait()


def body(nf, nc, fluid_pop, heat_pop, solid_temp, material, cond, nbr, wall, snbr, sflu):
    hbm = pl.BlockSpec(memory_space=pltpu.HBM)

    def vm(*shape):
        return pltpu.VMEM(shape, F32)

    vmem = pl.BlockSpec(memory_space=pltpu.VMEM)
    fields = pl.pallas_call(
        functools.partial(kernel, nf, nc),
        out_shape=(
            vm(FB, 19, E, W),
            vm(FB, 7, E, W),
            vm(SB, E, W),
        ),
        in_specs=[hbm] * 9,
        out_specs=(vmem, vmem, vmem),
        scratch_shapes=[
            vm(FB, 19, E, W),
            vm(FB, 7, E, W),
            vm(SB, E, W),
            pltpu.VMEM((SB, E, W), jnp.int32),
            vm(SB, E, W),
            vm(2, FB, 8, W),
            vm(2, FB, 8, W),
            vm(2, FB, E, H),
            vm(2, FB, E, H),
            vm(4, FB, 1, H),
            vm(2, SB, 2, W),
            vm(2, SB, 2, W),
            vm(2, E, H),
            vm(2, E, H),
            vm(2, 2, SB, W),
            vm(2, 2, SB, W),
            vm(2, 2, E, H),
            vm(2, 2, E, H),
            pltpu.SMEM(cond.shape, F32),
            pltpu.SMEM(nbr.shape, jnp.int32),
            pltpu.SMEM(wall.shape, jnp.int32),
            pltpu.SMEM(snbr.shape, jnp.int32),
            pltpu.SMEM(sflu.shape, jnp.int32),
            pltpu.SemaphoreType.DMA((13,)),
            pltpu.SemaphoreType.DMA((N_COPY,)),
            pltpu.SemaphoreType.DMA((N_COPY,)),
        ],
        compiler_params=pltpu.CompilerParams(
            collective_id=0, has_side_effects=True, vmem_limit_bytes=LIMIT
        ),
    )(fluid_pop, heat_pop, solid_temp, material, cond, nbr, wall, snbr, sflu)
    return pl.pallas_call(
        store_kernel,
        out_shape=(
            jax.ShapeDtypeStruct(fluid_pop.shape, F32),
            jax.ShapeDtypeStruct(heat_pop.shape, F32),
            jax.ShapeDtypeStruct(solid_temp.shape, F32),
        ),
        in_specs=[pl.BlockSpec(memory_space=pl.ANY)] * 3,
        out_specs=(hbm, hbm, hbm),
        scratch_shapes=[pltpu.SemaphoreType.DMA((3,))],
        compiler_params=pltpu.CompilerParams(vmem_limit_bytes=8 * 1024 * 1024),
    )(*fields)


def solution(mesh):
    both = ("flow", "cross")
    in_specs = (
        P(both, None, None),
        P(both, None, None),
        P(both, None),
        P(both, None),
        P(),
        P(both, None),
        P(both, None),
        P(both, None),
        P(both, None),
    )
    out_specs = (P(both, None, None), P(both, None, None), P(both, None))
    return jax.shard_map(
        functools.partial(body, mesh.shape["flow"], mesh.shape["cross"]),
        mesh=mesh,
        in_specs=in_specs,
        out_specs=out_specs,
        check_vma=False,
    )
```

```python
import functools

import jax
import jax.numpy as jnp
from jax import lax
from jax.experimental import pallas as pl
from jax.experimental.pallas import tpu as pltpu
from jax.sharding import PartitionSpec as P

MESH = pl.DeviceIdType.MESH
F32 = jnp.float32
E = 16
W = 256
H = 128
FB = 3
SB = 2
C = [
    (0, 0, 0),
    (1, 0, 0),
    (-1, 0, 0),
    (0, 1, 0),
    (0, -1, 0),
    (0, 0, 1),
    (0, 0, -1),
    (1, 1, 0),
    (-1, -1, 0),
    (1, -1, 0),
    (-1, 1, 0),
    (1, 0, 1),
    (-1, 0, -1),
    (1, 0, -1),
    (-1, 0, 1),
    (0, 1, 1),
    (0, -1, -1),
    (0, 1, -1),
    (0, -1, 1),
]
OPP = [0, 2, 1, 4, 3, 6, 5, 8, 7, 10, 9, 12, 11, 14, 13, 16, 15, 18, 17]
PX = ([1, 7, 9, 11, 13], [2, 8, 10, 12, 14])
PY = ([3, 7, 10, 15, 17], [4, 8, 9, 16, 18])
HEAT = 5
SIDES = [(1, 0), (-1, 0), (0, 1), (0, -1)]
CORNERS = [(1, 1), (1, -1), (-1, -1), (-1, 1)]
PEERS = SIDES + CORNERS
CORNER_SRC = [(0, 1, 1), (0, 2, 0), (1, 1, 0), (1, 2, 1)]
CORNER_OF = {7: 0, 9: 1, 8: 2, 10: 3}
EDGE_Z = 6
CROSS = 7
N_COPY = 16
NZ = 5
EX = 24
EL = 384
LIMIT = 60 * 1024 * 1024


def lroll(v, s):
    n = v.shape[1]
    s = s % n
    return v if s == 0 else pltpu.roll(v, s, axis=1)


def rroll(v, s):
    n = v.shape[0]
    s = s % n
    return v if s == 0 else pltpu.roll(v, s, axis=0)


def lanes(shape):
    return lax.broadcasted_iota(jnp.int32, shape, 1)


def rows(shape):
    return lax.broadcasted_iota(jnp.int32, shape, 0)


def collide_tile(G, Q, b, rs, ls):
    def ld(p):
        return G[b, p, rs, ls]

    f = [ld(p) for p in range(19)]
    d = [None] * 19
    for p in (1, 3, 5, 7, 9, 11, 13, 15, 17):
        d[p] = f[p] - f[p + 1]
    s1 = ((f[1] + f[2]) + (f[3] + f[4])) + (f[5] + f[6])
    s2 = (((f[7] + f[8]) + (f[9] + f[10])) + ((f[11] + f[12]) + (f[13] + f[14]))) + (
        (f[15] + f[16]) + (f[17] + f[18])
    )
    rho = f[0] * (1.0 / 3.0) + s1 * (1.0 / 18.0) + s2 * (1.0 / 36.0)
    jx = d[1] * (1.0 / 18.0) + ((d[7] + d[9]) + (d[11] + d[13])) * (1.0 / 36.0)
    jy = d[3] * (1.0 / 18.0) + ((d[7] - d[9]) + (d[15] + d[17])) * (1.0 / 36.0)
    jz = d[5] * (1.0 / 18.0) + ((d[11] - d[13]) + (d[15] - d[17])) * (1.0 / 36.0)
    inv = 1.0 / rho
    u = (jx * inv, jy * inv, jz * inv)
    j = (jx, jy, jz)
    base = 1.25 * rho - 1.875 * (jx * u[0] + jy * u[1] + jz * u[2])
    G[b, 0, rs, ls] = base - 0.25 * f[0]
    cus = {}
    for p in (1, 3, 5, 7, 9, 11, 13, 15, 17):
        cj = None
        cu = None
        for a in range(3):
            s = C[p][a]
            if s == 0:
                continue
            if cj is None:
                cj, cu = j[a], u[a]
            elif s > 0:
                cj, cu = cj + j[a], cu + u[a]
            else:
                cj, cu = cj - j[a], cu - u[a]
        even = base + 5.625 * (cj * cu)
        odd = 3.75 * cj
        G[b, p, rs, ls] = (even + odd) - 0.25 * f[p]
        G[b, p + 1, rs, ls] = (even - odd) - 0.25 * f[p + 1]
        cus[p] = cu
    h = [Q[b, k, rs, ls] for k in range(7)]
    hs = ((h[1] + h[2]) + (h[3] + h[4])) + (h[5] + h[6])
    t11 = (h[0] * 0.25 + hs * 0.125) * 1.1
    t44 = 4.0 * t11
    Q[b, 0, rs, ls] = t11 - 0.1 * h[0]
    for k in (1, 3, 5):
        o = t44 * cus[k]
        Q[b, k, rs, ls] = (t11 + o) - 0.1 * h[k]
        Q[b, k + 1, rs, ls] = (t11 - o) - 0.1 * h[k + 1]


def kernel(
    nf,
    nc,
    fluid_in,
    heat_in,
    temp_in,
    mat_in,
    cond_in,
    nbr_in,
    wall_in,
    snbr_in,
    sflu_in,
    GO,
    QO,
    TO,
    G,
    Q,
    T,
    M,
    KAP,
    XS,
    XR,
    YS,
    YR,
    CS,
    CR,
    XES,
    XER,
    YES,
    YER,
    CER,
    TE,
    KE,
    WE,
    LX,
    LY,
    LZ,
    R,
    D,
    SX,
    SY,
    SZ,
    U,
    cond,
    nbr,
    wall,
    snbr,
    sflu,
    in_sem,
    send_sem,
    recv_sem,
):
    fl = lax.axis_index("flow")
    cr = lax.axis_index("cross")
    inside = {-1: (fl > 0, cr > 0), 0: (True, True), 1: (fl < nf - 1, cr < nc - 1)}

    def near(df, dc):
        a, b = inside[df][0], inside[dc][1]
        if df == 0:
            return b
        return a if dc == 0 else jnp.logical_and(a, b)

    barrier = pltpu.get_barrier_semaphore()
    for df, dc in PEERS:

        @pl.when(near(df, dc))
        def _():
            pl.semaphore_signal(
                barrier, inc=1, device_id=(fl + df, cr + dc), device_id_type=MESH
            )

    nx = 2 - (fl == 0).astype(jnp.int32) - (fl == nf - 1).astype(jnp.int32)
    ny = 2 - (cr == 0).astype(jnp.int32) - (cr == nc - 1).astype(jnp.int32)
    n_peers = nx + ny + nx * ny

    def load(src, dst, sem):
        for x in range(E):
            pltpu.make_async_copy(
                src.at[..., pl.ds(W * x, W)], dst.at[..., x, :], sem
            ).start()

    def all_of(ref, sem):
        return pltpu.make_async_copy(ref, ref, sem)

    tables = [
        (cond_in, cond, 8),
        (nbr_in, nbr, 9),
        (wall_in, wall, 10),
        (snbr_in, snbr, 11),
        (sflu_in, sflu, 12),
    ]
    tables = [pltpu.make_async_copy(a, b, in_sem.at[i]) for a, b, i in tables]
    for c in tables:
        c.start()
    load(temp_in, T, in_sem.at[0])
    load(mat_in, M, in_sem.at[1])
    for b in range(FB):
        load(fluid_in.at[b], G.at[b], in_sem.at[2 + 2 * b])
        load(heat_in.at[b], Q.at[b], in_sem.at[3 + 2 * b])

    copies = {}
    steps = {}

    def send(i, src, dst, df, dc):
        copies[i] = pltpu.make_async_remote_copy(
            src_ref=src,
            dst_ref=dst,
            send_sem=send_sem.at[i],
            recv_sem=recv_sem.at[i],
            device_id=(fl + df, cr + dc),
            device_id_type=MESH,
        )
        steps[i] = (df, dc)

        @pl.when(near(df, dc))
        def _():
            copies[i].start()

    def received(i):
        @pl.when(near(-steps[i][0], -steps[i][1]))
        def _():
            copies[i].wait_recv()

    wide = (E, W)
    lw = lanes(wide)
    zw = jnp.bitwise_and(lw, E - 1)
    lh = lanes((E, H))
    zh = jnp.bitwise_and(lh, E - 1)
    group = jnp.right_shift(lh, 4)
    r8 = rows((8, W))
    l8 = lanes((8, W))
    z8 = jnp.bitwise_and(l8, E - 1)
    q8 = rows((8, H))
    g8 = jnp.right_shift(lanes((8, H)), 4)

    def base_of(df, dc):
        return (fl + df) * nc + (cr + dc)

    def slot(idv, base, n):
        return jnp.clip(idv - base * n, 0, n - 1)

    def num(flag):
        return jnp.where(flag, 1, 0)

    def on(flag, like):
        return jnp.full(like.shape, flag) > 0

    for c in tables:
        c.wait()

    here = base_of(0, 0)
    below0 = sflu[0, 5]
    below1 = sflu[1, 5]
    z0 = jnp.where(below0 >= 0, slot(below0, here, FB) + 1, 0)
    z1 = jnp.where(below1 >= 0, slot(below1, here, FB) + 2, z0 + 1)
    own_z = (z0, z1)
    flu_z = [b + num(b >= z0) + num(b + 1 >= z1) for b in range(FB)]

    def column(za, zb, exists):
        res = []
        for p in range(NZ):
            solid = num(jnp.logical_or(za == p, zb == p)) * exists
            res.append(
                (
                    solid,
                    exists - solid,
                    num(zb == p),
                    jnp.clip(p - num(za < p) - num(zb < p), 0, FB - 1),
                )
            )
        return res

    own = column(z0, z1, num(fl >= 0))
    beside = []
    for k in range(4):
        df, dc = C[k + 1][0], C[k + 1][1]
        first = base_of(df, dc) * SB
        za = zb = 0
        pairs = [(wall[b, k], flu_z[b]) for b in range(FB)]
        pairs += [(snbr[s, k], own_z[s]) for s in range(SB)]
        for idv, z in pairs:
            za = za + jnp.where(idv == first, z, 0)
            zb = zb + jnp.where(idv == first + 1, z, 0)
        beside.append(column(za, zb, num(near(df, dc))))

    with jax.named_scope("wait_solid"):
        all_of(T, in_sem.at[0]).wait()
        all_of(M, in_sem.at[1]).wait()
    for s in range(SB):
        m = M[s]
        k = jnp.full(wide, cond[0], F32)
        for i in range(1, 8):
            k = jnp.where(m == i, cond[i], k)
        KAP[s] = k
        zf = jnp.full((8, W), own_z[s]).astype(F32)
        t = T[s]
        XES[0, s] = jnp.where(r8 > 4, t[8:], jnp.where(r8 == 4, zf, rroll(k[8:], 4)))
        XES[1, s] = jnp.where(r8 < 3, t[:8], jnp.where(r8 == 3, zf, rroll(k[:8], 4)))
        YES[0, s] = jnp.where(lh >= 64, t[:, H:], lroll(k[:, H:], 64))
        YES[1, s] = jnp.where(lh < 64, t[:, :H], lroll(k[:, :H], 64))

    with jax.named_scope("entry_barrier"):
        pl.semaphore_wait(barrier, n_peers)
    for i, (df, dc) in enumerate(SIDES):
        side = i % 2
        if i < 2:
            send(i, XES.at[side], XER.at[side], df, dc)
        else:
            send(i, YES.at[side], YER.at[side], df, dc)
    for i, (df, dc) in enumerate(CORNERS):
        side, _, half = CORNER_SRC[i]
        send(4 + i, XES.at[side, :, :, pl.ds(H * half, H)], CER.at[i], df, dc)

    def pack_y(pieces, side):
        acc = None
        for g, v in enumerate(pieces):
            r = lroll(v, E * g - (H - E)) if side == 0 else lroll(v, E * g)
            acc = r if acc is None else jnp.where(group == g, r, acc)
        return acc

    def two(v, first, second, z):
        return jnp.where((z == 0) | (z == E - 1), v, jnp.where(z < 8, first, second))

    for b in range(FB):
        with jax.named_scope("wait_pops"):
            all_of(G.at[b], in_sem.at[2 + 2 * b]).wait()
            all_of(Q.at[b], in_sem.at[3 + 2 * b]).wait()
        with jax.named_scope("collide"):
            for xh in range(2):
                for yh in range(2):
                    collide_tile(G, Q, b, pl.ds(8 * xh, 8), pl.ds(H * yh, H))
        for side in range(2):
            x = E - 1 if side == 0 else 0
            inner = E - 2 if side == 0 else 1

            def line(x_at, lo, n):
                zz = jnp.bitwise_and(lanes((1, n)), E - 1)
                up = Q[b, 6, x_at : x_at + 1, lo : lo + n]
                return jnp.where(zz < 8, up, Q[b, 5, x_at : x_at + 1, lo : lo + n])

            for r in range(5):
                XS[side, b, r : r + 1, :] = G[b, PX[side][r], x : x + 1, :]
            XS[side, b, HEAT : HEAT + 1, :] = Q[b, 1 + side, x : x + 1, :]
            z1w = jnp.bitwise_and(lanes((1, W)), E - 1)
            v = line(inner, 0, W)
            XS[side, b, EDGE_Z : EDGE_Z + 1, :] = two(
                line(x, 0, W), lroll(v, 1), lroll(v, -1), z1w
            )
            XS[side, b, CROSS : CROSS + 1, :H] = Q[b, 4, x : x + 1, :H]
            XS[side, b, CROSS : CROSS + 1, H:] = Q[b, 3, x : x + 1, H:]

            half = pl.ds(H, H) if side == 0 else pl.ds(0, H)
            sgn = 1 if side == 0 else -1
            hz = jnp.where(zh < 8, Q[b, 6, :, half], Q[b, 5, :, half])
            hx = jnp.concatenate([Q[b, 2, 0:8, half], Q[b, 1, 8:16, half]], axis=0)
            YS[side, b] = pack_y(
                [G[b, PY[side][r], :, half] for r in range(5)]
                + [
                    Q[b, 3 + side, :, half],
                    two(hz, lroll(hz, sgn * E + 1), lroll(hz, sgn * E - 1), zh),
                    hx,
                ],
                side,
            )
            for i in range(4):
                cs, row, ch = CORNER_SRC[i]
                if cs != side:
                    continue
                sg = -1 if ch else 1
                hp = 3 if ch else 4
                lo = H * ch
                gg = jnp.right_shift(lanes((1, H)), 4)
                at = (lambda d: 7 - d) if ch else (lambda d: d)
                acc = Q[b, 1 + side, x : x + 1, lo : lo + H]
                extra = [
                    (2, line(x, lo, H)),
                    (3, G[b, PX[side][row], x : x + 1, lo : lo + H]),
                    (4, Q[b, hp, x : x + 1, lo : lo + H]),
                    (5, Q[b, hp, inner : inner + 1, lo : lo + H]),
                ]
                for d, v in extra:
                    acc = jnp.where(gg == at(d), lroll(v, sg * E * d), acc)
                CS[i, b] = acc

    for i, (df, dc) in enumerate(SIDES):
        side = i % 2
        if i < 2:
            send(8 + i, XS.at[side], XR.at[side], df, dc)
        else:
            send(8 + i, YS.at[side], YR.at[side], df, dc)
    for i, (df, dc) in enumerate(CORNERS):
        send(12 + i, CS.at[i], CR.at[i], df, dc)

    def stream(b):
        def main(ref, p):
            cx, cy, cz = C[p]
            s = E * cy + cz
            out = lroll(rroll(ref[b, p], cx), s)
            if cz:
                back = ref[b, OPP[p]]
                adj = (b - cz) % FB
                if ref is Q:
                    wid = wall[b, (6 if cz > 0 else 5) - 1]
                    tw = lroll(T[slot(wid, here, SB)], -(E - 1) * cz)
                    back = jnp.where(jnp.full(wide, wid) >= 0, 2.0 * tw - back, back)
                if 0 <= b - cz < FB:
                    other = lroll(rroll(ref[adj, p], cx), E * cy - (E - 1) * cz)
                    zid = nbr[b, (6 if cz > 0 else 5) - 1]
                    back = jnp.where(jnp.full(wide, zid) >= 0, other, back)
                edge = zw == 0 if cz > 0 else zw == E - 1
                out = jnp.where(edge, back, out)
            return out

        GO[b, 0] = G[b, 0]
        QO[b, 0] = Q[b, 0]
        for p in range(1, 19):
            GO[b, p] = main(G, p)
        for p in range(1, 7):
            QO[b, p] = main(Q, p)

    with jax.named_scope("stream"):
        for b in range(FB):
            stream(b)

    ext = (EX, EL)
    ze = jnp.bitwise_and(lanes(ext), E - 1)

    def piece(flag, v):
        return jnp.where(on(flag, v), v, 0.0)

    for i in range(8):
        received(i)

    def corner_z(i):
        side = CORNER_SRC[i][0]
        r = 4 if side == 0 else 3
        return [
            jnp.broadcast_to(CER[i, s, r : r + 1, :], (8, H))
            for s in range(SB)
        ]

    quad = [[2, 3], [1, 0]]
    cz = [corner_z(i) for i in range(4)]
    chas = [jnp.full((8, H), num(near(-df, -dc))) > 0 for df, dc in CORNERS]

    def quadrants(fn):
        up = jnp.where(g8 < 4, fn(quad[0][0]), fn(quad[0][1]))
        down = jnp.where(g8 < 4, fn(quad[1][0]), fn(quad[1][1]))
        return jnp.where(q8 < 4, up, down)

    for p in range(NZ):
        solid, wet, ss, _ = own[p]
        TE[p, 0:E, 0:W] = piece(solid, T[ss])
        KE[p, 0:E, 0:W] = piece(solid, KAP[ss])
        WE[p, 0:E, 0:W] = jnp.full(wide, wet).astype(F32)
        a = piece(beside[0][p][0], XER[1, beside[0][p][2]])
        c = piece(beside[1][p][0], XER[0, beside[1][p][2]])
        TE[p, E:EX, 0:W] = jnp.where(r8 < 4, a, c)
        KE[p, E:EX, 0:W] = rroll(jnp.where(r8 < 4, c, a), 4)
        WE[p, E:EX, 0:W] = jnp.where(
            r8 < 4, jnp.full((8, W), beside[0][p][1]), jnp.full((8, W), beside[1][p][1])
        ).astype(F32)
        a = piece(beside[2][p][0], YER[1, beside[2][p][2]])
        c = piece(beside[3][p][0], YER[0, beside[3][p][2]])
        TE[p, 0:E, W:EL] = jnp.where(group < 4, a, c)
        KE[p, 0:E, W:EL] = lroll(jnp.where(group < 4, c, a), 64)
        WE[p, 0:E, W:EL] = jnp.where(
            group < 4,
            jnp.full((E, H), beside[2][p][1]),
            jnp.full((E, H), beside[3][p][1]),
        ).astype(F32)

        def corner_solid(i):
            v = jnp.where(cz[i][1] == p, CER[i, 1], 0.0)
            v = jnp.where(cz[i][0] == p, CER[i, 0], v)
            return jnp.where(chas[i], v, 0.0)

        def corner_wet(i):
            return jnp.where(chas[i] & (cz[i][0] != p) & (cz[i][1] != p), 1.0, 0.0)

        TE[p, E:EX, W:EL] = quadrants(corner_solid)
        KE[p, E:EX, W:EL] = quadrants(lambda i: rroll(corner_solid(i), 4))
        WE[p, E:EX, W:EL] = quadrants(corner_wet)

    def z_up(ref, p):
        v = lroll(ref[p], -1)
        over = lroll(ref[p + 1], E - 1) if p + 1 < NZ else 0.0
        return jnp.where(ze == E - 1, over, v)

    def z_down(v, before):
        under = lroll(before, 1 - E) if before is not None else 0.0
        return jnp.where(ze == 0, under, lroll(v, 1))

    def both(v, p, ref):
        below = ref[p - 1] if p else None
        return (
            rroll(v, 1) + rroll(v, -1),
            lroll(v, E) + lroll(v, -E),
            z_up(ref, p) + z_down(v, below),
        )

    def link(k, kb):
        return (2.0 * k * kb) / jnp.maximum(k + kb, 0.05)

    def divergence(v, up, p, before):
        fx = LX[p] * (rroll(v, -1) - v)
        fy = LY[p] * (lroll(v, -E) - v)
        fz = LZ[p] * (up - v)
        div = (fx - rroll(fx, 1)) + (fy - lroll(fy, E)) + (fz - z_down(fz, before))
        return div, fz

    before = None
    for p in range(NZ):
        k = KE[p]
        LX[p] = link(k, rroll(k, -1))
        LY[p] = link(k, lroll(k, -E))
        LZ[p] = link(k, z_up(KE, p))
        t = TE[p]
        div, before = divergence(t, z_up(TE, p), p, before)
        wx, wy, wz = both(WE[p], p, WE)
        R[p] = div - jnp.where(k > 0.0, (wx + wy + wz) * t, 0.0)

    kmax = cond[0]
    for i in range(1, 8):
        kmax = jnp.maximum(kmax, cond[i])
    radius = jnp.full((8, H), kmax * 6.0, F32)
    center = radius + 1.0
    sigma = center / radius

    def grow(v):
        v = jnp.concatenate([v] * (EX // 8), axis=0)
        return jnp.concatenate([v] * (EL // H), axis=1)

    inv_center = grow(1.0 / center)
    rho0 = 1.0 / sigma
    rho1 = 1.0 / (2.0 * sigma - rho0)
    rho2 = 1.0 / (2.0 * sigma - rho1)
    coef = [
        (grow(rho1 * rho0), grow(2.0 * rho1 / radius)),
        (grow(rho2 * rho1), grow(2.0 * rho2 / radius)),
    ]

    with jax.named_scope("wait_faces"):
        for i in range(8, 16):
            received(i)

    def corner_heat(i, p):
        f = p - jnp.where(cz[i][0] < p, 1, 0) - jnp.where(cz[i][1] < p, 1, 0)
        a, b, c = [jnp.broadcast_to(CR[i, j], (8, H)) for j in range(FB)]
        v = jnp.where(f <= 0, a, jnp.where(f == 1, b, c))
        wet = chas[i] & (cz[i][0] != p) & (cz[i][1] != p)
        return jnp.where(wet, v, 0.0)

    row_edge = (q8 == 0) | (q8 == 7)
    for p in range(NZ):
        _, wet, _, f = own[p]
        SX[p, 0:8, 0:W] = piece(wet, Q[f, 2, 0:8])
        SX[p, 8:E, 0:W] = piece(wet, Q[f, 1, 8:E])
        SY[p, 0:E, 0:H] = piece(wet, Q[f, 4, :, 0:H])
        SY[p, 0:E, H:W] = piece(wet, Q[f, 3, :, H:W])
        SZ[p, 0:E, 0:W] = piece(wet, jnp.where(zw < 8, Q[f, 6], Q[f, 5]))

        def side_row(r):
            v = []
            for k in range(2):
                _, w, _, g = beside[k][p]
                row = jnp.broadcast_to(XR[1 - k, g, r : r + 1, :], (8, W))
                v.append(piece(w, row))
            return jnp.where(r8 < 4, v[0], v[1])

        SX[p, E:EX, 0:W] = side_row(HEAT)
        SY[p, E:EX, 0:W] = side_row(CROSS)
        v = side_row(EDGE_Z)
        SZ[p, E:EX, 0:W] = jnp.where(
            (r8 == 0) | (r8 == 7), v, jnp.where(z8 < 8, lroll(v, -1), lroll(v, 1))
        )
        a = piece(beside[2][p][1], YR[1, beside[2][p][3]])
        c = piece(beside[3][p][1], YR[0, beside[3][p][3]])
        SX[p, 0:E, W:EL] = jnp.where(group < 4, lroll(a, E), c)
        SY[p, 0:E, W:EL] = jnp.where(group < 4, lroll(a, -5 * E), lroll(c, 2 * E))
        low = jnp.where(zh < 8, lroll(a, -5 * E - 1), lroll(a, 1 - 5 * E))
        low = jnp.where(group == 0, lroll(a, -6 * E), low)
        high = jnp.where(zh < 8, lroll(c, -1), lroll(c, 1))
        high = jnp.where(group == 7, lroll(c, E), high)
        SZ[p, 0:E, W:EL] = jnp.where(group < 4, low, high)

        def sgn(i):
            return 1 if CORNER_SRC[i][2] else -1

        ch = [corner_heat(i, p) for i in range(4)]
        SX[p, E:EX, W:EL] = quadrants(lambda i: ch[i])
        SY[p, E:EX, W:EL] = quadrants(
            lambda i: jnp.where(row_edge, lroll(ch[i], 4 * E), lroll(ch[i], sgn(i) * 5 * E))
        )
        SZ[p, E:EX, W:EL] = quadrants(lambda i: lroll(ch[i], sgn(i) * 2 * E))

    for p in range(NZ):
        sx, sy = SX[p], SY[p]
        heat = (rroll(sx, 1) + rroll(sx, -1)) + (lroll(sy, E) + lroll(sy, -E))
        heat = heat + (z_up(SZ, p) + z_down(SZ[p], SZ[p - 1] if p else None))
        acc = R[p] + jnp.where(KE[p] > 0.0, heat, 0.0)
        R[p] = acc
        d = acc * inv_center
        D[p] = d
        U[p] = TE[p, 0:E, 0:W] + d[0:E, 0:W]
    for n in range(2):
        before = None
        for p in range(NZ):
            v = D[p]
            div, before = divergence(v, z_up(D, p), p, before)
            r = R[p] - (v - div)
            d = coef[n][0] * v + coef[n][1] * r
            if n == 0:
                R[p] = r
                D[p] = d
            U[p] = U[p] + d[0:E, 0:W]
    for s in range(SB):
        TO[s] = U[own_z[s]]

    def x_face(b, side):
        shape = (8, W)
        df = -1 if side == 0 else 1
        dirn = 2 if side == 0 else 1
        bf = base_of(df, 0)
        main_id = nbr[b, dirn - 1]
        a = XR[side, slot(main_id, bf, FB)]
        val = a
        ids = jnp.full(shape, main_id)
        for r, p in enumerate(PX[side]):
            _, cy, cz = C[p]
            if r == 0:
                continue
            cid = nbr[b, OPP[p] - 1]
            if cy:
                corner = CR[CORNER_OF[p], slot(cid, base_of(df, -cy), FB)]
                corner = lroll(jnp.broadcast_to(corner, (8, H)), 4 * E)
                corner = jnp.concatenate([corner, corner], axis=1)
                edge = l8 < E if cy > 0 else l8 >= W - E
                cand = jnp.where(edge, corner, lroll(a, E * cy))
            else:
                other = XR[side, slot(cid, bf, FB)]
                edge = z8 == 0 if cz > 0 else z8 == E - 1
                cand = jnp.where(edge, lroll(other, -(E - 1) * cz), lroll(a, cz))
            val = jnp.where(r8 == r, cand, val)
            ids = jnp.where((r8 == r) & edge, jnp.full(shape, cid), ids)
        fall = XS[1 - side, b]
        wid = wall[b, dirn - 1]
        row = 7 if side == 0 else 0
        tw = XER[side, slot(wid, bf, SB), row : row + 1, :]
        hot = (r8 == HEAT) & (jnp.full(shape, wid) >= 0)
        fall = jnp.where(hot, 2.0 * tw - fall, fall)
        return jnp.where(ids >= 0, val, fall)

    def y_face(b, side):
        shape = (E, H)
        dc = -1 if side == 0 else 1
        dirn = 4 if side == 0 else 3
        bf = base_of(0, dc)
        main_id = nbr[b, dirn - 1]
        a = YR[side, slot(main_id, bf, FB)]
        val = a
        ids = jnp.full(shape, main_id)
        for r, p in enumerate(PY[side]):
            cx, _, cz = C[p]
            if r == 0:
                continue
            if cx:
                val = jnp.where(group == r, rroll(a, cx), val)
                continue
            cid = nbr[b, OPP[p] - 1]
            other = YR[side, slot(cid, bf, FB)]
            edge = zh == 0 if cz > 0 else zh == E - 1
            cand = jnp.where(edge, lroll(other, -(E - 1) * cz), lroll(a, cz))
            val = jnp.where(group == r, cand, val)
            ids = jnp.where((group == r) & edge, jnp.full(shape, cid), ids)
        fall = YS[1 - side, b]
        wid = wall[b, dirn - 1]
        tw = YER[side, slot(wid, bf, SB)]
        tw = lroll(tw, -2 * E if side == 0 else HEAT * E)
        hot = (group == HEAT) & (jnp.full(shape, wid) >= 0)
        fall = jnp.where(hot, 2.0 * tw - fall, fall)
        return jnp.where(ids >= 0, val, fall)

    for b in range(FB):
        for side in range(2):
            yf = y_face(b, side)
            half = pl.ds(0, H) if side == 0 else pl.ds(H, H)
            edge = lh < E if side == 0 else lh >= H - E
            back = 0 if side == 0 else H - E
            for q, p in enumerate(PY[side]):
                v = lroll(yf, back - E * q)
                GO[b, p, :, half] = jnp.where(edge, v, GO[b, p, :, half])
            v = lroll(yf, back - E * HEAT)
            QO[b, 3 + side, :, half] = jnp.where(edge, v, QO[b, 3 + side, :, half])
        for side in range(2):
            xf = x_face(b, side)
            x = 0 if side == 0 else E - 1
            for r, p in enumerate(PX[side]):
                GO[b, p, x : x + 1, :] = xf[r : r + 1]
            QO[b, 1 + side, x : x + 1, :] = xf[HEAT : HEAT + 1]

    for i in range(N_COPY):

        @pl.when(near(*steps[i]))
        def _():
            copies[i].wait_send()


def store_kernel(fluid, heat, solid, fluid_out, heat_out, solid_out, sem):
    pairs = [(fluid, fluid_out), (heat, heat_out), (solid, solid_out)]
    for i, (src, dst) in enumerate(pairs):
        for x in range(E):
            pltpu.make_async_copy(
                src.at[..., x, :], dst.at[..., pl.ds(W * x, W)], sem.at[i]
            ).start()
    for i, (src, dst) in enumerate(pairs):
        pltpu.make_async_copy(src, src, sem.at[i]).wait()


def body(nf, nc, fluid_pop, heat_pop, solid_temp, material, cond, nbr, wall, snbr, sflu):
    hbm = pl.BlockSpec(memory_space=pltpu.HBM)

    def vm(*shape):
        return pltpu.VMEM(shape, F32)

    vmem = pl.BlockSpec(memory_space=pltpu.VMEM)
    fields = pl.pallas_call(
        functools.partial(kernel, nf, nc),
        out_shape=(
            vm(FB, 19, E, W),
            vm(FB, 7, E, W),
            vm(SB, E, W),
        ),
        in_specs=[hbm] * 9,
        out_specs=(vmem, vmem, vmem),
        scratch_shapes=[
            vm(FB, 19, E, W),
            vm(FB, 7, E, W),
            vm(SB, E, W),
            pltpu.VMEM((SB, E, W), jnp.int32),
            vm(SB, E, W),
            vm(2, FB, 8, W),
            vm(2, FB, 8, W),
            vm(2, FB, E, H),
            vm(2, FB, E, H),
            vm(4, FB, 1, H),
            vm(4, FB, 1, H),
            vm(2, SB, 8, W),
            vm(2, SB, 8, W),
            vm(2, SB, E, H),
            vm(2, SB, E, H),
            vm(4, SB, 8, H),
        ]
        + [vm(NZ, EX, EL)] * 11
        + [
            vm(NZ, E, W),
            pltpu.SMEM(cond.shape, F32),
            pltpu.SMEM(nbr.shape, jnp.int32),
            pltpu.SMEM(wall.shape, jnp.int32),
            pltpu.SMEM(snbr.shape, jnp.int32),
            pltpu.SMEM(sflu.shape, jnp.int32),
            pltpu.SemaphoreType.DMA((13,)),
            pltpu.SemaphoreType.DMA((N_COPY,)),
            pltpu.SemaphoreType.DMA((N_COPY,)),
        ],
        compiler_params=pltpu.CompilerParams(
            collective_id=0, has_side_effects=True, vmem_limit_bytes=LIMIT
        ),
    )(fluid_pop, heat_pop, solid_temp, material, cond, nbr, wall, snbr, sflu)
    return pl.pallas_call(
        store_kernel,
        out_shape=(
            jax.ShapeDtypeStruct(fluid_pop.shape, F32),
            jax.ShapeDtypeStruct(heat_pop.shape, F32),
            jax.ShapeDtypeStruct(solid_temp.shape, F32),
        ),
        in_specs=[pl.BlockSpec(memory_space=pl.ANY)] * 3,
        out_specs=(hbm, hbm, hbm),
        scratch_shapes=[pltpu.SemaphoreType.DMA((3,))],
        compiler_params=pltpu.CompilerParams(vmem_limit_bytes=8 * 1024 * 1024),
    )(*fields)


def solution(mesh):
    both = ("flow", "cross")
    in_specs = (
        P(both, None, None),
        P(both, None, None),
        P(both, None),
        P(both, None),
        P(),
        P(both, None),
        P(both, None),
        P(both, None),
        P(both, None),
    )
    out_specs = (P(both, None, None), P(both, None, None), P(both, None))
    return jax.shard_map(
        functools.partial(body, mesh.shape["flow"], mesh.shape["cross"]),
        mesh=mesh,
        in_specs=in_specs,
        out_specs=out_specs,
        check_vma=False,
    )
```

```python
import functools

import jax
import jax.numpy as jnp
from jax import lax
from jax.experimental import pallas as pl
from jax.experimental.pallas import tpu as pltpu
from jax.sharding import PartitionSpec as P

MESH = pl.DeviceIdType.MESH
F32 = jnp.float32
E = 16
W = 256
H = 128
FB = 3
SB = 2
C = [
    (0, 0, 0),
    (1, 0, 0),
    (-1, 0, 0),
    (0, 1, 0),
    (0, -1, 0),
    (0, 0, 1),
    (0, 0, -1),
    (1, 1, 0),
    (-1, -1, 0),
    (1, -1, 0),
    (-1, 1, 0),
    (1, 0, 1),
    (-1, 0, -1),
    (1, 0, -1),
    (-1, 0, 1),
    (0, 1, 1),
    (0, -1, -1),
    (0, 1, -1),
    (0, -1, 1),
]
OPP = [0, 2, 1, 4, 3, 6, 5, 8, 7, 10, 9, 12, 11, 14, 13, 16, 15, 18, 17]
PX = ([1, 7, 9, 11, 13], [2, 8, 10, 12, 14])
PY = ([3, 7, 10, 15, 17], [4, 8, 9, 16, 18])
HEAT = 5
SIDES = [(1, 0), (-1, 0), (0, 1), (0, -1)]
CORNERS = [(1, 1), (1, -1), (-1, -1), (-1, 1)]
PEERS = SIDES + CORNERS
CORNER_SRC = [(0, 1, 1), (0, 2, 0), (1, 1, 0), (1, 2, 1)]
CORNER_OF = {7: 0, 9: 1, 8: 2, 10: 3}
EDGE_Z = 6
CROSS = 7
N_COPY = 16
NZ = 5
NONE = -9
EX = 24
EL = 384
LIMIT = 60 * 1024 * 1024


def lroll(v, s):
    n = v.shape[1]
    s = s % n
    return v if s == 0 else pltpu.roll(v, s, axis=1)


def rroll(v, s):
    n = v.shape[0]
    s = s % n
    return v if s == 0 else pltpu.roll(v, s, axis=0)


def lanes(shape):
    return lax.broadcasted_iota(jnp.int32, shape, 1)


def rows(shape):
    return lax.broadcasted_iota(jnp.int32, shape, 0)


def collide_tile(G, Q, b, rs, ls):
    def ld(p):
        return G[b, p, rs, ls]

    f = [ld(p) for p in range(19)]
    d = [None] * 19
    for p in (1, 3, 5, 7, 9, 11, 13, 15, 17):
        d[p] = f[p] - f[p + 1]
    s1 = ((f[1] + f[2]) + (f[3] + f[4])) + (f[5] + f[6])
    s2 = (((f[7] + f[8]) + (f[9] + f[10])) + ((f[11] + f[12]) + (f[13] + f[14]))) + (
        (f[15] + f[16]) + (f[17] + f[18])
    )
    rho = f[0] * (1.0 / 3.0) + s1 * (1.0 / 18.0) + s2 * (1.0 / 36.0)
    jx = d[1] * (1.0 / 18.0) + ((d[7] + d[9]) + (d[11] + d[13])) * (1.0 / 36.0)
    jy = d[3] * (1.0 / 18.0) + ((d[7] - d[9]) + (d[15] + d[17])) * (1.0 / 36.0)
    jz = d[5] * (1.0 / 18.0) + ((d[11] - d[13]) + (d[15] - d[17])) * (1.0 / 36.0)
    inv = 1.0 / rho
    u = (jx * inv, jy * inv, jz * inv)
    j = (jx, jy, jz)
    base = 1.25 * rho - 1.875 * (jx * u[0] + jy * u[1] + jz * u[2])
    G[b, 0, rs, ls] = base - 0.25 * f[0]
    cus = {}
    for p in (1, 3, 5, 7, 9, 11, 13, 15, 17):
        cj = None
        cu = None
        for a in range(3):
            s = C[p][a]
            if s == 0:
                continue
            if cj is None:
                cj, cu = j[a], u[a]
            elif s > 0:
                cj, cu = cj + j[a], cu + u[a]
            else:
                cj, cu = cj - j[a], cu - u[a]
        even = base + 5.625 * (cj * cu)
        odd = 3.75 * cj
        G[b, p, rs, ls] = (even + odd) - 0.25 * f[p]
        G[b, p + 1, rs, ls] = (even - odd) - 0.25 * f[p + 1]
        cus[p] = cu
    h = [Q[b, k, rs, ls] for k in range(7)]
    hs = ((h[1] + h[2]) + (h[3] + h[4])) + (h[5] + h[6])
    t11 = (h[0] * 0.25 + hs * 0.125) * 1.1
    t44 = 4.0 * t11
    Q[b, 0, rs, ls] = t11 - 0.1 * h[0]
    for k in (1, 3, 5):
        o = t44 * cus[k]
        Q[b, k, rs, ls] = (t11 + o) - 0.1 * h[k]
        Q[b, k + 1, rs, ls] = (t11 - o) - 0.1 * h[k + 1]


def kernel(
    nf,
    nc,
    fluid_in,
    heat_in,
    temp_in,
    mat_in,
    cond_in,
    nbr_in,
    wall_in,
    snbr_in,
    sflu_in,
    GO,
    QO,
    TO,
    G,
    Q,
    T,
    M,
    KAP,
    XS,
    XR,
    YS,
    YR,
    CS,
    CR,
    XES,
    XER,
    YES,
    YER,
    CER,
    TE,
    KE,
    WX,
    WY,
    WZ,
    LX,
    LY,
    LZ,
    R,
    CODE,
    cond,
    nbr,
    wall,
    snbr,
    sflu,
    in_sem,
    send_sem,
    recv_sem,
):
    fl = lax.axis_index("flow")
    cr = lax.axis_index("cross")
    inside = {-1: (fl > 0, cr > 0), 0: (True, True), 1: (fl < nf - 1, cr < nc - 1)}

    def near(df, dc):
        a, b = inside[df][0], inside[dc][1]
        if df == 0:
            return b
        return a if dc == 0 else jnp.logical_and(a, b)

    barrier = pltpu.get_barrier_semaphore()
    for df, dc in PEERS:

        @pl.when(near(df, dc))
        def _():
            pl.semaphore_signal(
                barrier, inc=1, device_id=(fl + df, cr + dc), device_id_type=MESH
            )

    nx = 2 - (fl == 0).astype(jnp.int32) - (fl == nf - 1).astype(jnp.int32)
    ny = 2 - (cr == 0).astype(jnp.int32) - (cr == nc - 1).astype(jnp.int32)
    n_peers = nx + ny + nx * ny

    def load(src, dst, sem):
        for x in range(E):
            pltpu.make_async_copy(
                src.at[..., pl.ds(W * x, W)], dst.at[..., x, :], sem
            ).start()

    def all_of(ref, sem):
        return pltpu.make_async_copy(ref, ref, sem)

    tables = [
        (cond_in, cond, 8),
        (nbr_in, nbr, 9),
        (wall_in, wall, 10),
        (snbr_in, snbr, 11),
        (sflu_in, sflu, 12),
    ]
    tables = [pltpu.make_async_copy(a, b, in_sem.at[i]) for a, b, i in tables]
    for c in tables:
        c.start()
    load(temp_in, T, in_sem.at[0])
    load(mat_in, M, in_sem.at[1])
    for b in range(FB):
        load(fluid_in.at[b], G.at[b], in_sem.at[2 + 2 * b])
        load(heat_in.at[b], Q.at[b], in_sem.at[3 + 2 * b])

    copies = {}
    steps = {}

    def send(i, src, dst, df, dc):
        copies[i] = pltpu.make_async_remote_copy(
            src_ref=src,
            dst_ref=dst,
            send_sem=send_sem.at[i],
            recv_sem=recv_sem.at[i],
            device_id=(fl + df, cr + dc),
            device_id_type=MESH,
        )
        steps[i] = (df, dc)

        @pl.when(near(df, dc))
        def _():
            copies[i].start()

    def received(i):
        @pl.when(near(-steps[i][0], -steps[i][1]))
        def _():
            copies[i].wait_recv()

    wide = (E, W)
    lw = lanes(wide)
    zw = jnp.bitwise_and(lw, E - 1)
    lh = lanes((E, H))
    zh = jnp.bitwise_and(lh, E - 1)
    group = jnp.right_shift(lh, 4)
    r8 = rows((8, W))
    l8 = lanes((8, W))
    z8 = jnp.bitwise_and(l8, E - 1)
    q8 = rows((8, H))
    g8 = jnp.right_shift(lanes((8, H)), 4)

    def base_of(df, dc):
        return (fl + df) * nc + (cr + dc)

    def slot(idv, base, n):
        return jnp.clip(idv - base * n, 0, n - 1)

    def num(flag):
        return jnp.where(flag, 1, 0)

    def on(flag, like):
        return jnp.full(like.shape, flag) > 0

    for c in tables:
        c.wait()

    here = base_of(0, 0)
    below0 = sflu[0, 5]
    below1 = sflu[1, 5]
    z0 = jnp.where(below0 >= 0, slot(below0, here, FB) + 1, 0)
    z1 = jnp.where(below1 >= 0, slot(below1, here, FB) + 2, z0 + 1)
    own_z = (z0, z1)
    flu_z = [b + num(b >= z0) + num(b + 1 >= z1) for b in range(FB)]

    def fluid_slot(za, zb, z):
        return jnp.clip(z - num(za < z) - num(zb < z), 0, FB - 1)

    nbr_z = []
    nbr_has = []
    for k in range(4):
        df, dc = C[k + 1][0], C[k + 1][1]
        first = base_of(df, dc) * SB
        za = zb = 0
        pairs = [(wall[b, k], flu_z[b]) for b in range(FB)]
        pairs += [(snbr[s, k], own_z[s]) for s in range(SB)]
        for idv, z in pairs:
            za = za + jnp.where(idv == first, z, 0)
            zb = zb + jnp.where(idv == first + 1, z, 0)
        has = num(near(df, dc))
        nbr_has.append(has)
        nbr_z.append((jnp.where(has > 0, za, NONE), jnp.where(has > 0, zb, NONE)))

    with jax.named_scope("wait_solid"):
        all_of(T, in_sem.at[0]).wait()
        all_of(M, in_sem.at[1]).wait()
    for s in range(SB):
        m = M[s]
        k = jnp.full(wide, cond[0], F32)
        for i in range(1, 8):
            k = jnp.where(m == i, cond[i], k)
        KAP[s] = k
        zf = jnp.full((8, W), own_z[s]).astype(F32)
        t = T[s]
        XES[0, s] = jnp.where(r8 > 4, t[8:], jnp.where(r8 == 4, zf, rroll(k[8:], 4)))
        XES[1, s] = jnp.where(r8 < 3, t[:8], jnp.where(r8 == 3, zf, rroll(k[:8], 4)))
        YES[0, s] = jnp.where(lh >= 64, t[:, H:], lroll(k[:, H:], 64))
        YES[1, s] = jnp.where(lh < 64, t[:, :H], lroll(k[:, :H], 64))

    with jax.named_scope("entry_barrier"):
        pl.semaphore_wait(barrier, n_peers)
    for i, (df, dc) in enumerate(SIDES):
        side = i % 2
        if i < 2:
            send(i, XES.at[side], XER.at[side], df, dc)
        else:
            send(i, YES.at[side], YER.at[side], df, dc)
    for i, (df, dc) in enumerate(CORNERS):
        side, _, half = CORNER_SRC[i]
        send(4 + i, XES.at[side, :, :, pl.ds(H * half, H)], CER.at[i], df, dc)

    def pack_y(pieces, side):
        acc = None
        for g, v in enumerate(pieces):
            r = lroll(v, E * g - (H - E)) if side == 0 else lroll(v, E * g)
            acc = r if acc is None else jnp.where(group == g, r, acc)
        return acc

    def two(v, first, second, z):
        return jnp.where((z == 0) | (z == E - 1), v, jnp.where(z < 8, first, second))

    for b in range(FB):
        with jax.named_scope("wait_pops"):
            all_of(G.at[b], in_sem.at[2 + 2 * b]).wait()
            all_of(Q.at[b], in_sem.at[3 + 2 * b]).wait()
        with jax.named_scope("collide"):
            for xh in range(2):
                for yh in range(2):
                    collide_tile(G, Q, b, pl.ds(8 * xh, 8), pl.ds(H * yh, H))
        for side in range(2):
            x = E - 1 if side == 0 else 0
            inner = E - 2 if side == 0 else 1

            def line(x_at, lo, n):
                zz = jnp.bitwise_and(lanes((1, n)), E - 1)
                up = Q[b, 6, x_at : x_at + 1, lo : lo + n]
                return jnp.where(zz < 8, up, Q[b, 5, x_at : x_at + 1, lo : lo + n])

            for r in range(5):
                XS[side, b, r : r + 1, :] = G[b, PX[side][r], x : x + 1, :]
            XS[side, b, HEAT : HEAT + 1, :] = Q[b, 1 + side, x : x + 1, :]
            z1w = jnp.bitwise_and(lanes((1, W)), E - 1)
            v = line(inner, 0, W)
            XS[side, b, EDGE_Z : EDGE_Z + 1, :] = two(
                line(x, 0, W), lroll(v, 1), lroll(v, -1), z1w
            )
            XS[side, b, CROSS : CROSS + 1, :H] = Q[b, 4, x : x + 1, :H]
            XS[side, b, CROSS : CROSS + 1, H:] = Q[b, 3, x : x + 1, H:]

            half = pl.ds(H, H) if side == 0 else pl.ds(0, H)
            sgn = 1 if side == 0 else -1
            hz = jnp.where(zh < 8, Q[b, 6, :, half], Q[b, 5, :, half])
            hx = jnp.concatenate([Q[b, 2, 0:8, half], Q[b, 1, 8:16, half]], axis=0)
            YS[side, b] = pack_y(
                [G[b, PY[side][r], :, half] for r in range(5)]
                + [
                    Q[b, 3 + side, :, half],
                    two(hz, lroll(hz, sgn * E + 1), lroll(hz, sgn * E - 1), zh),
                    hx,
                ],
                side,
            )
            for i in range(4):
                cs, row, ch = CORNER_SRC[i]
                if cs != side:
                    continue
                sg = -1 if ch else 1
                hp = 3 if ch else 4
                lo = H * ch
                gg = jnp.right_shift(lanes((1, H)), 4)
                at = (lambda d: 7 - d) if ch else (lambda d: d)
                acc = Q[b, 1 + side, x : x + 1, lo : lo + H]
                extra = [
                    (2, line(x, lo, H)),
                    (3, G[b, PX[side][row], x : x + 1, lo : lo + H]),
                    (4, Q[b, hp, x : x + 1, lo : lo + H]),
                    (5, Q[b, hp, inner : inner + 1, lo : lo + H]),
                ]
                for d, v in extra:
                    acc = jnp.where(gg == at(d), lroll(v, sg * E * d), acc)
                CS[i, b] = acc

    for i, (df, dc) in enumerate(SIDES):
        side = i % 2
        if i < 2:
            send(8 + i, XS.at[side], XR.at[side], df, dc)
        else:
            send(8 + i, YS.at[side], YR.at[side], df, dc)
    for i, (df, dc) in enumerate(CORNERS):
        send(12 + i, CS.at[i], CR.at[i], df, dc)

    def stream(b):
        def main(ref, p):
            cx, cy, cz = C[p]
            s = E * cy + cz
            out = lroll(rroll(ref[b, p], cx), s)
            if cz:
                back = ref[b, OPP[p]]
                adj = (b - cz) % FB
                if ref is Q:
                    wid = wall[b, (6 if cz > 0 else 5) - 1]
                    tw = lroll(T[slot(wid, here, SB)], -(E - 1) * cz)
                    back = jnp.where(jnp.full(wide, wid) >= 0, 2.0 * tw - back, back)
                if 0 <= b - cz < FB:
                    other = lroll(rroll(ref[adj, p], cx), E * cy - (E - 1) * cz)
                    zid = nbr[b, (6 if cz > 0 else 5) - 1]
                    back = jnp.where(jnp.full(wide, zid) >= 0, other, back)
                edge = zw == 0 if cz > 0 else zw == E - 1
                out = jnp.where(edge, back, out)
            return out

        GO[b, 0] = G[b, 0]
        QO[b, 0] = Q[b, 0]
        for p in range(1, 19):
            GO[b, p] = main(G, p)
        for p in range(1, 7):
            QO[b, p] = main(Q, p)

    with jax.named_scope("stream"):
        for b in range(FB):
            stream(b)

    ext = (EX, EL)
    ze = jnp.bitwise_and(lanes(ext), E - 1)

    def piece(flag, v):
        return jnp.where(on(flag, v), v, 0.0)

    for i in range(8):
        received(i)

    def corner_z(i):
        side = CORNER_SRC[i][0]
        r = 4 if side == 0 else 3
        return [
            jnp.broadcast_to(CER[i, s, r : r + 1, :], (8, H))
            for s in range(SB)
        ]

    quad = [[2, 3], [1, 0]]
    chas = [jnp.full((8, H), num(near(-df, -dc))) > 0 for df, dc in CORNERS]
    cz = [[jnp.where(chas[i], v, float(NONE)) for v in corner_z(i)] for i in range(4)]

    def quadrants(fn):
        up = jnp.where(g8 < 4, fn(quad[0][0]), fn(quad[0][1]))
        down = jnp.where(g8 < 4, fn(quad[1][0]), fn(quad[1][1]))
        return jnp.where(q8 < 4, up, down)

    def splat(shape, v):
        return jnp.full(shape, v).astype(F32)

    Z = []
    for s in range(SB):
        TE[s, 0:E, 0:W] = T[s]
        KE[s, 0:E, 0:W] = KAP[s]
        a = piece(nbr_has[0], XER[1, s])
        c = piece(nbr_has[1], XER[0, s])
        TE[s, E:EX, 0:W] = jnp.where(r8 < 4, a, c)
        KE[s, E:EX, 0:W] = rroll(jnp.where(r8 < 4, c, a), 4)
        zx = jnp.where(r8 < 4, splat((8, W), nbr_z[0][s]), splat((8, W), nbr_z[1][s]))
        a = piece(nbr_has[2], YER[1, s])
        c = piece(nbr_has[3], YER[0, s])
        TE[s, 0:E, W:EL] = jnp.where(group < 4, a, c)
        KE[s, 0:E, W:EL] = lroll(jnp.where(group < 4, c, a), 64)
        zy = jnp.where(group < 4, splat((E, H), nbr_z[2][s]), splat((E, H), nbr_z[3][s]))

        def corner_solid(i):
            return jnp.where(chas[i], CER[i, s], 0.0)

        TE[s, E:EX, W:EL] = quadrants(corner_solid)
        KE[s, E:EX, W:EL] = quadrants(lambda i: rroll(corner_solid(i), 4))
        top = jnp.concatenate([splat(wide, own_z[s]), zy], axis=1)
        low = jnp.concatenate([zx, quadrants(lambda i: cz[i][s])], axis=1)
        Z.append(jnp.concatenate([top, low], axis=0))

    def link(k, kb):
        return (2.0 * k * kb) / jnp.maximum(k + kb, 0.05)

    def toward(k, v):
        return rroll(v, -1 if k == 0 else 1) if k < 2 else lroll(v, -E if k == 2 else E)

    wet = [[0.0, 0.0] for _ in range(SB)]
    for k in range(4):
        za, zb = toward(k, Z[0]), toward(k, Z[1])
        for s in range(SB):
            code = jnp.where(zb == Z[s], 1, jnp.where(za == Z[s], 0, 2))
            CODE[k, s] = code
            wet[s][k // 2] = jnp.where((code == 2) & (za >= 0.0), 1.0, wet[s][k // 2])
    adj = Z[1] == Z[0] + 1.0
    top, bottom = ze == E - 1, ze == 0
    wet_z = [
        (top & (~adj) & (Z[0] < NZ - 1.0) & (Z[0] >= 0.0)) | (bottom & (Z[0] > 0.0)),
        (top & (Z[1] < NZ - 1.0) & (Z[1] >= 0.0)) | (bottom & (~adj) & (Z[1] >= 0.0)),
    ]
    for s in range(SB):
        WX[s] = wet[s][0]
        WY[s] = wet[s][1]
        WZ[s] = jnp.where(wet_z[s], 1.0, 0.0)

    def chosen(k, s, v):
        code = CODE[k, s]
        return jnp.where(code == 1, v[1], jnp.where(code == 0, v[0], 0.0))

    def z_up(v):
        return [jnp.where(top, lroll(v[1], E - 1), lroll(v[0], -1)), lroll(v[1], -1)]

    def divergence(v):
        div = []
        for k, links in ((0, LX), (2, LY)):
            over = [toward(k, x) for x in v]
            f = [
                links[s] * (jnp.where(CODE[k, s] == 1, over[1], over[0]) - v[s])
                for s in range(SB)
            ]
            under = [toward(k + 1, x) for x in f]
            part = [f[s] - chosen(k + 1, s, under) for s in range(SB)]
            div = part if k == 0 else [a + b for a, b in zip(div, part)]
        up = z_up(v)
        f = [LZ[s] * (up[s] - v[s]) for s in range(SB)]
        under = [
            jnp.where(bottom, 0.0, lroll(f[0], 1)),
            jnp.where(bottom, lroll(f[0], 1 - E), lroll(f[1], 1)),
        ]
        return [div[s] + (f[s] - under[s]) for s in range(SB)]

    kk = [KE[s] for s in range(SB)]
    for k, links in ((0, LX), (2, LY)):
        over = [toward(k, x) for x in kk]
        for s in range(SB):
            links[s] = link(kk[s], chosen(k, s, over))
    up = z_up(kk)
    LZ[0] = link(kk[0], jnp.where(top & ~adj, 0.0, up[0]))
    LZ[1] = link(kk[1], jnp.where(top, 0.0, up[1]))
    tt = [TE[s] for s in range(SB)]
    div = divergence(tt)
    for s in range(SB):
        R[s] = div[s] - (WX[s] + WY[s] + WZ[s]) * tt[s]

    kmax = cond[0]
    for i in range(1, 8):
        kmax = jnp.maximum(kmax, cond[i])
    radius = jnp.full((8, H), kmax * 6.0, F32)
    center = radius + 1.0
    sigma = center / radius

    def grow(v):
        v = jnp.concatenate([v] * (EX // 8), axis=0)
        return jnp.concatenate([v] * (EL // H), axis=1)

    inv_center = grow(1.0 / center)
    rho0 = 1.0 / sigma
    rho1 = 1.0 / (2.0 * sigma - rho0)
    rho2 = 1.0 / (2.0 * sigma - rho1)
    coef = [
        (grow(rho1 * rho0), grow(2.0 * rho1 / radius)),
        (grow(rho2 * rho1), grow(2.0 * rho2 / radius)),
    ]

    with jax.named_scope("wait_faces"):
        for i in range(8, 16):
            received(i)

    def corner_heat(i, z):
        f = z - jnp.where(cz[i][0] < z, 1.0, 0.0) - jnp.where(cz[i][1] < z, 1.0, 0.0)
        a, b, c = [jnp.broadcast_to(CR[i, j], (8, H)) for j in range(FB)]
        return jnp.where(f < 0.5, a, jnp.where(f < 1.5, b, c))

    def of_three(za, zb, z, fn):
        f = z - jnp.where(za < z, 1.0, 0.0) - jnp.where(zb < z, 1.0, 0.0)
        return jnp.where(f < 0.5, fn(0), jnp.where(f < 1.5, fn(1), fn(2)))

    row_edge = (q8 == 0) | (q8 == 7)
    wide_edge = (r8 == 0) | (r8 == 7)

    def stack(v):
        return jnp.concatenate([v, v], axis=0)

    for s in range(SB):
        oz = own_z[s]
        nz = [nbr_z[k][s] for k in range(4)]
        ozf = splat((8, H), oz)
        nzf = [splat((8, H), z) for z in nz]
        f_side = [fluid_slot(nbr_z[k][0], nbr_z[k][1], oz) for k in range(4)]
        f_own = [fluid_slot(z0, z1, nz[k]) for k in range(4)]

        own_lo = jnp.broadcast_to(XR[0, f_side[1], HEAT : HEAT + 1, :], (8, W))
        own_hi = jnp.broadcast_to(XR[1, f_side[0], HEAT : HEAT + 1, :], (8, W))
        x_tile = jnp.where(
            r8 < 4,
            jnp.broadcast_to(Q[f_own[0], 1, E - 1 : E, :], (8, W)),
            jnp.broadcast_to(Q[f_own[1], 2, 0:1, :], (8, W)),
        )
        y_lo = jnp.where(g8 < 4, corner_heat(1, nzf[2]), corner_heat(0, nzf[3]))
        y_hi = jnp.where(g8 < 4, corner_heat(2, nzf[2]), corner_heat(3, nzf[3]))

        def from_y(i):
            half = CORNER_SRC[i][2]
            k = 3 if half else 2
            row = 0 if i < 2 else E - 1
            v = of_three(
                nbr_z[k][0],
                nbr_z[k][1],
                cz[i][s],
                lambda j: jnp.broadcast_to(YR[1 - half, j, row : row + 1, :], (8, H))
                if not half
                else jnp.broadcast_to(YR[0, j, row : row + 1, :], (8, H)),
            )
            return v if half else lroll(v, E)

        heat = jnp.concatenate(
            [
                jnp.concatenate([own_lo, y_lo], axis=1),
                jnp.concatenate([own_hi, y_hi], axis=1),
                jnp.concatenate([x_tile, quadrants(from_y)], axis=1),
            ],
            axis=0,
        )
        acc = R[s] + jnp.where(WX[s] > 0.5, heat, 0.0)

        left = lroll(YR[0, f_side[3]], -5 * E)
        right = lroll(YR[1, f_side[2]], 2 * E)

        def from_corner(i, z):
            v = corner_heat(i, z)
            if CORNER_SRC[i][2]:
                return jnp.where(row_edge, lroll(v, -3 * E), lroll(v, -2 * E))
            return jnp.where(row_edge, lroll(v, 3 * E), lroll(v, 2 * E))

        x_left = jnp.where(q8 < 4, from_corner(3, nzf[0]), from_corner(0, nzf[1]))
        x_right = jnp.where(q8 < 4, from_corner(2, nzf[0]), from_corner(1, nzf[1]))
        y_tile = jnp.where(
            group < 4,
            lroll(Q[f_own[2], 3, :, H:W], E),
            lroll(Q[f_own[3], 4, :, 0:H], -E),
        )

        def from_x(i):
            half = CORNER_SRC[i][2]
            k = 1 if i < 2 else 0
            lo = 0 if half else H
            v = of_three(
                nbr_z[k][0],
                nbr_z[k][1],
                cz[i][s],
                lambda j: jnp.broadcast_to(
                    XR[1 - k, j, CROSS : CROSS + 1, lo : lo + H], (8, H)
                ),
            )
            return lroll(v, -E if half else E)

        heat = jnp.concatenate(
            [
                jnp.concatenate([left, right, y_tile], axis=1),
                jnp.concatenate([x_left, x_right, quadrants(from_x)], axis=1),
            ],
            axis=0,
        )
        acc = acc + jnp.where(WY[s] > 0.5, heat, 0.0)

        def updown(k):
            za, zb = nbr_z[k]
            return fluid_slot(za, zb, nz[k] + 1), fluid_slot(za, zb, nz[k] - 1)

        tile = jnp.where(
            zw < 8,
            lroll(Q[fluid_slot(z0, z1, oz - 1), 5], 1 - E),
            lroll(Q[fluid_slot(z0, z1, oz + 1), 6], E - 1),
        )
        a, c = [], []
        for k in range(2):
            u, d = updown(k)
            a.append(jnp.broadcast_to(XR[1 - k, u, EDGE_Z : EDGE_Z + 1, :], (8, W)))
            c.append(jnp.broadcast_to(XR[1 - k, d, EDGE_Z : EDGE_Z + 1, :], (8, W)))
        a = jnp.where(r8 < 4, a[0], a[1])
        c = jnp.where(r8 < 4, c[0], c[1])
        x_tile = jnp.where(
            z8 < 8,
            jnp.where(wide_edge, lroll(c, 1 - E), lroll(c, 2 - E)),
            jnp.where(wide_edge, lroll(a, E - 1), lroll(a, E - 2)),
        )
        u, d = updown(2)
        a, c = YR[1, u], YR[1, d]
        y_up = jnp.where(
            zh < 8,
            jnp.where(group == 0, lroll(c, -7 * E + 1), lroll(c, -6 * E + 2)),
            jnp.where(group == 0, lroll(a, -5 * E - 1), lroll(a, -4 * E - 2)),
        )
        u, d = updown(3)
        a, c = YR[0, u], YR[0, d]
        y_down = jnp.where(
            zh < 8,
            jnp.where(group == 7, lroll(c, 1), lroll(c, 2 - E)),
            jnp.where(group == 7, lroll(a, 2 * E - 1), lroll(a, E - 2)),
        )

        def from_z(i):
            shift = 2 * E if CORNER_SRC[i][2] else -2 * E
            a = lroll(corner_heat(i, cz[i][s] + 1.0), shift + E - 1)
            c = lroll(corner_heat(i, cz[i][s] - 1.0), shift + 1 - E)
            return jnp.where(z8[:, :H] < 8, c, a)

        heat = jnp.concatenate(
            [
                jnp.concatenate([tile, jnp.where(group < 4, y_up, y_down)], axis=1),
                jnp.concatenate([x_tile, quadrants(from_z)], axis=1),
            ],
            axis=0,
        )
        R[s] = acc + jnp.where(WZ[s] > 0.5, heat, 0.0)

    upd = []
    sol = []
    for s in range(SB):
        d = R[s] * inv_center
        upd.append(d)
        sol.append(T[s] + d[0:E, 0:W])
    for n in range(2):
        div = divergence(upd)
        for s in range(SB):
            r = R[s] - (upd[s] - div[s])
            d = coef[n][0] * upd[s] + coef[n][1] * r
            if n == 0:
                R[s] = r
            upd[s] = d
            sol[s] = sol[s] + d[0:E, 0:W]
    for s in range(SB):
        TO[s] = sol[s]

    def x_face(b, side):
        shape = (8, W)
        df = -1 if side == 0 else 1
        dirn = 2 if side == 0 else 1
        bf = base_of(df, 0)
        main_id = nbr[b, dirn - 1]
        a = XR[side, slot(main_id, bf, FB)]
        val = a
        ids = jnp.full(shape, main_id)
        for r, p in enumerate(PX[side]):
            _, cy, cz = C[p]
            if r == 0:
                continue
            cid = nbr[b, OPP[p] - 1]
            if cy:
                corner = CR[CORNER_OF[p], slot(cid, base_of(df, -cy), FB)]
                corner = lroll(jnp.broadcast_to(corner, (8, H)), 4 * E)
                corner = jnp.concatenate([corner, corner], axis=1)
                edge = l8 < E if cy > 0 else l8 >= W - E
                cand = jnp.where(edge, corner, lroll(a, E * cy))
            else:
                other = XR[side, slot(cid, bf, FB)]
                edge = z8 == 0 if cz > 0 else z8 == E - 1
                cand = jnp.where(edge, lroll(other, -(E - 1) * cz), lroll(a, cz))
            val = jnp.where(r8 == r, cand, val)
            ids = jnp.where((r8 == r) & edge, jnp.full(shape, cid), ids)
        fall = XS[1 - side, b]
        wid = wall[b, dirn - 1]
        row = 7 if side == 0 else 0
        tw = XER[side, slot(wid, bf, SB), row : row + 1, :]
        hot = (r8 == HEAT) & (jnp.full(shape, wid) >= 0)
        fall = jnp.where(hot, 2.0 * tw - fall, fall)
        return jnp.where(ids >= 0, val, fall)

    def y_face(b, side):
        shape = (E, H)
        dc = -1 if side == 0 else 1
        dirn = 4 if side == 0 else 3
        bf = base_of(0, dc)
        main_id = nbr[b, dirn - 1]
        a = YR[side, slot(main_id, bf, FB)]
        val = a
        ids = jnp.full(shape, main_id)
        for r, p in enumerate(PY[side]):
            cx, _, cz = C[p]
            if r == 0:
                continue
            if cx:
                val = jnp.where(group == r, rroll(a, cx), val)
                continue
            cid = nbr[b, OPP[p] - 1]
            other = YR[side, slot(cid, bf, FB)]
            edge = zh == 0 if cz > 0 else zh == E - 1
            cand = jnp.where(edge, lroll(other, -(E - 1) * cz), lroll(a, cz))
            val = jnp.where(group == r, cand, val)
            ids = jnp.where((group == r) & edge, jnp.full(shape, cid), ids)
        fall = YS[1 - side, b]
        wid = wall[b, dirn - 1]
        tw = YER[side, slot(wid, bf, SB)]
        tw = lroll(tw, -2 * E if side == 0 else HEAT * E)
        hot = (group == HEAT) & (jnp.full(shape, wid) >= 0)
        fall = jnp.where(hot, 2.0 * tw - fall, fall)
        return jnp.where(ids >= 0, val, fall)

    for b in range(FB):
        for side in range(2):
            yf = y_face(b, side)
            half = pl.ds(0, H) if side == 0 else pl.ds(H, H)
            edge = lh < E if side == 0 else lh >= H - E
            back = 0 if side == 0 else H - E
            for q, p in enumerate(PY[side]):
                v = lroll(yf, back - E * q)
                GO[b, p, :, half] = jnp.where(edge, v, GO[b, p, :, half])
            v = lroll(yf, back - E * HEAT)
            QO[b, 3 + side, :, half] = jnp.where(edge, v, QO[b, 3 + side, :, half])
        for side in range(2):
            xf = x_face(b, side)
            x = 0 if side == 0 else E - 1
            for r, p in enumerate(PX[side]):
                GO[b, p, x : x + 1, :] = xf[r : r + 1]
            QO[b, 1 + side, x : x + 1, :] = xf[HEAT : HEAT + 1]

    for i in range(N_COPY):

        @pl.when(near(*steps[i]))
        def _():
            copies[i].wait_send()


def store_kernel(fluid, heat, solid, fluid_out, heat_out, solid_out, sem):
    pairs = [(fluid, fluid_out), (heat, heat_out), (solid, solid_out)]
    for i, (src, dst) in enumerate(pairs):
        for x in range(E):
            pltpu.make_async_copy(
                src.at[..., x, :], dst.at[..., pl.ds(W * x, W)], sem.at[i]
            ).start()
    for i, (src, dst) in enumerate(pairs):
        pltpu.make_async_copy(src, src, sem.at[i]).wait()


def body(nf, nc, fluid_pop, heat_pop, solid_temp, material, cond, nbr, wall, snbr, sflu):
    hbm = pl.BlockSpec(memory_space=pltpu.HBM)

    def vm(*shape):
        return pltpu.VMEM(shape, F32)

    vmem = pl.BlockSpec(memory_space=pltpu.VMEM)
    fields = pl.pallas_call(
        functools.partial(kernel, nf, nc),
        out_shape=(
            vm(FB, 19, E, W),
            vm(FB, 7, E, W),
            vm(SB, E, W),
        ),
        in_specs=[hbm] * 9,
        out_specs=(vmem, vmem, vmem),
        scratch_shapes=[
            vm(FB, 19, E, W),
            vm(FB, 7, E, W),
            vm(SB, E, W),
            pltpu.VMEM((SB, E, W), jnp.int32),
            vm(SB, E, W),
            vm(2, FB, 8, W),
            vm(2, FB, 8, W),
            vm(2, FB, E, H),
            vm(2, FB, E, H),
            vm(4, FB, 1, H),
            vm(4, FB, 1, H),
            vm(2, SB, 8, W),
            vm(2, SB, 8, W),
            vm(2, SB, E, H),
            vm(2, SB, E, H),
            vm(4, SB, 8, H),
        ]
        + [vm(SB, EX, EL)] * 9
        + [
            pltpu.VMEM((4, SB, EX, EL), jnp.int32),
            pltpu.SMEM(cond.shape, F32),
            pltpu.SMEM(nbr.shape, jnp.int32),
            pltpu.SMEM(wall.shape, jnp.int32),
            pltpu.SMEM(snbr.shape, jnp.int32),
            pltpu.SMEM(sflu.shape, jnp.int32),
            pltpu.SemaphoreType.DMA((13,)),
            pltpu.SemaphoreType.DMA((N_COPY,)),
            pltpu.SemaphoreType.DMA((N_COPY,)),
        ],
        compiler_params=pltpu.CompilerParams(
            collective_id=0, has_side_effects=True, vmem_limit_bytes=LIMIT
        ),
    )(fluid_pop, heat_pop, solid_temp, material, cond, nbr, wall, snbr, sflu)
    return pl.pallas_call(
        store_kernel,
        out_shape=(
            jax.ShapeDtypeStruct(fluid_pop.shape, F32),
            jax.ShapeDtypeStruct(heat_pop.shape, F32),
            jax.ShapeDtypeStruct(solid_temp.shape, F32),
        ),
        in_specs=[pl.BlockSpec(memory_space=pl.ANY)] * 3,
        out_specs=(hbm, hbm, hbm),
        scratch_shapes=[pltpu.SemaphoreType.DMA((3,))],
        compiler_params=pltpu.CompilerParams(vmem_limit_bytes=8 * 1024 * 1024),
    )(*fields)


def solution(mesh):
    both = ("flow", "cross")
    in_specs = (
        P(both, None, None),
        P(both, None, None),
        P(both, None),
        P(both, None),
        P(),
        P(both, None),
        P(both, None),
        P(both, None),
        P(both, None),
    )
    out_specs = (P(both, None, None), P(both, None, None), P(both, None))
    return jax.shard_map(
        functools.partial(body, mesh.shape["flow"], mesh.shape["cross"]),
        mesh=mesh,
        in_specs=in_specs,
        out_specs=out_specs,
        check_vma=False,
    )
```

```python
import functools

import jax
import jax.numpy as jnp
from jax import lax
from jax.experimental import pallas as pl
from jax.experimental.pallas import tpu as pltpu
from jax.sharding import PartitionSpec as P

MESH = pl.DeviceIdType.MESH
F32 = jnp.float32
E = 16
W = 256
H = 128
FB = 3
SB = 2
C = [
    (0, 0, 0),
    (1, 0, 0),
    (-1, 0, 0),
    (0, 1, 0),
    (0, -1, 0),
    (0, 0, 1),
    (0, 0, -1),
    (1, 1, 0),
    (-1, -1, 0),
    (1, -1, 0),
    (-1, 1, 0),
    (1, 0, 1),
    (-1, 0, -1),
    (1, 0, -1),
    (-1, 0, 1),
    (0, 1, 1),
    (0, -1, -1),
    (0, 1, -1),
    (0, -1, 1),
]
OPP = [0, 2, 1, 4, 3, 6, 5, 8, 7, 10, 9, 12, 11, 14, 13, 16, 15, 18, 17]
PX = ([1, 7, 9, 11, 13], [2, 8, 10, 12, 14])
PY = ([3, 7, 10, 15, 17], [4, 8, 9, 16, 18])
HEAT = 5
SIDES = [(1, 0), (-1, 0), (0, 1), (0, -1)]
CORNERS = [(1, 1), (1, -1), (-1, -1), (-1, 1)]
PEERS = CORNERS + SIDES
CORNER_SRC = [(0, 1, 1), (0, 2, 0), (1, 1, 0), (1, 2, 1)]
CORNER_OF = {7: 0, 9: 1, 8: 2, 10: 3}
EDGE_Z = 6
CROSS = 7
N_COPY = 8
NZ = 5
NONE = -9
EX = 24
EL = 384
LIMIT = 60 * 1024 * 1024


def lroll(v, s):
    n = v.shape[1]
    s = s % n
    return v if s == 0 else pltpu.roll(v, s, axis=1)


def rroll(v, s):
    n = v.shape[0]
    s = s % n
    return v if s == 0 else pltpu.roll(v, s, axis=0)


def lanes(shape):
    return lax.broadcasted_iota(jnp.int32, shape, 1)


def rows(shape):
    return lax.broadcasted_iota(jnp.int32, shape, 0)


def collide_tile(G, Q, b, rs, ls):
    def ld(p):
        return G[b, p, rs, ls]

    f = [ld(p) for p in range(19)]
    d = [None] * 19
    for p in (1, 3, 5, 7, 9, 11, 13, 15, 17):
        d[p] = f[p] - f[p + 1]
    s1 = ((f[1] + f[2]) + (f[3] + f[4])) + (f[5] + f[6])
    s2 = (((f[7] + f[8]) + (f[9] + f[10])) + ((f[11] + f[12]) + (f[13] + f[14]))) + (
        (f[15] + f[16]) + (f[17] + f[18])
    )
    rho = f[0] * (1.0 / 3.0) + s1 * (1.0 / 18.0) + s2 * (1.0 / 36.0)
    jx = d[1] * (1.0 / 18.0) + ((d[7] + d[9]) + (d[11] + d[13])) * (1.0 / 36.0)
    jy = d[3] * (1.0 / 18.0) + ((d[7] - d[9]) + (d[15] + d[17])) * (1.0 / 36.0)
    jz = d[5] * (1.0 / 18.0) + ((d[11] - d[13]) + (d[15] - d[17])) * (1.0 / 36.0)
    inv = 1.0 / rho
    u = (jx * inv, jy * inv, jz * inv)
    j = (jx, jy, jz)
    base = 1.25 * rho - 1.875 * (jx * u[0] + jy * u[1] + jz * u[2])
    G[b, 0, rs, ls] = base - 0.25 * f[0]
    cus = {}
    for p in (1, 3, 5, 7, 9, 11, 13, 15, 17):
        cj = None
        cu = None
        for a in range(3):
            s = C[p][a]
            if s == 0:
                continue
            if cj is None:
                cj, cu = j[a], u[a]
            elif s > 0:
                cj, cu = cj + j[a], cu + u[a]
            else:
                cj, cu = cj - j[a], cu - u[a]
        even = base + 5.625 * (cj * cu)
        odd = 3.75 * cj
        G[b, p, rs, ls] = (even + odd) - 0.25 * f[p]
        G[b, p + 1, rs, ls] = (even - odd) - 0.25 * f[p + 1]
        cus[p] = cu
    h = [Q[b, k, rs, ls] for k in range(7)]
    hs = ((h[1] + h[2]) + (h[3] + h[4])) + (h[5] + h[6])
    t11 = (h[0] * 0.25 + hs * 0.125) * 1.1
    t44 = 4.0 * t11
    Q[b, 0, rs, ls] = t11 - 0.1 * h[0]
    for k in (1, 3, 5):
        o = t44 * cus[k]
        Q[b, k, rs, ls] = (t11 + o) - 0.1 * h[k]
        Q[b, k + 1, rs, ls] = (t11 - o) - 0.1 * h[k + 1]


def kernel(
    nf,
    nc,
    fluid_in,
    heat_in,
    temp_in,
    mat_in,
    cond_in,
    nbr_in,
    wall_in,
    snbr_in,
    sflu_in,
    GO,
    QO,
    TO,
    G,
    Q,
    T,
    M,
    KAP,
    FX,
    FY,
    XS,
    XR,
    YS,
    YR,
    CS,
    CR,
    TE,
    KE,
    WX,
    WY,
    WZ,
    LX,
    LY,
    LZ,
    R,
    CODE,
    cond,
    nbr,
    wall,
    snbr,
    sflu,
    in_sem,
    send_sem,
    recv_sem,
):
    fl = lax.axis_index("flow")
    cr = lax.axis_index("cross")
    inside = {-1: (fl > 0, cr > 0), 0: (True, True), 1: (fl < nf - 1, cr < nc - 1)}

    def near(df, dc):
        a, b = inside[df][0], inside[dc][1]
        if df == 0:
            return b
        return a if dc == 0 else jnp.logical_and(a, b)

    barrier = pltpu.get_barrier_semaphore()
    for df, dc in PEERS:

        @pl.when(near(df, dc))
        def _():
            pl.semaphore_signal(
                barrier, inc=1, device_id=(fl + df, cr + dc), device_id_type=MESH
            )

    nx = 2 - (fl == 0).astype(jnp.int32) - (fl == nf - 1).astype(jnp.int32)
    ny = 2 - (cr == 0).astype(jnp.int32) - (cr == nc - 1).astype(jnp.int32)
    n_peers = nx + ny + nx * ny

    def load(src, dst, sem):
        for x in range(E):
            pltpu.make_async_copy(
                src.at[..., pl.ds(W * x, W)], dst.at[..., x, :], sem
            ).start()

    def all_of(ref, sem):
        return pltpu.make_async_copy(ref, ref, sem)

    tables = [
        (cond_in, cond, 4),
        (nbr_in, nbr, 5),
        (wall_in, wall, 6),
        (snbr_in, snbr, 7),
        (sflu_in, sflu, 8),
    ]
    tables = [pltpu.make_async_copy(a, b, in_sem.at[i]) for a, b, i in tables]
    for c in tables:
        c.start()
    load(temp_in, T, in_sem.at[0])
    load(mat_in, M, in_sem.at[1])
    load(fluid_in, G, in_sem.at[2])
    load(heat_in, Q, in_sem.at[3])

    copies = {}
    steps = {}

    def send(i, src, dst, df, dc):
        copies[i] = pltpu.make_async_remote_copy(
            src_ref=src,
            dst_ref=dst,
            send_sem=send_sem.at[i],
            recv_sem=recv_sem.at[i],
            device_id=(fl + df, cr + dc),
            device_id_type=MESH,
        )
        steps[i] = (df, dc)

        @pl.when(near(df, dc))
        def _():
            copies[i].start()

    def received(i):
        @pl.when(near(-steps[i][0], -steps[i][1]))
        def _():
            copies[i].wait_recv()

    wide = (E, W)
    lw = lanes(wide)
    zw = jnp.bitwise_and(lw, E - 1)
    lh = lanes((E, H))
    zh = jnp.bitwise_and(lh, E - 1)
    group = jnp.right_shift(lh, 4)
    r8 = rows((8, W))
    l8 = lanes((8, W))
    z8 = jnp.bitwise_and(l8, E - 1)
    q8 = rows((8, H))
    g8 = jnp.right_shift(lanes((8, H)), 4)

    def base_of(df, dc):
        return (fl + df) * nc + (cr + dc)

    def slot(idv, base, n):
        return jnp.clip(idv - base * n, 0, n - 1)

    def num(flag):
        return jnp.where(flag, 1, 0)

    def on(flag, like):
        return jnp.full(like.shape, flag) > 0

    for c in tables:
        c.wait()

    here = base_of(0, 0)
    below0 = sflu[0, 5]
    below1 = sflu[1, 5]
    z0 = jnp.where(below0 >= 0, slot(below0, here, FB) + 1, 0)
    z1 = jnp.where(below1 >= 0, slot(below1, here, FB) + 2, z0 + 1)
    own_z = (z0, z1)
    flu_z = [b + num(b >= z0) + num(b + 1 >= z1) for b in range(FB)]

    def fluid_slot(za, zb, z):
        return jnp.clip(z - num(za < z) - num(zb < z), 0, FB - 1)

    nbr_z = []
    nbr_has = []
    for k in range(4):
        df, dc = C[k + 1][0], C[k + 1][1]
        first = base_of(df, dc) * SB
        za = zb = 0
        pairs = [(wall[b, k], flu_z[b]) for b in range(FB)]
        pairs += [(snbr[s, k], own_z[s]) for s in range(SB)]
        for idv, z in pairs:
            za = za + jnp.where(idv == first, z, 0)
            zb = zb + jnp.where(idv == first + 1, z, 0)
        has = num(near(df, dc))
        nbr_has.append(has)
        nbr_z.append((jnp.where(has > 0, za, NONE), jnp.where(has > 0, zb, NONE)))

    with jax.named_scope("wait_solid"):
        all_of(T, in_sem.at[0]).wait()
        all_of(M, in_sem.at[1]).wait()
    for s in range(SB):
        m = M[s]
        k = jnp.full(wide, cond[0], F32)
        for i in range(1, 8):
            k = jnp.where(m == i, cond[i], k)
        KAP[s] = k
        zf = jnp.full((8, W), own_z[s]).astype(F32)
        t = T[s]
        XS[0, FB + s] = jnp.where(r8 > 4, t[8:], jnp.where(r8 == 4, zf, rroll(k[8:], 4)))
        XS[1, FB + s] = jnp.where(r8 < 3, t[:8], jnp.where(r8 == 3, zf, rroll(k[:8], 4)))
        YS[0, FB + s] = jnp.where(lh >= 64, t[:, H:], lroll(k[:, H:], 64))
        YS[1, FB + s] = jnp.where(lh < 64, t[:, :H], lroll(k[:, :H], 64))

    def pack_y(pieces, side):
        acc = None
        for g, v in enumerate(pieces):
            r = lroll(v, E * g - (H - E)) if side == 0 else lroll(v, E * g)
            acc = r if acc is None else jnp.where(group == g, r, acc)
        return acc

    def ahead(v, p, z):
        _, cy, cz = C[p]
        if cz:
            edge = z == 0 if cz > 0 else z == E - 1
            return jnp.where(edge, lroll(v, -(E - 1) * cz), lroll(v, cz))
        return lroll(v, E * cy)

    def two(v, first, second, z):
        return jnp.where((z == 0) | (z == E - 1), v, jnp.where(z < 8, first, second))

    with jax.named_scope("wait_pops"):
        all_of(G, in_sem.at[2]).wait()
        all_of(Q, in_sem.at[3]).wait()
    for b in range(FB):
        with jax.named_scope("collide"):
            for xh in range(2):
                for yh in range(2):
                    collide_tile(G, Q, b, pl.ds(8 * xh, 8), pl.ds(H * yh, H))
        for side in range(2):
            x = E - 1 if side == 0 else 0
            inner = E - 2 if side == 0 else 1

            def line(x_at, lo, n):
                zz = jnp.bitwise_and(lanes((1, n)), E - 1)
                up = Q[b, 6, x_at : x_at + 1, lo : lo + n]
                return jnp.where(zz < 8, up, Q[b, 5, x_at : x_at + 1, lo : lo + n])

            for r in range(5):
                FX[side, b, r : r + 1, :] = G[b, PX[side][r], x : x + 1, :]
            FX[side, b, HEAT : HEAT + 1, :] = Q[b, 1 + side, x : x + 1, :]
            z1w = jnp.bitwise_and(lanes((1, W)), E - 1)
            v = line(inner, 0, W)
            FX[side, b, EDGE_Z : EDGE_Z + 1, :] = two(
                line(x, 0, W), lroll(v, 1), lroll(v, -1), z1w
            )
            FX[side, b, CROSS : CROSS + 1, :H] = Q[b, 4, x : x + 1, :H]
            FX[side, b, CROSS : CROSS + 1, H:] = Q[b, 3, x : x + 1, H:]

            raw = FX[side, b]
            out = raw
            for r, p in enumerate(PX[side]):
                if r:
                    out = jnp.where(r8 == r, ahead(raw, p, z8), out)
            XS[side, b] = out

            half = pl.ds(H, H) if side == 0 else pl.ds(0, H)
            sgn = 1 if side == 0 else -1
            hz = jnp.where(zh < 8, Q[b, 6, :, half], Q[b, 5, :, half])
            hx = jnp.concatenate([Q[b, 2, 0:8, half], Q[b, 1, 8:16, half]], axis=0)
            raw = pack_y(
                [G[b, PY[side][r], :, half] for r in range(5)]
                + [
                    Q[b, 3 + side, :, half],
                    two(hz, lroll(hz, sgn * E + 1), lroll(hz, sgn * E - 1), zh),
                    hx,
                ],
                side,
            )
            FY[side, b] = raw
            out = raw
            for q, p in enumerate(PY[side]):
                cx = C[p][0]
                if q:
                    v = rroll(raw, cx) if cx else ahead(raw, p, zh)
                    out = jnp.where(group == q, v, out)
            YS[side, b] = out
            for i in range(4):
                cs, row, ch = CORNER_SRC[i]
                if cs != side:
                    continue
                sg = -1 if ch else 1
                hp = 3 if ch else 4
                lo = H * ch
                gg = jnp.right_shift(lanes((1, H)), 4)
                at = (lambda d: 7 - d) if ch else (lambda d: d)
                acc = Q[b, 1 + side, x : x + 1, lo : lo + H]
                extra = [
                    (2, line(x, lo, H)),
                    (7, G[b, PX[side][row], x : x + 1, lo : lo + H]),
                    (4, Q[b, hp, x : x + 1, lo : lo + H]),
                    (5, Q[b, hp, inner : inner + 1, lo : lo + H]),
                ]
                for d, v in extra:
                    acc = jnp.where(gg == at(d), lroll(v, sg * E * d), acc)
                CS[i, 0, b : b + 1, :] = acc

    for i in range(4):
        side, _, ch = CORNER_SRC[i]
        for s in range(SB):
            CS[i, 1 + s] = XS[side, FB + s, :, H * ch : H * ch + H]

    with jax.named_scope("entry_barrier"):
        pl.semaphore_wait(barrier, n_peers)
    for i, (df, dc) in enumerate(CORNERS):
        send(4 + i, CS.at[i], CR.at[i], df, dc)
    for i, (df, dc) in enumerate(SIDES):
        side = i % 2
        if i < 2:
            send(i, XS.at[side], XR.at[side], df, dc)
        else:
            send(i, YS.at[side], YR.at[side], df, dc)

    def stream(b):
        def main(ref, p):
            cx, cy, cz = C[p]
            s = E * cy + cz
            out = lroll(rroll(ref[b, p], cx), s)
            if cz:
                back = ref[b, OPP[p]]
                adj = (b - cz) % FB
                if ref is Q:
                    wid = wall[b, (6 if cz > 0 else 5) - 1]
                    tw = lroll(T[slot(wid, here, SB)], -(E - 1) * cz)
                    back = jnp.where(jnp.full(wide, wid) >= 0, 2.0 * tw - back, back)
                if 0 <= b - cz < FB:
                    other = lroll(rroll(ref[adj, p], cx), E * cy - (E - 1) * cz)
                    zid = nbr[b, (6 if cz > 0 else 5) - 1]
                    back = jnp.where(jnp.full(wide, zid) >= 0, other, back)
                edge = zw == 0 if cz > 0 else zw == E - 1
                out = jnp.where(edge, back, out)
            return out

        GO[b, 0] = G[b, 0]
        QO[b, 0] = Q[b, 0]
        for p in range(1, 19):
            GO[b, p] = main(G, p)
        for p in range(1, 7):
            QO[b, p] = main(Q, p)

    with jax.named_scope("stream"):
        for b in range(FB):
            stream(b)

    ext = (EX, EL)
    ze = jnp.bitwise_and(lanes(ext), E - 1)

    def piece(flag, v):
        return jnp.where(on(flag, v), v, 0.0)

    with jax.named_scope("wait_faces"):
        for i in range(8):
            received(i)

    def corner_z(i):
        side = CORNER_SRC[i][0]
        r = 4 if side == 0 else 3
        return [
            jnp.broadcast_to(CR[i, 1 + s, r : r + 1, :], (8, H))
            for s in range(SB)
        ]

    quad = [[2, 3], [1, 0]]
    chas = [jnp.full((8, H), num(near(-df, -dc))) > 0 for df, dc in CORNERS]
    cz = [[jnp.where(chas[i], v, float(NONE)) for v in corner_z(i)] for i in range(4)]

    def quadrants(fn):
        up = jnp.where(g8 < 4, fn(quad[0][0]), fn(quad[0][1]))
        down = jnp.where(g8 < 4, fn(quad[1][0]), fn(quad[1][1]))
        return jnp.where(q8 < 4, up, down)

    def splat(shape, v):
        return jnp.full(shape, v).astype(F32)

    Z = []
    for s in range(SB):
        TE[s, 0:E, 0:W] = T[s]
        KE[s, 0:E, 0:W] = KAP[s]
        a = piece(nbr_has[0], XR[1, FB + s])
        c = piece(nbr_has[1], XR[0, FB + s])
        TE[s, E:EX, 0:W] = jnp.where(r8 < 4, a, c)
        KE[s, E:EX, 0:W] = rroll(jnp.where(r8 < 4, c, a), 4)
        zx = jnp.where(r8 < 4, splat((8, W), nbr_z[0][s]), splat((8, W), nbr_z[1][s]))
        a = piece(nbr_has[2], YR[1, FB + s])
        c = piece(nbr_has[3], YR[0, FB + s])
        TE[s, 0:E, W:EL] = jnp.where(group < 4, a, c)
        KE[s, 0:E, W:EL] = lroll(jnp.where(group < 4, c, a), 64)
        zy = jnp.where(group < 4, splat((E, H), nbr_z[2][s]), splat((E, H), nbr_z[3][s]))

        def corner_solid(i):
            return jnp.where(chas[i], CR[i, 1 + s], 0.0)

        TE[s, E:EX, W:EL] = quadrants(corner_solid)
        KE[s, E:EX, W:EL] = quadrants(lambda i: rroll(corner_solid(i), 4))
        top = jnp.concatenate([splat(wide, own_z[s]), zy], axis=1)
        low = jnp.concatenate([zx, quadrants(lambda i: cz[i][s])], axis=1)
        Z.append(jnp.concatenate([top, low], axis=0))

    def link(k, kb):
        return (2.0 * k * kb) / jnp.maximum(k + kb, 0.05)

    def toward(k, v):
        return rroll(v, -1 if k == 0 else 1) if k < 2 else lroll(v, -E if k == 2 else E)

    wet = [[0.0, 0.0] for _ in range(SB)]
    for k in range(4):
        za, zb = toward(k, Z[0]), toward(k, Z[1])
        for s in range(SB):
            code = jnp.where(zb == Z[s], 1, jnp.where(za == Z[s], 0, 2))
            CODE[k, s] = code
            wet[s][k // 2] = jnp.where((code == 2) & (za >= 0.0), 1.0, wet[s][k // 2])
    adj = Z[1] == Z[0] + 1.0
    top, bottom = ze == E - 1, ze == 0
    wet_z = [
        (top & (~adj) & (Z[0] < NZ - 1.0) & (Z[0] >= 0.0)) | (bottom & (Z[0] > 0.0)),
        (top & (Z[1] < NZ - 1.0) & (Z[1] >= 0.0)) | (bottom & (~adj) & (Z[1] >= 0.0)),
    ]
    for s in range(SB):
        WX[s] = wet[s][0]
        WY[s] = wet[s][1]
        WZ[s] = jnp.where(wet_z[s], 1.0, 0.0)

    def chosen(k, s, v):
        code = CODE[k, s]
        return jnp.where(code == 1, v[1], jnp.where(code == 0, v[0], 0.0))

    def z_up(v):
        return [jnp.where(top, lroll(v[1], E - 1), lroll(v[0], -1)), lroll(v[1], -1)]

    def divergence(v):
        div = []
        for k, links in ((0, LX), (2, LY)):
            over = [toward(k, x) for x in v]
            f = [
                links[s] * (jnp.where(CODE[k, s] == 1, over[1], over[0]) - v[s])
                for s in range(SB)
            ]
            under = [toward(k + 1, x) for x in f]
            part = [f[s] - chosen(k + 1, s, under) for s in range(SB)]
            div = part if k == 0 else [a + b for a, b in zip(div, part)]
        up = z_up(v)
        f = [LZ[s] * (up[s] - v[s]) for s in range(SB)]
        under = [
            jnp.where(bottom, 0.0, lroll(f[0], 1)),
            jnp.where(bottom, lroll(f[0], 1 - E), lroll(f[1], 1)),
        ]
        return [div[s] + (f[s] - under[s]) for s in range(SB)]

    kk = [KE[s] for s in range(SB)]
    for k, links in ((0, LX), (2, LY)):
        over = [toward(k, x) for x in kk]
        for s in range(SB):
            links[s] = link(kk[s], chosen(k, s, over))
    up = z_up(kk)
    LZ[0] = link(kk[0], jnp.where(top & ~adj, 0.0, up[0]))
    LZ[1] = link(kk[1], jnp.where(top, 0.0, up[1]))
    tt = [TE[s] for s in range(SB)]
    div = divergence(tt)
    for s in range(SB):
        R[s] = div[s] - (WX[s] + WY[s] + WZ[s]) * tt[s]

    kmax = cond[0]
    for i in range(1, 8):
        kmax = jnp.maximum(kmax, cond[i])
    radius = jnp.full((8, H), kmax * 6.0, F32)
    center = radius + 1.0
    sigma = center / radius

    def grow(v):
        v = jnp.concatenate([v] * (EX // 8), axis=0)
        return jnp.concatenate([v] * (EL // H), axis=1)

    inv_center = grow(1.0 / center)
    rho0 = 1.0 / sigma
    rho1 = 1.0 / (2.0 * sigma - rho0)
    rho2 = 1.0 / (2.0 * sigma - rho1)
    coef = [
        (grow(rho1 * rho0), grow(2.0 * rho1 / radius)),
        (grow(rho2 * rho1), grow(2.0 * rho2 / radius)),
    ]


    def corner_rows(i):
        return [jnp.broadcast_to(CR[i, 0, j : j + 1, :], (8, H)) for j in range(FB)]

    def corner_heat(i, z):
        f = z - jnp.where(cz[i][0] < z, 1.0, 0.0) - jnp.where(cz[i][1] < z, 1.0, 0.0)
        a, b, c = corner_rows(i)
        return jnp.where(f < 0.5, a, jnp.where(f < 1.5, b, c))

    def of_three(za, zb, z, fn):
        f = z - jnp.where(za < z, 1.0, 0.0) - jnp.where(zb < z, 1.0, 0.0)
        return jnp.where(f < 0.5, fn(0), jnp.where(f < 1.5, fn(1), fn(2)))

    row_edge = (q8 == 0) | (q8 == 7)
    wide_edge = (r8 == 0) | (r8 == 7)

    def stack(v):
        return jnp.concatenate([v, v], axis=0)

    for s in range(SB):
        oz = own_z[s]
        nz = [nbr_z[k][s] for k in range(4)]
        ozf = splat((8, H), oz)
        nzf = [splat((8, H), z) for z in nz]
        f_side = [fluid_slot(nbr_z[k][0], nbr_z[k][1], oz) for k in range(4)]
        f_own = [fluid_slot(z0, z1, nz[k]) for k in range(4)]

        own_lo = jnp.broadcast_to(XR[0, f_side[1], HEAT : HEAT + 1, :], (8, W))
        own_hi = jnp.broadcast_to(XR[1, f_side[0], HEAT : HEAT + 1, :], (8, W))
        x_tile = jnp.where(
            r8 < 4,
            jnp.broadcast_to(Q[f_own[0], 1, E - 1 : E, :], (8, W)),
            jnp.broadcast_to(Q[f_own[1], 2, 0:1, :], (8, W)),
        )
        y_lo = jnp.where(g8 < 4, corner_heat(1, nzf[2]), corner_heat(0, nzf[3]))
        y_hi = jnp.where(g8 < 4, corner_heat(2, nzf[2]), corner_heat(3, nzf[3]))

        def from_y(i):
            half = CORNER_SRC[i][2]
            k = 3 if half else 2
            row = 0 if i < 2 else E - 1
            v = of_three(
                nbr_z[k][0],
                nbr_z[k][1],
                cz[i][s],
                lambda j: jnp.broadcast_to(YR[1 - half, j, row : row + 1, :], (8, H))
                if not half
                else jnp.broadcast_to(YR[0, j, row : row + 1, :], (8, H)),
            )
            return v if half else lroll(v, E)

        heat = jnp.concatenate(
            [
                jnp.concatenate([own_lo, y_lo], axis=1),
                jnp.concatenate([own_hi, y_hi], axis=1),
                jnp.concatenate([x_tile, quadrants(from_y)], axis=1),
            ],
            axis=0,
        )
        acc = R[s] + jnp.where(WX[s] > 0.5, heat, 0.0)

        left = lroll(YR[0, f_side[3]], -5 * E)
        right = lroll(YR[1, f_side[2]], 2 * E)

        def from_corner(i, z):
            v = corner_heat(i, z)
            if CORNER_SRC[i][2]:
                return jnp.where(row_edge, lroll(v, -3 * E), lroll(v, -2 * E))
            return jnp.where(row_edge, lroll(v, 3 * E), lroll(v, 2 * E))

        x_left = jnp.where(q8 < 4, from_corner(3, nzf[0]), from_corner(0, nzf[1]))
        x_right = jnp.where(q8 < 4, from_corner(2, nzf[0]), from_corner(1, nzf[1]))
        y_tile = jnp.where(
            group < 4,
            lroll(Q[f_own[2], 3, :, H:W], E),
            lroll(Q[f_own[3], 4, :, 0:H], -E),
        )

        def from_x(i):
            half = CORNER_SRC[i][2]
            k = 1 if i < 2 else 0
            lo = 0 if half else H
            v = of_three(
                nbr_z[k][0],
                nbr_z[k][1],
                cz[i][s],
                lambda j: jnp.broadcast_to(
                    XR[1 - k, j, CROSS : CROSS + 1, lo : lo + H], (8, H)
                ),
            )
            return lroll(v, -E if half else E)

        heat = jnp.concatenate(
            [
                jnp.concatenate([left, right, y_tile], axis=1),
                jnp.concatenate([x_left, x_right, quadrants(from_x)], axis=1),
            ],
            axis=0,
        )
        acc = acc + jnp.where(WY[s] > 0.5, heat, 0.0)

        def updown(k):
            za, zb = nbr_z[k]
            return fluid_slot(za, zb, nz[k] + 1), fluid_slot(za, zb, nz[k] - 1)

        tile = jnp.where(
            zw < 8,
            lroll(Q[fluid_slot(z0, z1, oz - 1), 5], 1 - E),
            lroll(Q[fluid_slot(z0, z1, oz + 1), 6], E - 1),
        )
        a, c = [], []
        for k in range(2):
            u, d = updown(k)
            a.append(jnp.broadcast_to(XR[1 - k, u, EDGE_Z : EDGE_Z + 1, :], (8, W)))
            c.append(jnp.broadcast_to(XR[1 - k, d, EDGE_Z : EDGE_Z + 1, :], (8, W)))
        a = jnp.where(r8 < 4, a[0], a[1])
        c = jnp.where(r8 < 4, c[0], c[1])
        x_tile = jnp.where(
            z8 < 8,
            jnp.where(wide_edge, lroll(c, 1 - E), lroll(c, 2 - E)),
            jnp.where(wide_edge, lroll(a, E - 1), lroll(a, E - 2)),
        )
        u, d = updown(2)
        a, c = YR[1, u], YR[1, d]
        y_up = jnp.where(
            zh < 8,
            jnp.where(group == 0, lroll(c, -7 * E + 1), lroll(c, -6 * E + 2)),
            jnp.where(group == 0, lroll(a, -5 * E - 1), lroll(a, -4 * E - 2)),
        )
        u, d = updown(3)
        a, c = YR[0, u], YR[0, d]
        y_down = jnp.where(
            zh < 8,
            jnp.where(group == 7, lroll(c, 1), lroll(c, 2 - E)),
            jnp.where(group == 7, lroll(a, 2 * E - 1), lroll(a, E - 2)),
        )

        def from_z(i):
            shift = 2 * E if CORNER_SRC[i][2] else -2 * E
            a = lroll(corner_heat(i, cz[i][s] + 1.0), shift + E - 1)
            c = lroll(corner_heat(i, cz[i][s] - 1.0), shift + 1 - E)
            return jnp.where(z8[:, :H] < 8, c, a)

        heat = jnp.concatenate(
            [
                jnp.concatenate([tile, jnp.where(group < 4, y_up, y_down)], axis=1),
                jnp.concatenate([x_tile, quadrants(from_z)], axis=1),
            ],
            axis=0,
        )
        R[s] = acc + jnp.where(WZ[s] > 0.5, heat, 0.0)

    upd = []
    sol = []
    for s in range(SB):
        d = R[s] * inv_center
        upd.append(d)
        sol.append(T[s] + d[0:E, 0:W])
    div = divergence(upd)
    for s in range(SB):
        r = R[s] - (upd[s] - div[s])
        R[s] = r
        upd[s] = coef[0][0] * upd[s] + coef[0][1] * r
        sol[s] = sol[s] + upd[s][0:E, 0:W]

    v = [x[:, 0:W] for x in upd]
    over = [rroll(x, -1) for x in v]
    f = [
        LX[s, :, 0:W] * (jnp.where(CODE[0, s, :, 0:W] == 1, over[1], over[0]) - v[s])
        for s in range(SB)
    ]
    under = [rroll(x, 1)[0:E] for x in f]
    code = [CODE[1, s, 0:E, 0:W] for s in range(SB)]
    div = []
    for s in range(SB):
        u = jnp.where(code[s] == 1, under[1], jnp.where(code[s] == 0, under[0], 0.0))
        div.append(f[s][0:E] - u)
    v = [x[0:E] for x in upd]
    over = [lroll(x, -E) for x in v]
    f = [
        LY[s, 0:E] * (jnp.where(CODE[2, s, 0:E] == 1, over[1], over[0]) - v[s])
        for s in range(SB)
    ]
    under = [lroll(x, E)[:, 0:W] for x in f]
    code = [CODE[3, s, 0:E, 0:W] for s in range(SB)]
    for s in range(SB):
        u = jnp.where(code[s] == 1, under[1], jnp.where(code[s] == 0, under[0], 0.0))
        div[s] = div[s] + (f[s][:, 0:W] - u)
    v = [x[0:E, 0:W] for x in upd]
    last, first = zw == E - 1, zw == 0
    up = [jnp.where(last, lroll(v[1], E - 1), lroll(v[0], -1)), lroll(v[1], -1)]
    f = [LZ[s, 0:E, 0:W] * (up[s] - v[s]) for s in range(SB)]
    under = [
        jnp.where(first, 0.0, lroll(f[0], 1)),
        jnp.where(first, lroll(f[0], 1 - E), lroll(f[1], 1)),
    ]
    for s in range(SB):
        r = R[s, 0:E, 0:W] - (v[s] - div[s] - (f[s] - under[s]))
        TO[s] = sol[s] + (coef[1][0][0:E, 0:W] * v[s] + coef[1][1][0:E, 0:W] * r)

    def x_face(b, side):
        shape = (8, W)
        df = -1 if side == 0 else 1
        dirn = 2 if side == 0 else 1
        bf = base_of(df, 0)
        main_id = nbr[b, dirn - 1]
        a = XR[side, slot(main_id, bf, FB)]
        val = a
        ids = jnp.full(shape, main_id)
        for r, p in enumerate(PX[side]):
            _, cy, cz = C[p]
            if r == 0:
                continue
            cid = nbr[b, OPP[p] - 1]
            if cy:
                which = jnp.full((8, H), slot(cid, base_of(df, -cy), FB))
                first, second, third = corner_rows(CORNER_OF[p])
                corner = jnp.where(which == 1, second, first)
                corner = jnp.where(which == 2, third, corner)
                corner = jnp.concatenate([corner, corner], axis=1)
                edge = l8 < E if cy > 0 else l8 >= W - E
                cand = jnp.where(edge, corner, a)
            else:
                edge = z8 == 0 if cz > 0 else z8 == E - 1
                cand = jnp.where(edge, XR[side, slot(cid, bf, FB)], a)
            val = jnp.where(r8 == r, cand, val)
            ids = jnp.where((r8 == r) & edge, jnp.full(shape, cid), ids)
        fall = FX[1 - side, b]
        wid = wall[b, dirn - 1]
        row = 7 if side == 0 else 0
        tw = XR[side, FB + slot(wid, bf, SB), row : row + 1, :]
        hot = (r8 == HEAT) & (jnp.full(shape, wid) >= 0)
        fall = jnp.where(hot, 2.0 * tw - fall, fall)
        return jnp.where(ids >= 0, val, fall)

    def y_face(b, side):
        shape = (E, H)
        dc = -1 if side == 0 else 1
        dirn = 4 if side == 0 else 3
        bf = base_of(0, dc)
        main_id = nbr[b, dirn - 1]
        a = YR[side, slot(main_id, bf, FB)]
        val = a
        ids = jnp.full(shape, main_id)
        for r, p in enumerate(PY[side]):
            cx, _, cz = C[p]
            if r == 0:
                continue
            if cx:
                continue
            cid = nbr[b, OPP[p] - 1]
            edge = (group == r) & (zh == 0 if cz > 0 else zh == E - 1)
            val = jnp.where(edge, YR[side, slot(cid, bf, FB)], val)
            ids = jnp.where(edge, jnp.full(shape, cid), ids)
        fall = FY[1 - side, b]
        wid = wall[b, dirn - 1]
        tw = YR[side, FB + slot(wid, bf, SB)]
        tw = lroll(tw, -2 * E if side == 0 else HEAT * E)
        hot = (group == HEAT) & (jnp.full(shape, wid) >= 0)
        fall = jnp.where(hot, 2.0 * tw - fall, fall)
        return jnp.where(ids >= 0, val, fall)

    for b in range(FB):
        for side in range(2):
            yf = y_face(b, side)
            half = pl.ds(0, H) if side == 0 else pl.ds(H, H)
            edge = lh < E if side == 0 else lh >= H - E
            back = 0 if side == 0 else H - E
            for q, p in enumerate(PY[side]):
                v = lroll(yf, back - E * q)
                GO[b, p, :, half] = jnp.where(edge, v, GO[b, p, :, half])
            v = lroll(yf, back - E * HEAT)
            QO[b, 3 + side, :, half] = jnp.where(edge, v, QO[b, 3 + side, :, half])
        for side in range(2):
            xf = x_face(b, side)
            x = 0 if side == 0 else E - 1
            for r, p in enumerate(PX[side]):
                GO[b, p, x : x + 1, :] = xf[r : r + 1]
            QO[b, 1 + side, x : x + 1, :] = xf[HEAT : HEAT + 1]

    for i in range(N_COPY):

        @pl.when(near(*steps[i]))
        def _():
            copies[i].wait_send()


def store_kernel(fluid, heat, solid, fluid_out, heat_out, solid_out, sem):
    pairs = [(fluid, fluid_out), (heat, heat_out), (solid, solid_out)]
    for i, (src, dst) in enumerate(pairs):
        for x in range(E):
            pltpu.make_async_copy(
                src.at[..., x, :], dst.at[..., pl.ds(W * x, W)], sem.at[i]
            ).start()
    for i, (src, dst) in enumerate(pairs):
        pltpu.make_async_copy(src, src, sem.at[i]).wait()


def body(nf, nc, fluid_pop, heat_pop, solid_temp, material, cond, nbr, wall, snbr, sflu):
    hbm = pl.BlockSpec(memory_space=pltpu.HBM)

    def vm(*shape):
        return pltpu.VMEM(shape, F32)

    vmem = pl.BlockSpec(memory_space=pltpu.VMEM)
    fields = pl.pallas_call(
        functools.partial(kernel, nf, nc),
        out_shape=(
            vm(FB, 19, E, W),
            vm(FB, 7, E, W),
            vm(SB, E, W),
        ),
        in_specs=[hbm] * 9,
        out_specs=(vmem, vmem, vmem),
        scratch_shapes=[
            vm(FB, 19, E, W),
            vm(FB, 7, E, W),
            vm(SB, E, W),
            pltpu.VMEM((SB, E, W), jnp.int32),
            vm(SB, E, W),
            vm(2, FB, 8, W),
            vm(2, FB, E, H),
            vm(2, FB + SB, 8, W),
            vm(2, FB + SB, 8, W),
            vm(2, FB + SB, E, H),
            vm(2, FB + SB, E, H),
            vm(4, 1 + SB, 8, H),
            vm(4, 1 + SB, 8, H),
        ]
        + [vm(SB, EX, EL)] * 9
        + [
            pltpu.VMEM((4, SB, EX, EL), jnp.int32),
            pltpu.SMEM(cond.shape, F32),
            pltpu.SMEM(nbr.shape, jnp.int32),
            pltpu.SMEM(wall.shape, jnp.int32),
            pltpu.SMEM(snbr.shape, jnp.int32),
            pltpu.SMEM(sflu.shape, jnp.int32),
            pltpu.SemaphoreType.DMA((9,)),
            pltpu.SemaphoreType.DMA((N_COPY,)),
            pltpu.SemaphoreType.DMA((N_COPY,)),
        ],
        compiler_params=pltpu.CompilerParams(
            collective_id=0, has_side_effects=True, vmem_limit_bytes=LIMIT
        ),
    )(fluid_pop, heat_pop, solid_temp, material, cond, nbr, wall, snbr, sflu)
    return pl.pallas_call(
        store_kernel,
        out_shape=(
            jax.ShapeDtypeStruct(fluid_pop.shape, F32),
            jax.ShapeDtypeStruct(heat_pop.shape, F32),
            jax.ShapeDtypeStruct(solid_temp.shape, F32),
        ),
        in_specs=[pl.BlockSpec(memory_space=pl.ANY)] * 3,
        out_specs=(hbm, hbm, hbm),
        scratch_shapes=[pltpu.SemaphoreType.DMA((3,))],
        compiler_params=pltpu.CompilerParams(vmem_limit_bytes=8 * 1024 * 1024),
    )(*fields)


def solution(mesh):
    both = ("flow", "cross")
    in_specs = (
        P(both, None, None),
        P(both, None, None),
        P(both, None),
        P(both, None),
        P(),
        P(both, None),
        P(both, None),
        P(both, None),
        P(both, None),
    )
    out_specs = (P(both, None, None), P(both, None, None), P(both, None))
    return jax.shard_map(
        functools.partial(body, mesh.shape["flow"], mesh.shape["cross"]),
        mesh=mesh,
        in_specs=in_specs,
        out_specs=out_specs,
        check_vma=False,
    )
```

```python
import functools

import jax
import jax.numpy as jnp
from jax import lax
from jax.experimental import pallas as pl
from jax.experimental.pallas import tpu as pltpu
from jax.sharding import PartitionSpec as P

MESH = pl.DeviceIdType.MESH
F32 = jnp.float32
E = 16
W = 256
H = 128
FB = 3
SB = 2
C = [
    (0, 0, 0),
    (1, 0, 0),
    (-1, 0, 0),
    (0, 1, 0),
    (0, -1, 0),
    (0, 0, 1),
    (0, 0, -1),
    (1, 1, 0),
    (-1, -1, 0),
    (1, -1, 0),
    (-1, 1, 0),
    (1, 0, 1),
    (-1, 0, -1),
    (1, 0, -1),
    (-1, 0, 1),
    (0, 1, 1),
    (0, -1, -1),
    (0, 1, -1),
    (0, -1, 1),
]
OPP = [0, 2, 1, 4, 3, 6, 5, 8, 7, 10, 9, 12, 11, 14, 13, 16, 15, 18, 17]
PX = ([1, 7, 9, 11, 13], [2, 8, 10, 12, 14])
PY = ([3, 7, 10, 15, 17], [4, 8, 9, 16, 18])
HEAT = 5
SIDES = [(1, 0), (-1, 0), (0, 1), (0, -1)]
CORNERS = [(1, 1), (1, -1), (-1, -1), (-1, 1)]
PEERS = CORNERS + SIDES
CORNER_SRC = [(0, 1, 1), (0, 2, 0), (1, 1, 0), (1, 2, 1)]
CORNER_OF = {7: 0, 9: 1, 8: 2, 10: 3}
EDGE_Z = 6
CROSS = 7
N_COPY = 8
NZ = 5
NONE = -9
EX = 24
EL = 384
LIMIT = 60 * 1024 * 1024


def lroll(v, s):
    n = v.shape[1]
    s = s % n
    return v if s == 0 else pltpu.roll(v, s, axis=1)


def rroll(v, s):
    n = v.shape[0]
    s = s % n
    return v if s == 0 else pltpu.roll(v, s, axis=0)


def lanes(shape):
    return lax.broadcasted_iota(jnp.int32, shape, 1)


def rows(shape):
    return lax.broadcasted_iota(jnp.int32, shape, 0)


def collide_tile(G, Q, b, rs, ls):
    def ld(p):
        return G[b, p, rs, ls]

    f = [ld(p) for p in range(19)]
    d = [None] * 19
    for p in (1, 3, 5, 7, 9, 11, 13, 15, 17):
        d[p] = f[p] - f[p + 1]
    s1 = ((f[1] + f[2]) + (f[3] + f[4])) + (f[5] + f[6])
    s2 = (((f[7] + f[8]) + (f[9] + f[10])) + ((f[11] + f[12]) + (f[13] + f[14]))) + (
        (f[15] + f[16]) + (f[17] + f[18])
    )
    rho = f[0] * (1.0 / 3.0) + s1 * (1.0 / 18.0) + s2 * (1.0 / 36.0)
    jx = d[1] * (1.0 / 18.0) + ((d[7] + d[9]) + (d[11] + d[13])) * (1.0 / 36.0)
    jy = d[3] * (1.0 / 18.0) + ((d[7] - d[9]) + (d[15] + d[17])) * (1.0 / 36.0)
    jz = d[5] * (1.0 / 18.0) + ((d[11] - d[13]) + (d[15] - d[17])) * (1.0 / 36.0)
    inv = 1.0 / rho
    u = (jx * inv, jy * inv, jz * inv)
    j = (jx, jy, jz)
    base = 1.25 * rho - 1.875 * (jx * u[0] + jy * u[1] + jz * u[2])
    G[b, 0, rs, ls] = base - 0.25 * f[0]
    cus = {}
    for p in (1, 3, 5, 7, 9, 11, 13, 15, 17):
        cj = None
        cu = None
        for a in range(3):
            s = C[p][a]
            if s == 0:
                continue
            if cj is None:
                cj, cu = j[a], u[a]
            elif s > 0:
                cj, cu = cj + j[a], cu + u[a]
            else:
                cj, cu = cj - j[a], cu - u[a]
        even = base + 5.625 * (cj * cu)
        odd = 3.75 * cj
        G[b, p, rs, ls] = (even + odd) - 0.25 * f[p]
        G[b, p + 1, rs, ls] = (even - odd) - 0.25 * f[p + 1]
        cus[p] = cu
    h = [Q[b, k, rs, ls] for k in range(7)]
    hs = ((h[1] + h[2]) + (h[3] + h[4])) + (h[5] + h[6])
    t11 = (h[0] * 0.25 + hs * 0.125) * 1.1
    t44 = 4.0 * t11
    Q[b, 0, rs, ls] = t11 - 0.1 * h[0]
    for k in (1, 3, 5):
        o = t44 * cus[k]
        Q[b, k, rs, ls] = (t11 + o) - 0.1 * h[k]
        Q[b, k + 1, rs, ls] = (t11 - o) - 0.1 * h[k + 1]


def kernel(
    nf,
    nc,
    fluid_in,
    heat_in,
    temp_in,
    mat_in,
    cond_in,
    nbr_in,
    wall_in,
    snbr_in,
    sflu_in,
    GO,
    QO,
    TO,
    G,
    Q,
    T,
    M,
    KAP,
    FX,
    FY,
    XS,
    XR,
    YS,
    YR,
    CS,
    CR,
    TE,
    KE,
    WX,
    WY,
    WZ,
    LX,
    LY,
    LZ,
    R,
    CODE,
    cond,
    nbr,
    wall,
    snbr,
    sflu,
    in_sem,
    send_sem,
    recv_sem,
):
    fl = lax.axis_index("flow")
    cr = lax.axis_index("cross")
    inside = {-1: (fl > 0, cr > 0), 0: (True, True), 1: (fl < nf - 1, cr < nc - 1)}

    def near(df, dc):
        a, b = inside[df][0], inside[dc][1]
        if df == 0:
            return b
        return a if dc == 0 else jnp.logical_and(a, b)

    barrier = pltpu.get_barrier_semaphore()
    for df, dc in PEERS:

        @pl.when(near(df, dc))
        def _():
            pl.semaphore_signal(
                barrier, inc=1, device_id=(fl + df, cr + dc), device_id_type=MESH
            )

    nx = 2 - (fl == 0).astype(jnp.int32) - (fl == nf - 1).astype(jnp.int32)
    ny = 2 - (cr == 0).astype(jnp.int32) - (cr == nc - 1).astype(jnp.int32)
    n_peers = nx + ny + nx * ny

    def load(src, dst, sem):
        for x in range(E):
            pltpu.make_async_copy(
                src.at[..., pl.ds(W * x, W)], dst.at[..., x, :], sem
            ).start()

    def all_of(ref, sem):
        return pltpu.make_async_copy(ref, ref, sem)

    tables = [
        (cond_in, cond, 4),
        (nbr_in, nbr, 5),
        (wall_in, wall, 6),
        (snbr_in, snbr, 7),
        (sflu_in, sflu, 8),
    ]
    tables = [pltpu.make_async_copy(a, b, in_sem.at[i]) for a, b, i in tables]
    for c in tables:
        c.start()
    load(temp_in, T, in_sem.at[0])
    load(mat_in, M, in_sem.at[1])
    load(fluid_in, G, in_sem.at[2])
    load(heat_in, Q, in_sem.at[3])

    copies = {}
    steps = {}

    def send(i, src, dst, df, dc):
        copies[i] = pltpu.make_async_remote_copy(
            src_ref=src,
            dst_ref=dst,
            send_sem=send_sem.at[i],
            recv_sem=recv_sem.at[i],
            device_id=(fl + df, cr + dc),
            device_id_type=MESH,
        )
        steps[i] = (df, dc)

        @pl.when(near(df, dc))
        def _():
            copies[i].start()

    def received(i):
        @pl.when(near(-steps[i][0], -steps[i][1]))
        def _():
            copies[i].wait_recv()

    wide = (E, W)
    lw = lanes(wide)
    zw = jnp.bitwise_and(lw, E - 1)
    lh = lanes((E, H))
    zh = jnp.bitwise_and(lh, E - 1)
    group = jnp.right_shift(lh, 4)
    r8 = rows((8, W))
    l8 = lanes((8, W))
    z8 = jnp.bitwise_and(l8, E - 1)
    q8 = rows((8, H))
    g8 = jnp.right_shift(lanes((8, H)), 4)

    def base_of(df, dc):
        return (fl + df) * nc + (cr + dc)

    def slot(idv, base, n):
        return jnp.clip(idv - base * n, 0, n - 1)

    def num(flag):
        return jnp.where(flag, 1, 0)

    def on(flag, like):
        return jnp.full(like.shape, flag) > 0

    for c in tables:
        c.wait()

    here = base_of(0, 0)
    below0 = sflu[0, 5]
    below1 = sflu[1, 5]
    z0 = jnp.where(below0 >= 0, slot(below0, here, FB) + 1, 0)
    z1 = jnp.where(below1 >= 0, slot(below1, here, FB) + 2, z0 + 1)
    own_z = (z0, z1)
    flu_z = [b + num(b >= z0) + num(b + 1 >= z1) for b in range(FB)]

    def fluid_slot(za, zb, z):
        return jnp.clip(z - num(za < z) - num(zb < z), 0, FB - 1)

    nbr_z = []
    nbr_has = []
    for k in range(4):
        df, dc = C[k + 1][0], C[k + 1][1]
        first = base_of(df, dc) * SB
        za = zb = 0
        pairs = [(wall[b, k], flu_z[b]) for b in range(FB)]
        pairs += [(snbr[s, k], own_z[s]) for s in range(SB)]
        for idv, z in pairs:
            za = za + jnp.where(idv == first, z, 0)
            zb = zb + jnp.where(idv == first + 1, z, 0)
        has = num(near(df, dc))
        nbr_has.append(has)
        nbr_z.append((jnp.where(has > 0, za, NONE), jnp.where(has > 0, zb, NONE)))

    with jax.named_scope("wait_solid"):
        all_of(T, in_sem.at[0]).wait()
        all_of(M, in_sem.at[1]).wait()
    for s in range(SB):
        m = M[s]
        k = jnp.full(wide, cond[0], F32)
        for i in range(1, 8):
            k = jnp.where(m == i, cond[i], k)
        KAP[s] = k
        zf = jnp.full((8, W), own_z[s]).astype(F32)
        t = T[s]
        XS[0, FB + s] = jnp.where(r8 > 4, t[8:], jnp.where(r8 == 4, zf, rroll(k[8:], 4)))
        XS[1, FB + s] = jnp.where(r8 < 3, t[:8], jnp.where(r8 == 3, zf, rroll(k[:8], 4)))
        YS[0, FB + s] = jnp.where(lh >= 64, t[:, H:], lroll(k[:, H:], 64))
        YS[1, FB + s] = jnp.where(lh < 64, t[:, :H], lroll(k[:, :H], 64))

    def pack_y(pieces, side):
        acc = None
        for g, v in enumerate(pieces):
            r = lroll(v, E * g - (H - E)) if side == 0 else lroll(v, E * g)
            acc = r if acc is None else jnp.where(group == g, r, acc)
        return acc

    def ahead(v, p, z):
        _, cy, cz = C[p]
        if cz:
            edge = z == 0 if cz > 0 else z == E - 1
            return jnp.where(edge, lroll(v, -(E - 1) * cz), lroll(v, cz))
        return lroll(v, E * cy)

    def two(v, first, second, z):
        return jnp.where((z == 0) | (z == E - 1), v, jnp.where(z < 8, first, second))

    with jax.named_scope("wait_pops"):
        all_of(G, in_sem.at[2]).wait()
        all_of(Q, in_sem.at[3]).wait()
    for b in range(FB):
        with jax.named_scope("collide"):
            for xh in range(2):
                for yh in range(2):
                    collide_tile(G, Q, b, pl.ds(8 * xh, 8), pl.ds(H * yh, H))
        for side in range(2):
            x = E - 1 if side == 0 else 0
            inner = E - 2 if side == 0 else 1

            def line(x_at, lo, n):
                zz = jnp.bitwise_and(lanes((1, n)), E - 1)
                up = Q[b, 6, x_at : x_at + 1, lo : lo + n]
                return jnp.where(zz < 8, up, Q[b, 5, x_at : x_at + 1, lo : lo + n])

            for r in range(5):
                FX[side, b, r : r + 1, :] = G[b, PX[side][r], x : x + 1, :]
            FX[side, b, HEAT : HEAT + 1, :] = Q[b, 1 + side, x : x + 1, :]
            z1w = jnp.bitwise_and(lanes((1, W)), E - 1)
            v = line(inner, 0, W)
            FX[side, b, EDGE_Z : EDGE_Z + 1, :] = two(
                line(x, 0, W), lroll(v, 1), lroll(v, -1), z1w
            )
            FX[side, b, CROSS : CROSS + 1, :H] = Q[b, 4, x : x + 1, :H]
            FX[side, b, CROSS : CROSS + 1, H:] = Q[b, 3, x : x + 1, H:]

            raw = FX[side, b]
            out = raw
            for r, p in enumerate(PX[side]):
                if r:
                    out = jnp.where(r8 == r, ahead(raw, p, z8), out)
            XS[side, b] = out

            half = pl.ds(H, H) if side == 0 else pl.ds(0, H)
            sgn = 1 if side == 0 else -1
            hz = jnp.where(zh < 8, Q[b, 6, :, half], Q[b, 5, :, half])
            hx = jnp.concatenate([Q[b, 2, 0:8, half], Q[b, 1, 8:16, half]], axis=0)
            raw = pack_y(
                [G[b, PY[side][r], :, half] for r in range(5)]
                + [
                    Q[b, 3 + side, :, half],
                    two(hz, lroll(hz, sgn * E + 1), lroll(hz, sgn * E - 1), zh),
                    hx,
                ],
                side,
            )
            FY[side, b] = raw
            out = raw
            for q, p in enumerate(PY[side]):
                cx = C[p][0]
                if q:
                    v = rroll(raw, cx) if cx else ahead(raw, p, zh)
                    out = jnp.where(group == q, v, out)
            YS[side, b] = out
            for i in range(4):
                cs, row, ch = CORNER_SRC[i]
                if cs != side:
                    continue
                sg = -1 if ch else 1
                hp = 3 if ch else 4
                lo = H * ch
                gg = jnp.right_shift(lanes((1, H)), 4)
                at = (lambda d: 7 - d) if ch else (lambda d: d)
                acc = Q[b, 1 + side, x : x + 1, lo : lo + H]
                extra = [
                    (2, line(x, lo, H)),
                    (7, G[b, PX[side][row], x : x + 1, lo : lo + H]),
                    (4, Q[b, hp, x : x + 1, lo : lo + H]),
                    (5, Q[b, hp, inner : inner + 1, lo : lo + H]),
                ]
                for d, v in extra:
                    acc = jnp.where(gg == at(d), lroll(v, sg * E * d), acc)
                CS[i, 0, b : b + 1, :] = acc

    for i in range(4):
        side, _, ch = CORNER_SRC[i]
        for s in range(SB):
            CS[i, 1 + s] = XS[side, FB + s, :, H * ch : H * ch + H]

    with jax.named_scope("entry_barrier"):
        pl.semaphore_wait(barrier, n_peers)
    for i, (df, dc) in enumerate(CORNERS):
        send(4 + i, CS.at[i], CR.at[i], df, dc)
    for i, (df, dc) in enumerate(SIDES):
        side = i % 2
        if i < 2:
            send(i, XS.at[side], XR.at[side], df, dc)
        else:
            send(i, YS.at[side], YR.at[side], df, dc)

    def stream(b):
        def main(ref, p):
            cx, cy, cz = C[p]
            s = E * cy + cz
            out = lroll(rroll(ref[b, p], cx), s)
            if cz:
                back = ref[b, OPP[p]]
                adj = (b - cz) % FB
                if ref is Q:
                    wid = wall[b, (6 if cz > 0 else 5) - 1]
                    tw = lroll(T[slot(wid, here, SB)], -(E - 1) * cz)
                    back = jnp.where(jnp.full(wide, wid) >= 0, 2.0 * tw - back, back)
                if 0 <= b - cz < FB:
                    other = lroll(rroll(ref[adj, p], cx), E * cy - (E - 1) * cz)
                    zid = nbr[b, (6 if cz > 0 else 5) - 1]
                    back = jnp.where(jnp.full(wide, zid) >= 0, other, back)
                edge = zw == 0 if cz > 0 else zw == E - 1
                out = jnp.where(edge, back, out)
            return out

        GO[b, 0] = G[b, 0]
        QO[b, 0] = Q[b, 0]
        for p in range(1, 19):
            GO[b, p] = main(G, p)
        for p in range(1, 7):
            QO[b, p] = main(Q, p)

    with jax.named_scope("stream"):
        for b in range(FB):
            stream(b)

    ext = (EX, EL)
    ze = jnp.bitwise_and(lanes(ext), E - 1)

    def piece(flag, v):
        return jnp.where(on(flag, v), v, 0.0)

    with jax.named_scope("wait_y"):
        for i in (2, 3):
            received(i)

    def y_face(b, side):
        shape = (E, H)
        dc = -1 if side == 0 else 1
        dirn = 4 if side == 0 else 3
        bf = base_of(0, dc)
        main_id = nbr[b, dirn - 1]
        a = YR[side, slot(main_id, bf, FB)]
        val = a
        ids = jnp.full(shape, main_id)
        for r, p in enumerate(PY[side]):
            cx, _, cz = C[p]
            if r == 0:
                continue
            if cx:
                continue
            cid = nbr[b, OPP[p] - 1]
            edge = (group == r) & (zh == 0 if cz > 0 else zh == E - 1)
            val = jnp.where(edge, YR[side, slot(cid, bf, FB)], val)
            ids = jnp.where(edge, jnp.full(shape, cid), ids)
        fall = FY[1 - side, b]
        wid = wall[b, dirn - 1]
        tw = YR[side, FB + slot(wid, bf, SB)]
        tw = lroll(tw, -2 * E if side == 0 else HEAT * E)
        hot = (group == HEAT) & (jnp.full(shape, wid) >= 0)
        fall = jnp.where(hot, 2.0 * tw - fall, fall)
        return jnp.where(ids >= 0, val, fall)

    for b in range(FB):
        for side in range(2):
            yf = y_face(b, side)
            half = pl.ds(0, H) if side == 0 else pl.ds(H, H)
            edge = lh < E if side == 0 else lh >= H - E
            back = 0 if side == 0 else H - E
            for q, p in enumerate(PY[side]):
                v = lroll(yf, back - E * q)
                GO[b, p, :, half] = jnp.where(edge, v, GO[b, p, :, half])
            v = lroll(yf, back - E * HEAT)
            QO[b, 3 + side, :, half] = jnp.where(edge, v, QO[b, 3 + side, :, half])
    with jax.named_scope("wait_x"):
        for i in (0, 1, 4, 5, 6, 7):
            received(i)

    def corner_z(i):
        side = CORNER_SRC[i][0]
        r = 4 if side == 0 else 3
        return [
            jnp.broadcast_to(CR[i, 1 + s, r : r + 1, :], (8, H))
            for s in range(SB)
        ]

    quad = [[2, 3], [1, 0]]
    chas = [jnp.full((8, H), num(near(-df, -dc))) > 0 for df, dc in CORNERS]
    cz = [[jnp.where(chas[i], v, float(NONE)) for v in corner_z(i)] for i in range(4)]

    def quadrants(fn):
        up = jnp.where(g8 < 4, fn(quad[0][0]), fn(quad[0][1]))
        down = jnp.where(g8 < 4, fn(quad[1][0]), fn(quad[1][1]))
        return jnp.where(q8 < 4, up, down)

    def splat(shape, v):
        return jnp.full(shape, v).astype(F32)

    Z = []
    for s in range(SB):
        TE[s, 0:E, 0:W] = T[s]
        KE[s, 0:E, 0:W] = KAP[s]
        a = piece(nbr_has[0], XR[1, FB + s])
        c = piece(nbr_has[1], XR[0, FB + s])
        TE[s, E:EX, 0:W] = jnp.where(r8 < 4, a, c)
        KE[s, E:EX, 0:W] = rroll(jnp.where(r8 < 4, c, a), 4)
        zx = jnp.where(r8 < 4, splat((8, W), nbr_z[0][s]), splat((8, W), nbr_z[1][s]))
        a = piece(nbr_has[2], YR[1, FB + s])
        c = piece(nbr_has[3], YR[0, FB + s])
        TE[s, 0:E, W:EL] = jnp.where(group < 4, a, c)
        KE[s, 0:E, W:EL] = lroll(jnp.where(group < 4, c, a), 64)
        zy = jnp.where(group < 4, splat((E, H), nbr_z[2][s]), splat((E, H), nbr_z[3][s]))

        def corner_solid(i):
            return jnp.where(chas[i], CR[i, 1 + s], 0.0)

        TE[s, E:EX, W:EL] = quadrants(corner_solid)
        KE[s, E:EX, W:EL] = quadrants(lambda i: rroll(corner_solid(i), 4))
        top = jnp.concatenate([splat(wide, own_z[s]), zy], axis=1)
        low = jnp.concatenate([zx, quadrants(lambda i: cz[i][s])], axis=1)
        Z.append(jnp.concatenate([top, low], axis=0))

    def link(k, kb):
        return (2.0 * k * kb) / jnp.maximum(k + kb, 0.05)

    def toward(k, v):
        return rroll(v, -1 if k == 0 else 1) if k < 2 else lroll(v, -E if k == 2 else E)

    wet = [[0.0, 0.0] for _ in range(SB)]
    for k in range(4):
        za, zb = toward(k, Z[0]), toward(k, Z[1])
        for s in range(SB):
            code = jnp.where(zb == Z[s], 1, jnp.where(za == Z[s], 0, 2))
            CODE[k, s] = code
            wet[s][k // 2] = jnp.where((code == 2) & (za >= 0.0), 1.0, wet[s][k // 2])
    adj = Z[1] == Z[0] + 1.0
    top, bottom = ze == E - 1, ze == 0
    wet_z = [
        (top & (~adj) & (Z[0] < NZ - 1.0) & (Z[0] >= 0.0)) | (bottom & (Z[0] > 0.0)),
        (top & (Z[1] < NZ - 1.0) & (Z[1] >= 0.0)) | (bottom & (~adj) & (Z[1] >= 0.0)),
    ]
    for s in range(SB):
        WX[s] = wet[s][0]
        WY[s] = wet[s][1]
        WZ[s] = jnp.where(wet_z[s], 1.0, 0.0)

    def chosen(k, s, v):
        code = CODE[k, s]
        return jnp.where(code == 1, v[1], jnp.where(code == 0, v[0], 0.0))

    def z_up(v):
        return [jnp.where(top, lroll(v[1], E - 1), lroll(v[0], -1)), lroll(v[1], -1)]

    def divergence(v):
        div = []
        for k, links in ((0, LX), (2, LY)):
            over = [toward(k, x) for x in v]
            f = [
                links[s] * (jnp.where(CODE[k, s] == 1, over[1], over[0]) - v[s])
                for s in range(SB)
            ]
            under = [toward(k + 1, x) for x in f]
            part = [f[s] - chosen(k + 1, s, under) for s in range(SB)]
            div = part if k == 0 else [a + b for a, b in zip(div, part)]
        up = z_up(v)
        f = [LZ[s] * (up[s] - v[s]) for s in range(SB)]
        under = [
            jnp.where(bottom, 0.0, lroll(f[0], 1)),
            jnp.where(bottom, lroll(f[0], 1 - E), lroll(f[1], 1)),
        ]
        return [div[s] + (f[s] - under[s]) for s in range(SB)]

    kk = [KE[s] for s in range(SB)]
    for k, links in ((0, LX), (2, LY)):
        over = [toward(k, x) for x in kk]
        for s in range(SB):
            links[s] = link(kk[s], chosen(k, s, over))
    up = z_up(kk)
    LZ[0] = link(kk[0], jnp.where(top & ~adj, 0.0, up[0]))
    LZ[1] = link(kk[1], jnp.where(top, 0.0, up[1]))
    tt = [TE[s] for s in range(SB)]
    div = divergence(tt)
    for s in range(SB):
        R[s] = div[s] - (WX[s] + WY[s] + WZ[s]) * tt[s]

    kmax = cond[0]
    for i in range(1, 8):
        kmax = jnp.maximum(kmax, cond[i])
    radius = jnp.full((8, H), kmax * 6.0, F32)
    center = radius + 1.0
    sigma = center / radius

    def grow(v):
        v = jnp.concatenate([v] * (EX // 8), axis=0)
        return jnp.concatenate([v] * (EL // H), axis=1)

    inv_center = grow(1.0 / center)
    rho0 = 1.0 / sigma
    rho1 = 1.0 / (2.0 * sigma - rho0)
    rho2 = 1.0 / (2.0 * sigma - rho1)
    coef = [
        (grow(rho1 * rho0), grow(2.0 * rho1 / radius)),
        (grow(rho2 * rho1), grow(2.0 * rho2 / radius)),
    ]


    def corner_rows(i):
        return [jnp.broadcast_to(CR[i, 0, j : j + 1, :], (8, H)) for j in range(FB)]

    def corner_heat(i, z):
        f = z - jnp.where(cz[i][0] < z, 1.0, 0.0) - jnp.where(cz[i][1] < z, 1.0, 0.0)
        a, b, c = corner_rows(i)
        return jnp.where(f < 0.5, a, jnp.where(f < 1.5, b, c))

    def of_three(za, zb, z, fn):
        f = z - jnp.where(za < z, 1.0, 0.0) - jnp.where(zb < z, 1.0, 0.0)
        return jnp.where(f < 0.5, fn(0), jnp.where(f < 1.5, fn(1), fn(2)))

    row_edge = (q8 == 0) | (q8 == 7)
    wide_edge = (r8 == 0) | (r8 == 7)

    def stack(v):
        return jnp.concatenate([v, v], axis=0)

    for s in range(SB):
        oz = own_z[s]
        nz = [nbr_z[k][s] for k in range(4)]
        ozf = splat((8, H), oz)
        nzf = [splat((8, H), z) for z in nz]
        f_side = [fluid_slot(nbr_z[k][0], nbr_z[k][1], oz) for k in range(4)]
        f_own = [fluid_slot(z0, z1, nz[k]) for k in range(4)]

        own_lo = jnp.broadcast_to(XR[0, f_side[1], HEAT : HEAT + 1, :], (8, W))
        own_hi = jnp.broadcast_to(XR[1, f_side[0], HEAT : HEAT + 1, :], (8, W))
        x_tile = jnp.where(
            r8 < 4,
            jnp.broadcast_to(Q[f_own[0], 1, E - 1 : E, :], (8, W)),
            jnp.broadcast_to(Q[f_own[1], 2, 0:1, :], (8, W)),
        )
        y_lo = jnp.where(g8 < 4, corner_heat(1, nzf[2]), corner_heat(0, nzf[3]))
        y_hi = jnp.where(g8 < 4, corner_heat(2, nzf[2]), corner_heat(3, nzf[3]))

        def from_y(i):
            half = CORNER_SRC[i][2]
            k = 3 if half else 2
            row = 0 if i < 2 else E - 1
            v = of_three(
                nbr_z[k][0],
                nbr_z[k][1],
                cz[i][s],
                lambda j: jnp.broadcast_to(YR[1 - half, j, row : row + 1, :], (8, H))
                if not half
                else jnp.broadcast_to(YR[0, j, row : row + 1, :], (8, H)),
            )
            return v if half else lroll(v, E)

        heat = jnp.concatenate(
            [
                jnp.concatenate([own_lo, y_lo], axis=1),
                jnp.concatenate([own_hi, y_hi], axis=1),
                jnp.concatenate([x_tile, quadrants(from_y)], axis=1),
            ],
            axis=0,
        )
        acc = R[s] + jnp.where(WX[s] > 0.5, heat, 0.0)

        left = lroll(YR[0, f_side[3]], -5 * E)
        right = lroll(YR[1, f_side[2]], 2 * E)

        def from_corner(i, z):
            v = corner_heat(i, z)
            if CORNER_SRC[i][2]:
                return jnp.where(row_edge, lroll(v, -3 * E), lroll(v, -2 * E))
            return jnp.where(row_edge, lroll(v, 3 * E), lroll(v, 2 * E))

        x_left = jnp.where(q8 < 4, from_corner(3, nzf[0]), from_corner(0, nzf[1]))
        x_right = jnp.where(q8 < 4, from_corner(2, nzf[0]), from_corner(1, nzf[1]))
        y_tile = jnp.where(
            group < 4,
            lroll(Q[f_own[2], 3, :, H:W], E),
            lroll(Q[f_own[3], 4, :, 0:H], -E),
        )

        def from_x(i):
            half = CORNER_SRC[i][2]
            k = 1 if i < 2 else 0
            lo = 0 if half else H
            v = of_three(
                nbr_z[k][0],
                nbr_z[k][1],
                cz[i][s],
                lambda j: jnp.broadcast_to(
                    XR[1 - k, j, CROSS : CROSS + 1, lo : lo + H], (8, H)
                ),
            )
            return lroll(v, -E if half else E)

        heat = jnp.concatenate(
            [
                jnp.concatenate([left, right, y_tile], axis=1),
                jnp.concatenate([x_left, x_right, quadrants(from_x)], axis=1),
            ],
            axis=0,
        )
        acc = acc + jnp.where(WY[s] > 0.5, heat, 0.0)

        def updown(k):
            za, zb = nbr_z[k]
            return fluid_slot(za, zb, nz[k] + 1), fluid_slot(za, zb, nz[k] - 1)

        tile = jnp.where(
            zw < 8,
            lroll(Q[fluid_slot(z0, z1, oz - 1), 5], 1 - E),
            lroll(Q[fluid_slot(z0, z1, oz + 1), 6], E - 1),
        )
        a, c = [], []
        for k in range(2):
            u, d = updown(k)
            a.append(jnp.broadcast_to(XR[1 - k, u, EDGE_Z : EDGE_Z + 1, :], (8, W)))
            c.append(jnp.broadcast_to(XR[1 - k, d, EDGE_Z : EDGE_Z + 1, :], (8, W)))
        a = jnp.where(r8 < 4, a[0], a[1])
        c = jnp.where(r8 < 4, c[0], c[1])
        x_tile = jnp.where(
            z8 < 8,
            jnp.where(wide_edge, lroll(c, 1 - E), lroll(c, 2 - E)),
            jnp.where(wide_edge, lroll(a, E - 1), lroll(a, E - 2)),
        )
        u, d = updown(2)
        a, c = YR[1, u], YR[1, d]
        y_up = jnp.where(
            zh < 8,
            jnp.where(group == 0, lroll(c, -7 * E + 1), lroll(c, -6 * E + 2)),
            jnp.where(group == 0, lroll(a, -5 * E - 1), lroll(a, -4 * E - 2)),
        )
        u, d = updown(3)
        a, c = YR[0, u], YR[0, d]
        y_down = jnp.where(
            zh < 8,
            jnp.where(group == 7, lroll(c, 1), lroll(c, 2 - E)),
            jnp.where(group == 7, lroll(a, 2 * E - 1), lroll(a, E - 2)),
        )

        def from_z(i):
            shift = 2 * E if CORNER_SRC[i][2] else -2 * E
            a = lroll(corner_heat(i, cz[i][s] + 1.0), shift + E - 1)
            c = lroll(corner_heat(i, cz[i][s] - 1.0), shift + 1 - E)
            return jnp.where(z8[:, :H] < 8, c, a)

        heat = jnp.concatenate(
            [
                jnp.concatenate([tile, jnp.where(group < 4, y_up, y_down)], axis=1),
                jnp.concatenate([x_tile, quadrants(from_z)], axis=1),
            ],
            axis=0,
        )
        R[s] = acc + jnp.where(WZ[s] > 0.5, heat, 0.0)

    upd = []
    sol = []
    for s in range(SB):
        d = R[s] * inv_center
        upd.append(d)
        sol.append(T[s] + d[0:E, 0:W])
    div = divergence(upd)
    for s in range(SB):
        r = R[s] - (upd[s] - div[s])
        R[s] = r
        upd[s] = coef[0][0] * upd[s] + coef[0][1] * r
        sol[s] = sol[s] + upd[s][0:E, 0:W]

    v = [x[:, 0:W] for x in upd]
    over = [rroll(x, -1) for x in v]
    f = [
        LX[s, :, 0:W] * (jnp.where(CODE[0, s, :, 0:W] == 1, over[1], over[0]) - v[s])
        for s in range(SB)
    ]
    under = [rroll(x, 1)[0:E] for x in f]
    code = [CODE[1, s, 0:E, 0:W] for s in range(SB)]
    div = []
    for s in range(SB):
        u = jnp.where(code[s] == 1, under[1], jnp.where(code[s] == 0, under[0], 0.0))
        div.append(f[s][0:E] - u)
    v = [x[0:E] for x in upd]
    over = [lroll(x, -E) for x in v]
    f = [
        LY[s, 0:E] * (jnp.where(CODE[2, s, 0:E] == 1, over[1], over[0]) - v[s])
        for s in range(SB)
    ]
    under = [lroll(x, E)[:, 0:W] for x in f]
    code = [CODE[3, s, 0:E, 0:W] for s in range(SB)]
    for s in range(SB):
        u = jnp.where(code[s] == 1, under[1], jnp.where(code[s] == 0, under[0], 0.0))
        div[s] = div[s] + (f[s][:, 0:W] - u)
    v = [x[0:E, 0:W] for x in upd]
    last, first = zw == E - 1, zw == 0
    up = [jnp.where(last, lroll(v[1], E - 1), lroll(v[0], -1)), lroll(v[1], -1)]
    f = [LZ[s, 0:E, 0:W] * (up[s] - v[s]) for s in range(SB)]
    under = [
        jnp.where(first, 0.0, lroll(f[0], 1)),
        jnp.where(first, lroll(f[0], 1 - E), lroll(f[1], 1)),
    ]
    for s in range(SB):
        r = R[s, 0:E, 0:W] - (v[s] - div[s] - (f[s] - under[s]))
        TO[s] = sol[s] + (coef[1][0][0:E, 0:W] * v[s] + coef[1][1][0:E, 0:W] * r)

    def x_face(b, side):
        shape = (8, W)
        df = -1 if side == 0 else 1
        dirn = 2 if side == 0 else 1
        bf = base_of(df, 0)
        main_id = nbr[b, dirn - 1]
        a = XR[side, slot(main_id, bf, FB)]
        val = a
        ids = jnp.full(shape, main_id)
        for r, p in enumerate(PX[side]):
            _, cy, cz = C[p]
            if r == 0:
                continue
            cid = nbr[b, OPP[p] - 1]
            if cy:
                which = jnp.full((8, H), slot(cid, base_of(df, -cy), FB))
                first, second, third = corner_rows(CORNER_OF[p])
                corner = jnp.where(which == 1, second, first)
                corner = jnp.where(which == 2, third, corner)
                corner = jnp.concatenate([corner, corner], axis=1)
                edge = l8 < E if cy > 0 else l8 >= W - E
                cand = jnp.where(edge, corner, a)
            else:
                edge = z8 == 0 if cz > 0 else z8 == E - 1
                cand = jnp.where(edge, XR[side, slot(cid, bf, FB)], a)
            val = jnp.where(r8 == r, cand, val)
            ids = jnp.where((r8 == r) & edge, jnp.full(shape, cid), ids)
        fall = FX[1 - side, b]
        wid = wall[b, dirn - 1]
        row = 7 if side == 0 else 0
        tw = XR[side, FB + slot(wid, bf, SB), row : row + 1, :]
        hot = (r8 == HEAT) & (jnp.full(shape, wid) >= 0)
        fall = jnp.where(hot, 2.0 * tw - fall, fall)
        return jnp.where(ids >= 0, val, fall)

    for b in range(FB):
        for side in range(2):
            xf = x_face(b, side)
            x = 0 if side == 0 else E - 1
            for r, p in enumerate(PX[side]):
                GO[b, p, x : x + 1, :] = xf[r : r + 1]
            QO[b, 1 + side, x : x + 1, :] = xf[HEAT : HEAT + 1]

    for i in range(N_COPY):

        @pl.when(near(*steps[i]))
        def _():
            copies[i].wait_send()


def store_kernel(fluid, heat, solid, fluid_out, heat_out, solid_out, sem):
    pairs = [(fluid, fluid_out), (heat, heat_out), (solid, solid_out)]
    for i, (src, dst) in enumerate(pairs):
        for x in range(E):
            pltpu.make_async_copy(
                src.at[..., x, :], dst.at[..., pl.ds(W * x, W)], sem.at[i]
            ).start()
    for i, (src, dst) in enumerate(pairs):
        pltpu.make_async_copy(src, src, sem.at[i]).wait()


def body(nf, nc, fluid_pop, heat_pop, solid_temp, material, cond, nbr, wall, snbr, sflu):
    hbm = pl.BlockSpec(memory_space=pltpu.HBM)

    def vm(*shape):
        return pltpu.VMEM(shape, F32)

    vmem = pl.BlockSpec(memory_space=pltpu.VMEM)
    fields = pl.pallas_call(
        functools.partial(kernel, nf, nc),
        out_shape=(
            vm(FB, 19, E, W),
            vm(FB, 7, E, W),
            vm(SB, E, W),
        ),
        in_specs=[hbm] * 9,
        out_specs=(vmem, vmem, vmem),
        scratch_shapes=[
            vm(FB, 19, E, W),
            vm(FB, 7, E, W),
            vm(SB, E, W),
            pltpu.VMEM((SB, E, W), jnp.int32),
            vm(SB, E, W),
            vm(2, FB, 8, W),
            vm(2, FB, E, H),
            vm(2, FB + SB, 8, W),
            vm(2, FB + SB, 8, W),
            vm(2, FB + SB, E, H),
            vm(2, FB + SB, E, H),
            vm(4, 1 + SB, 8, H),
            vm(4, 1 + SB, 8, H),
        ]
        + [vm(SB, EX, EL)] * 9
        + [
            pltpu.VMEM((4, SB, EX, EL), jnp.int32),
            pltpu.SMEM(cond.shape, F32),
            pltpu.SMEM(nbr.shape, jnp.int32),
            pltpu.SMEM(wall.shape, jnp.int32),
            pltpu.SMEM(snbr.shape, jnp.int32),
            pltpu.SMEM(sflu.shape, jnp.int32),
            pltpu.SemaphoreType.DMA((9,)),
            pltpu.SemaphoreType.DMA((N_COPY,)),
            pltpu.SemaphoreType.DMA((N_COPY,)),
        ],
        compiler_params=pltpu.CompilerParams(
            collective_id=0, has_side_effects=True, vmem_limit_bytes=LIMIT
        ),
    )(fluid_pop, heat_pop, solid_temp, material, cond, nbr, wall, snbr, sflu)
    return pl.pallas_call(
        store_kernel,
        out_shape=(
            jax.ShapeDtypeStruct(fluid_pop.shape, F32),
            jax.ShapeDtypeStruct(heat_pop.shape, F32),
            jax.ShapeDtypeStruct(solid_temp.shape, F32),
        ),
        in_specs=[pl.BlockSpec(memory_space=pl.ANY)] * 3,
        out_specs=(hbm, hbm, hbm),
        scratch_shapes=[pltpu.SemaphoreType.DMA((3,))],
        compiler_params=pltpu.CompilerParams(vmem_limit_bytes=8 * 1024 * 1024),
    )(*fields)


def solution(mesh):
    both = ("flow", "cross")
    in_specs = (
        P(both, None, None),
        P(both, None, None),
        P(both, None),
        P(both, None),
        P(),
        P(both, None),
        P(both, None),
        P(both, None),
        P(both, None),
    )
    out_specs = (P(both, None, None), P(both, None, None), P(both, None))
    return jax.shard_map(
        functools.partial(body, mesh.shape["flow"], mesh.shape["cross"]),
        mesh=mesh,
        in_specs=in_specs,
        out_specs=out_specs,
        check_vma=False,
    )
```

```python
import functools

import jax
import jax.numpy as jnp
from jax import lax
from jax.experimental import pallas as pl
from jax.experimental.pallas import tpu as pltpu
from jax.sharding import PartitionSpec as P

MESH = pl.DeviceIdType.MESH
F32 = jnp.float32
E = 16
W = 256
H = 128
FB = 3
SB = 2
C = [
    (0, 0, 0),
    (1, 0, 0),
    (-1, 0, 0),
    (0, 1, 0),
    (0, -1, 0),
    (0, 0, 1),
    (0, 0, -1),
    (1, 1, 0),
    (-1, -1, 0),
    (1, -1, 0),
    (-1, 1, 0),
    (1, 0, 1),
    (-1, 0, -1),
    (1, 0, -1),
    (-1, 0, 1),
    (0, 1, 1),
    (0, -1, -1),
    (0, 1, -1),
    (0, -1, 1),
]
OPP = [0, 2, 1, 4, 3, 6, 5, 8, 7, 10, 9, 12, 11, 14, 13, 16, 15, 18, 17]
PX = ([1, 7, 9, 11, 13], [2, 8, 10, 12, 14])
PY = ([3, 7, 10, 15, 17], [4, 8, 9, 16, 18])
HEAT = 5
SIDES = [(1, 0), (-1, 0), (0, 1), (0, -1)]
CORNERS = [(1, 1), (1, -1), (-1, -1), (-1, 1)]
PEERS = CORNERS + SIDES
CORNER_SRC = [(0, 1, 1), (0, 2, 0), (1, 1, 0), (1, 2, 1)]
CORNER_OF = {7: 0, 9: 1, 8: 2, 10: 3}
EDGE_Z = 6
CROSS = 7
N_COPY = 8
NZ = 5
NONE = -9
EX = 24
EL = 384
LIMIT = 60 * 1024 * 1024


def lroll(v, s):
    n = v.shape[1]
    s = s % n
    return v if s == 0 else pltpu.roll(v, s, axis=1)


def rroll(v, s):
    n = v.shape[0]
    s = s % n
    return v if s == 0 else pltpu.roll(v, s, axis=0)


def lanes(shape):
    return lax.broadcasted_iota(jnp.int32, shape, 1)


def rows(shape):
    return lax.broadcasted_iota(jnp.int32, shape, 0)


def collide_tile(G, Q, b, rs, ls):
    def ld(p):
        return G[b, p, rs, ls]

    f = [ld(p) for p in range(19)]
    w = [v * (1.0 / 3.0 if p == 0 else 1.0 / 18.0 if p < 7 else 1.0 / 36.0) for p, v in enumerate(f)]
    d = [None] * 19
    for p in (1, 3, 5, 7, 9, 11, 13, 15, 17):
        d[p] = w[p] - w[p + 1]
    s1 = ((w[1] + w[2]) + (w[3] + w[4])) + (w[5] + w[6])
    s2 = (((w[7] + w[8]) + (w[9] + w[10])) + ((w[11] + w[12]) + (w[13] + w[14]))) + (
        (w[15] + w[16]) + (w[17] + w[18])
    )
    rho = (w[0] + s1) + s2
    jx = d[1] + ((d[7] + d[9]) + (d[11] + d[13]))
    jy = d[3] + ((d[7] - d[9]) + (d[15] + d[17]))
    jz = d[5] + ((d[11] - d[13]) + (d[15] - d[17]))
    inv = 1.0 / rho
    u = (jx * inv, jy * inv, jz * inv)
    j = (jx, jy, jz)
    base = 1.25 * rho - 1.875 * (jx * u[0] + jy * u[1] + jz * u[2])
    G[b, 0, rs, ls] = base - 0.25 * f[0]
    cus = {}
    for p in (1, 3, 5, 7, 9, 11, 13, 15, 17):
        cj = None
        cu = None
        for a in range(3):
            s = C[p][a]
            if s == 0:
                continue
            if cj is None:
                cj, cu = j[a], u[a]
            elif s > 0:
                cj, cu = cj + j[a], cu + u[a]
            else:
                cj, cu = cj - j[a], cu - u[a]
        even = base + 5.625 * (cj * cu)
        odd = 3.75 * cj
        G[b, p, rs, ls] = (even + odd) - 0.25 * f[p]
        G[b, p + 1, rs, ls] = (even - odd) - 0.25 * f[p + 1]
        cus[p] = cu
    h = [Q[b, k, rs, ls] for k in range(7)]
    g = [v * (0.25 if k == 0 else 0.125) for k, v in enumerate(h)]
    gs = ((g[1] + g[2]) + (g[3] + g[4])) + (g[5] + g[6])
    t11 = (g[0] + gs) * 1.1
    t44 = 4.0 * t11
    Q[b, 0, rs, ls] = t11 - 0.1 * h[0]
    for k in (1, 3, 5):
        o = t44 * cus[k]
        Q[b, k, rs, ls] = (t11 + o) - 0.1 * h[k]
        Q[b, k + 1, rs, ls] = (t11 - o) - 0.1 * h[k + 1]


def kernel(
    nf,
    nc,
    fluid_in,
    heat_in,
    temp_in,
    mat_in,
    cond_in,
    nbr_in,
    wall_in,
    snbr_in,
    sflu_in,
    GO,
    QO,
    TO,
    G,
    Q,
    T,
    M,
    KAP,
    FX,
    FY,
    XS,
    XR,
    YS,
    YR,
    CS,
    CR,
    TE,
    KE,
    WX,
    WY,
    WZ,
    LX,
    LY,
    LZ,
    R,
    CODE,
    cond,
    nbr,
    wall,
    snbr,
    sflu,
    in_sem,
    send_sem,
    recv_sem,
):
    fl = lax.axis_index("flow")
    cr = lax.axis_index("cross")
    inside = {-1: (fl > 0, cr > 0), 0: (True, True), 1: (fl < nf - 1, cr < nc - 1)}

    def near(df, dc):
        a, b = inside[df][0], inside[dc][1]
        if df == 0:
            return b
        return a if dc == 0 else jnp.logical_and(a, b)

    barrier = pltpu.get_barrier_semaphore()
    for df, dc in PEERS:

        @pl.when(near(df, dc))
        def _():
            pl.semaphore_signal(
                barrier, inc=1, device_id=(fl + df, cr + dc), device_id_type=MESH
            )

    nx = 2 - (fl == 0).astype(jnp.int32) - (fl == nf - 1).astype(jnp.int32)
    ny = 2 - (cr == 0).astype(jnp.int32) - (cr == nc - 1).astype(jnp.int32)
    n_peers = nx + ny + nx * ny

    def load(src, dst, sem):
        for x in range(E):
            pltpu.make_async_copy(
                src.at[..., pl.ds(W * x, W)], dst.at[..., x, :], sem
            ).start()

    def all_of(ref, sem):
        return pltpu.make_async_copy(ref, ref, sem)

    tables = [
        (cond_in, cond, 4),
        (nbr_in, nbr, 5),
        (wall_in, wall, 6),
        (snbr_in, snbr, 7),
        (sflu_in, sflu, 8),
    ]
    tables = [pltpu.make_async_copy(a, b, in_sem.at[i]) for a, b, i in tables]
    for c in tables:
        c.start()
    load(temp_in, T, in_sem.at[0])
    load(mat_in, M, in_sem.at[1])
    load(fluid_in, G, in_sem.at[2])
    load(heat_in, Q, in_sem.at[3])

    copies = {}
    steps = {}

    def send(i, src, dst, df, dc):
        copies[i] = pltpu.make_async_remote_copy(
            src_ref=src,
            dst_ref=dst,
            send_sem=send_sem.at[i],
            recv_sem=recv_sem.at[i],
            device_id=(fl + df, cr + dc),
            device_id_type=MESH,
        )
        steps[i] = (df, dc)

        @pl.when(near(df, dc))
        def _():
            copies[i].start()

    def received(i):
        @pl.when(near(-steps[i][0], -steps[i][1]))
        def _():
            copies[i].wait_recv()

    wide = (E, W)
    lw = lanes(wide)
    zw = jnp.bitwise_and(lw, E - 1)
    lh = lanes((E, H))
    zh = jnp.bitwise_and(lh, E - 1)
    group = jnp.right_shift(lh, 4)
    r8 = rows((8, W))
    l8 = lanes((8, W))
    z8 = jnp.bitwise_and(l8, E - 1)
    q8 = rows((8, H))
    g8 = jnp.right_shift(lanes((8, H)), 4)

    def base_of(df, dc):
        return (fl + df) * nc + (cr + dc)

    def slot(idv, base, n):
        return jnp.clip(idv - base * n, 0, n - 1)

    def num(flag):
        return jnp.where(flag, 1, 0)

    def on(flag, like):
        return jnp.full(like.shape, flag) > 0

    for c in tables:
        c.wait()

    here = base_of(0, 0)
    below0 = sflu[0, 5]
    below1 = sflu[1, 5]
    z0 = jnp.where(below0 >= 0, slot(below0, here, FB) + 1, 0)
    z1 = jnp.where(below1 >= 0, slot(below1, here, FB) + 2, z0 + 1)
    own_z = (z0, z1)
    flu_z = [b + num(b >= z0) + num(b + 1 >= z1) for b in range(FB)]

    def fluid_slot(za, zb, z):
        return jnp.clip(z - num(za < z) - num(zb < z), 0, FB - 1)

    nbr_z = []
    nbr_has = []
    for k in range(4):
        df, dc = C[k + 1][0], C[k + 1][1]
        first = base_of(df, dc) * SB
        za = zb = 0
        pairs = [(wall[b, k], flu_z[b]) for b in range(FB)]
        pairs += [(snbr[s, k], own_z[s]) for s in range(SB)]
        for idv, z in pairs:
            za = za + jnp.where(idv == first, z, 0)
            zb = zb + jnp.where(idv == first + 1, z, 0)
        has = num(near(df, dc))
        nbr_has.append(has)
        nbr_z.append((jnp.where(has > 0, za, NONE), jnp.where(has > 0, zb, NONE)))

    with jax.named_scope("wait_solid"):
        all_of(T, in_sem.at[0]).wait()
        all_of(M, in_sem.at[1]).wait()
    for s in range(SB):
        m = M[s]
        k = jnp.full(wide, cond[0], F32)
        for i in range(1, 8):
            k = jnp.where(m == i, cond[i], k)
        KAP[s] = k
        zf = jnp.full((8, W), own_z[s]).astype(F32)
        t = T[s]
        XS[0, FB + s] = jnp.where(r8 > 4, t[8:], jnp.where(r8 == 4, zf, rroll(k[8:], 4)))
        XS[1, FB + s] = jnp.where(r8 < 3, t[:8], jnp.where(r8 == 3, zf, rroll(k[:8], 4)))
        YS[0, FB + s] = jnp.where(lh >= 64, t[:, H:], lroll(k[:, H:], 64))
        YS[1, FB + s] = jnp.where(lh < 64, t[:, :H], lroll(k[:, :H], 64))

    def pack_y(pieces, side):
        acc = None
        for g, v in enumerate(pieces):
            r = lroll(v, E * g - (H - E)) if side == 0 else lroll(v, E * g)
            acc = r if acc is None else jnp.where(group == g, r, acc)
        return acc

    def ahead(v, p, z):
        _, cy, cz = C[p]
        if cz:
            edge = z == 0 if cz > 0 else z == E - 1
            return jnp.where(edge, lroll(v, -(E - 1) * cz), lroll(v, cz))
        return lroll(v, E * cy)

    def two(v, first, second, z):
        return jnp.where((z == 0) | (z == E - 1), v, jnp.where(z < 8, first, second))

    with jax.named_scope("wait_pops"):
        all_of(G, in_sem.at[2]).wait()
        all_of(Q, in_sem.at[3]).wait()
    for b in range(FB):
        with jax.named_scope("collide"):
            for xh in range(2):
                for yh in range(2):
                    collide_tile(G, Q, b, pl.ds(8 * xh, 8), pl.ds(H * yh, H))
        for side in range(2):
            x = E - 1 if side == 0 else 0
            inner = E - 2 if side == 0 else 1

            def line(x_at, lo, n):
                zz = jnp.bitwise_and(lanes((1, n)), E - 1)
                up = Q[b, 6, x_at : x_at + 1, lo : lo + n]
                return jnp.where(zz < 8, up, Q[b, 5, x_at : x_at + 1, lo : lo + n])

            for r in range(5):
                FX[side, b, r : r + 1, :] = G[b, PX[side][r], x : x + 1, :]
            FX[side, b, HEAT : HEAT + 1, :] = Q[b, 1 + side, x : x + 1, :]
            z1w = jnp.bitwise_and(lanes((1, W)), E - 1)
            v = line(inner, 0, W)
            FX[side, b, EDGE_Z : EDGE_Z + 1, :] = two(
                line(x, 0, W), lroll(v, 1), lroll(v, -1), z1w
            )
            FX[side, b, CROSS : CROSS + 1, :H] = Q[b, 4, x : x + 1, :H]
            FX[side, b, CROSS : CROSS + 1, H:] = Q[b, 3, x : x + 1, H:]

            raw = FX[side, b]
            out = raw
            for r, p in enumerate(PX[side]):
                if r:
                    out = jnp.where(r8 == r, ahead(raw, p, z8), out)
            XS[side, b] = out

            half = pl.ds(H, H) if side == 0 else pl.ds(0, H)
            sgn = 1 if side == 0 else -1
            hz = jnp.where(zh < 8, Q[b, 6, :, half], Q[b, 5, :, half])
            hx = jnp.concatenate([Q[b, 2, 0:8, half], Q[b, 1, 8:16, half]], axis=0)
            raw = pack_y(
                [G[b, PY[side][r], :, half] for r in range(5)]
                + [
                    Q[b, 3 + side, :, half],
                    two(hz, lroll(hz, sgn * E + 1), lroll(hz, sgn * E - 1), zh),
                    hx,
                ],
                side,
            )
            FY[side, b] = raw
            out = raw
            for q, p in enumerate(PY[side]):
                cx = C[p][0]
                if q:
                    v = rroll(raw, cx) if cx else ahead(raw, p, zh)
                    out = jnp.where(group == q, v, out)
            YS[side, b] = out
            for i in range(4):
                cs, row, ch = CORNER_SRC[i]
                if cs != side:
                    continue
                sg = -1 if ch else 1
                hp = 3 if ch else 4
                lo = H * ch
                gg = jnp.right_shift(lanes((1, H)), 4)
                at = (lambda d: 7 - d) if ch else (lambda d: d)
                acc = Q[b, 1 + side, x : x + 1, lo : lo + H]
                extra = [
                    (2, line(x, lo, H)),
                    (7, G[b, PX[side][row], x : x + 1, lo : lo + H]),
                    (4, Q[b, hp, x : x + 1, lo : lo + H]),
                    (5, Q[b, hp, inner : inner + 1, lo : lo + H]),
                ]
                for d, v in extra:
                    acc = jnp.where(gg == at(d), lroll(v, sg * E * d), acc)
                CS[i, 0, b : b + 1, :] = acc

    for i in range(4):
        side, _, ch = CORNER_SRC[i]
        for s in range(SB):
            CS[i, 1 + s] = XS[side, FB + s, :, H * ch : H * ch + H]

    with jax.named_scope("entry_barrier"):
        pl.semaphore_wait(barrier, n_peers)
    for i, (df, dc) in enumerate(CORNERS):
        send(4 + i, CS.at[i], CR.at[i], df, dc)
    for i, (df, dc) in list(enumerate(SIDES))[::-1]:
        side = i % 2
        if i < 2:
            send(i, XS.at[side], XR.at[side], df, dc)
        else:
            send(i, YS.at[side], YR.at[side], df, dc)

    def stream(b):
        def main(ref, p):
            cx, cy, cz = C[p]
            s = E * cy + cz
            out = lroll(rroll(ref[b, p], cx), s)
            if cz:
                back = ref[b, OPP[p]]
                adj = (b - cz) % FB
                if ref is Q:
                    wid = wall[b, (6 if cz > 0 else 5) - 1]
                    tw = lroll(T[slot(wid, here, SB)], -(E - 1) * cz)
                    back = jnp.where(jnp.full(wide, wid) >= 0, 2.0 * tw - back, back)
                if 0 <= b - cz < FB:
                    other = lroll(rroll(ref[adj, p], cx), E * cy - (E - 1) * cz)
                    zid = nbr[b, (6 if cz > 0 else 5) - 1]
                    back = jnp.where(jnp.full(wide, zid) >= 0, other, back)
                edge = zw == 0 if cz > 0 else zw == E - 1
                out = jnp.where(edge, back, out)
            return out

        GO[b, 0] = G[b, 0]
        QO[b, 0] = Q[b, 0]
        for p in range(1, 19):
            GO[b, p] = main(G, p)
        for p in range(1, 7):
            QO[b, p] = main(Q, p)

    with jax.named_scope("stream"):
        for b in range(FB):
            stream(b)

    ext = (EX, EL)
    ze = jnp.bitwise_and(lanes(ext), E - 1)

    def piece(flag, v):
        return jnp.where(on(flag, v), v, 0.0)

    with jax.named_scope("wait_y"):
        for i in (2, 3):
            received(i)

    def y_face(b, side):
        shape = (E, H)
        dc = -1 if side == 0 else 1
        dirn = 4 if side == 0 else 3
        bf = base_of(0, dc)
        main_id = nbr[b, dirn - 1]
        a = YR[side, slot(main_id, bf, FB)]
        val = a
        ids = jnp.full(shape, main_id)
        for r, p in enumerate(PY[side]):
            cx, _, cz = C[p]
            if r == 0:
                continue
            if cx:
                continue
            cid = nbr[b, OPP[p] - 1]
            edge = (group == r) & (zh == 0 if cz > 0 else zh == E - 1)
            val = jnp.where(edge, YR[side, slot(cid, bf, FB)], val)
            ids = jnp.where(edge, jnp.full(shape, cid), ids)
        fall = FY[1 - side, b]
        wid = wall[b, dirn - 1]
        tw = YR[side, FB + slot(wid, bf, SB)]
        tw = lroll(tw, -2 * E if side == 0 else HEAT * E)
        hot = (group == HEAT) & (jnp.full(shape, wid) >= 0)
        fall = jnp.where(hot, 2.0 * tw - fall, fall)
        return jnp.where(ids >= 0, val, fall)

    for b in range(FB):
        for side in range(2):
            yf = y_face(b, side)
            half = pl.ds(0, H) if side == 0 else pl.ds(H, H)
            edge = lh < E if side == 0 else lh >= H - E
            back = 0 if side == 0 else H - E
            for q, p in enumerate(PY[side]):
                v = lroll(yf, back - E * q)
                GO[b, p, :, half] = jnp.where(edge, v, GO[b, p, :, half])
            v = lroll(yf, back - E * HEAT)
            QO[b, 3 + side, :, half] = jnp.where(edge, v, QO[b, 3 + side, :, half])
    with jax.named_scope("wait_x"):
        for i in (0, 1, 4, 5, 6, 7):
            received(i)

    def corner_z(i):
        side = CORNER_SRC[i][0]
        r = 4 if side == 0 else 3
        return [
            jnp.broadcast_to(CR[i, 1 + s, r : r + 1, :], (8, H))
            for s in range(SB)
        ]

    quad = [[2, 3], [1, 0]]
    chas = [jnp.full((8, H), num(near(-df, -dc))) > 0 for df, dc in CORNERS]
    cz = [[jnp.where(chas[i], v, float(NONE)) for v in corner_z(i)] for i in range(4)]

    def quadrants(fn):
        up = jnp.where(g8 < 4, fn(quad[0][0]), fn(quad[0][1]))
        down = jnp.where(g8 < 4, fn(quad[1][0]), fn(quad[1][1]))
        return jnp.where(q8 < 4, up, down)

    def splat(shape, v):
        return jnp.full(shape, v).astype(F32)

    Z = []
    for s in range(SB):
        TE[s, 0:E, 0:W] = T[s]
        KE[s, 0:E, 0:W] = KAP[s]
        a = piece(nbr_has[0], XR[1, FB + s])
        c = piece(nbr_has[1], XR[0, FB + s])
        TE[s, E:EX, 0:W] = jnp.where(r8 < 4, a, c)
        KE[s, E:EX, 0:W] = rroll(jnp.where(r8 < 4, c, a), 4)
        zx = jnp.where(r8 < 4, splat((8, W), nbr_z[0][s]), splat((8, W), nbr_z[1][s]))
        a = piece(nbr_has[2], YR[1, FB + s])
        c = piece(nbr_has[3], YR[0, FB + s])
        TE[s, 0:E, W:EL] = jnp.where(group < 4, a, c)
        KE[s, 0:E, W:EL] = lroll(jnp.where(group < 4, c, a), 64)
        zy = jnp.where(group < 4, splat((E, H), nbr_z[2][s]), splat((E, H), nbr_z[3][s]))

        def corner_solid(i):
            return jnp.where(chas[i], CR[i, 1 + s], 0.0)

        TE[s, E:EX, W:EL] = quadrants(corner_solid)
        KE[s, E:EX, W:EL] = quadrants(lambda i: rroll(corner_solid(i), 4))
        top = jnp.concatenate([splat(wide, own_z[s]), zy], axis=1)
        low = jnp.concatenate([zx, quadrants(lambda i: cz[i][s])], axis=1)
        Z.append(jnp.concatenate([top, low], axis=0))

    def link(k, kb):
        return (2.0 * k * kb) / jnp.maximum(k + kb, 0.05)

    def toward(k, v):
        return rroll(v, -1 if k == 0 else 1) if k < 2 else lroll(v, -E if k == 2 else E)

    wet = [[0.0, 0.0] for _ in range(SB)]
    for k in range(4):
        za, zb = toward(k, Z[0]), toward(k, Z[1])
        for s in range(SB):
            code = jnp.where(zb == Z[s], 1, jnp.where(za == Z[s], 0, 2))
            CODE[k, s] = code
            wet[s][k // 2] = jnp.where((code == 2) & (za >= 0.0), 1.0, wet[s][k // 2])
    adj = Z[1] == Z[0] + 1.0
    top, bottom = ze == E - 1, ze == 0
    wet_z = [
        (top & (~adj) & (Z[0] < NZ - 1.0) & (Z[0] >= 0.0)) | (bottom & (Z[0] > 0.0)),
        (top & (Z[1] < NZ - 1.0) & (Z[1] >= 0.0)) | (bottom & (~adj) & (Z[1] >= 0.0)),
    ]
    for s in range(SB):
        WX[s] = wet[s][0]
        WY[s] = wet[s][1]
        WZ[s] = jnp.where(wet_z[s], 1.0, 0.0)

    def chosen(k, s, v):
        code = CODE[k, s]
        return jnp.where(code == 1, v[1], jnp.where(code == 0, v[0], 0.0))

    def z_up(v):
        return [jnp.where(top, lroll(v[1], E - 1), lroll(v[0], -1)), lroll(v[1], -1)]

    def divergence(v):
        div = []
        for k, links in ((0, LX), (2, LY)):
            over = [toward(k, x) for x in v]
            f = [
                links[s] * (jnp.where(CODE[k, s] == 1, over[1], over[0]) - v[s])
                for s in range(SB)
            ]
            under = [toward(k + 1, x) for x in f]
            part = [f[s] - chosen(k + 1, s, under) for s in range(SB)]
            div = part if k == 0 else [a + b for a, b in zip(div, part)]
        up = z_up(v)
        f = [LZ[s] * (up[s] - v[s]) for s in range(SB)]
        under = [
            jnp.where(bottom, 0.0, lroll(f[0], 1)),
            jnp.where(bottom, lroll(f[0], 1 - E), lroll(f[1], 1)),
        ]
        return [div[s] + (f[s] - under[s]) for s in range(SB)]

    kk = [KE[s] for s in range(SB)]
    for k, links in ((0, LX), (2, LY)):
        over = [toward(k, x) for x in kk]
        for s in range(SB):
            links[s] = link(kk[s], chosen(k, s, over))
    up = z_up(kk)
    LZ[0] = link(kk[0], jnp.where(top & ~adj, 0.0, up[0]))
    LZ[1] = link(kk[1], jnp.where(top, 0.0, up[1]))
    tt = [TE[s] for s in range(SB)]
    div = divergence(tt)
    for s in range(SB):
        R[s] = div[s] - (WX[s] + WY[s] + WZ[s]) * tt[s]

    kmax = cond[0]
    for i in range(1, 8):
        kmax = jnp.maximum(kmax, cond[i])
    radius = jnp.full((8, H), kmax * 6.0, F32)
    center = radius + 1.0
    sigma = center / radius

    def grow(v):
        v = jnp.concatenate([v] * (EX // 8), axis=0)
        return jnp.concatenate([v] * (EL // H), axis=1)

    inv_center = grow(1.0 / center)
    rho0 = 1.0 / sigma
    rho1 = 1.0 / (2.0 * sigma - rho0)
    rho2 = 1.0 / (2.0 * sigma - rho1)
    coef = [
        (grow(rho1 * rho0), grow(2.0 * rho1 / radius)),
        (grow(rho2 * rho1), grow(2.0 * rho2 / radius)),
    ]


    def corner_rows(i):
        return [jnp.broadcast_to(CR[i, 0, j : j + 1, :], (8, H)) for j in range(FB)]

    def corner_heat(i, z):
        f = z - jnp.where(cz[i][0] < z, 1.0, 0.0) - jnp.where(cz[i][1] < z, 1.0, 0.0)
        a, b, c = corner_rows(i)
        return jnp.where(f < 0.5, a, jnp.where(f < 1.5, b, c))

    def of_three(za, zb, z, fn):
        f = z - jnp.where(za < z, 1.0, 0.0) - jnp.where(zb < z, 1.0, 0.0)
        return jnp.where(f < 0.5, fn(0), jnp.where(f < 1.5, fn(1), fn(2)))

    row_edge = (q8 == 0) | (q8 == 7)
    wide_edge = (r8 == 0) | (r8 == 7)

    def stack(v):
        return jnp.concatenate([v, v], axis=0)

    for s in range(SB):
        oz = own_z[s]
        nz = [nbr_z[k][s] for k in range(4)]
        ozf = splat((8, H), oz)
        nzf = [splat((8, H), z) for z in nz]
        f_side = [fluid_slot(nbr_z[k][0], nbr_z[k][1], oz) for k in range(4)]
        f_own = [fluid_slot(z0, z1, nz[k]) for k in range(4)]

        own_lo = jnp.broadcast_to(XR[0, f_side[1], HEAT : HEAT + 1, :], (8, W))
        own_hi = jnp.broadcast_to(XR[1, f_side[0], HEAT : HEAT + 1, :], (8, W))
        x_tile = jnp.where(
            r8 < 4,
            jnp.broadcast_to(Q[f_own[0], 1, E - 1 : E, :], (8, W)),
            jnp.broadcast_to(Q[f_own[1], 2, 0:1, :], (8, W)),
        )
        y_lo = jnp.where(g8 < 4, corner_heat(1, nzf[2]), corner_heat(0, nzf[3]))
        y_hi = jnp.where(g8 < 4, corner_heat(2, nzf[2]), corner_heat(3, nzf[3]))

        def from_y(i):
            half = CORNER_SRC[i][2]
            k = 3 if half else 2
            row = 0 if i < 2 else E - 1
            v = of_three(
                nbr_z[k][0],
                nbr_z[k][1],
                cz[i][s],
                lambda j: jnp.broadcast_to(YR[1 - half, j, row : row + 1, :], (8, H))
                if not half
                else jnp.broadcast_to(YR[0, j, row : row + 1, :], (8, H)),
            )
            return v if half else lroll(v, E)

        heat = jnp.concatenate(
            [
                jnp.concatenate([own_lo, y_lo], axis=1),
                jnp.concatenate([own_hi, y_hi], axis=1),
                jnp.concatenate([x_tile, quadrants(from_y)], axis=1),
            ],
            axis=0,
        )
        acc = R[s] + jnp.where(WX[s] > 0.5, heat, 0.0)

        left = lroll(YR[0, f_side[3]], -5 * E)
        right = lroll(YR[1, f_side[2]], 2 * E)

        def from_corner(i, z):
            v = corner_heat(i, z)
            if CORNER_SRC[i][2]:
                return jnp.where(row_edge, lroll(v, -3 * E), lroll(v, -2 * E))
            return jnp.where(row_edge, lroll(v, 3 * E), lroll(v, 2 * E))

        x_left = jnp.where(q8 < 4, from_corner(3, nzf[0]), from_corner(0, nzf[1]))
        x_right = jnp.where(q8 < 4, from_corner(2, nzf[0]), from_corner(1, nzf[1]))
        y_tile = jnp.where(
            group < 4,
            lroll(Q[f_own[2], 3, :, H:W], E),
            lroll(Q[f_own[3], 4, :, 0:H], -E),
        )

        def from_x(i):
            half = CORNER_SRC[i][2]
            k = 1 if i < 2 else 0
            lo = 0 if half else H
            v = of_three(
                nbr_z[k][0],
                nbr_z[k][1],
                cz[i][s],
                lambda j: jnp.broadcast_to(
                    XR[1 - k, j, CROSS : CROSS + 1, lo : lo + H], (8, H)
                ),
            )
            return lroll(v, -E if half else E)

        heat = jnp.concatenate(
            [
                jnp.concatenate([left, right, y_tile], axis=1),
                jnp.concatenate([x_left, x_right, quadrants(from_x)], axis=1),
            ],
            axis=0,
        )
        acc = acc + jnp.where(WY[s] > 0.5, heat, 0.0)

        def updown(k):
            za, zb = nbr_z[k]
            return fluid_slot(za, zb, nz[k] + 1), fluid_slot(za, zb, nz[k] - 1)

        tile = jnp.where(
            zw < 8,
            lroll(Q[fluid_slot(z0, z1, oz - 1), 5], 1 - E),
            lroll(Q[fluid_slot(z0, z1, oz + 1), 6], E - 1),
        )
        a, c = [], []
        for k in range(2):
            u, d = updown(k)
            a.append(jnp.broadcast_to(XR[1 - k, u, EDGE_Z : EDGE_Z + 1, :], (8, W)))
            c.append(jnp.broadcast_to(XR[1 - k, d, EDGE_Z : EDGE_Z + 1, :], (8, W)))
        a = jnp.where(r8 < 4, a[0], a[1])
        c = jnp.where(r8 < 4, c[0], c[1])
        x_tile = jnp.where(
            z8 < 8,
            jnp.where(wide_edge, lroll(c, 1 - E), lroll(c, 2 - E)),
            jnp.where(wide_edge, lroll(a, E - 1), lroll(a, E - 2)),
        )
        u, d = updown(2)
        a, c = YR[1, u], YR[1, d]
        y_up = jnp.where(
            zh < 8,
            jnp.where(group == 0, lroll(c, -7 * E + 1), lroll(c, -6 * E + 2)),
            jnp.where(group == 0, lroll(a, -5 * E - 1), lroll(a, -4 * E - 2)),
        )
        u, d = updown(3)
        a, c = YR[0, u], YR[0, d]
        y_down = jnp.where(
            zh < 8,
            jnp.where(group == 7, lroll(c, 1), lroll(c, 2 - E)),
            jnp.where(group == 7, lroll(a, 2 * E - 1), lroll(a, E - 2)),
        )

        def from_z(i):
            shift = 2 * E if CORNER_SRC[i][2] else -2 * E
            a = lroll(corner_heat(i, cz[i][s] + 1.0), shift + E - 1)
            c = lroll(corner_heat(i, cz[i][s] - 1.0), shift + 1 - E)
            return jnp.where(z8[:, :H] < 8, c, a)

        heat = jnp.concatenate(
            [
                jnp.concatenate([tile, jnp.where(group < 4, y_up, y_down)], axis=1),
                jnp.concatenate([x_tile, quadrants(from_z)], axis=1),
            ],
            axis=0,
        )
        R[s] = acc + jnp.where(WZ[s] > 0.5, heat, 0.0)

    upd = []
    sol = []
    for s in range(SB):
        d = R[s] * inv_center
        upd.append(d)
        sol.append(T[s] + d[0:E, 0:W])
    div = divergence(upd)
    for s in range(SB):
        r = R[s] - (upd[s] - div[s])
        R[s] = r
        upd[s] = coef[0][0] * upd[s] + coef[0][1] * r
        sol[s] = sol[s] + upd[s][0:E, 0:W]

    v = [x[:, 0:W] for x in upd]
    over = [rroll(x, -1) for x in v]
    f = [
        LX[s, :, 0:W] * (jnp.where(CODE[0, s, :, 0:W] == 1, over[1], over[0]) - v[s])
        for s in range(SB)
    ]
    under = [rroll(x, 1)[0:E] for x in f]
    code = [CODE[1, s, 0:E, 0:W] for s in range(SB)]
    div = []
    for s in range(SB):
        u = jnp.where(code[s] == 1, under[1], jnp.where(code[s] == 0, under[0], 0.0))
        div.append(f[s][0:E] - u)
    v = [x[0:E] for x in upd]
    over = [lroll(x, -E) for x in v]
    f = [
        LY[s, 0:E] * (jnp.where(CODE[2, s, 0:E] == 1, over[1], over[0]) - v[s])
        for s in range(SB)
    ]
    under = [lroll(x, E)[:, 0:W] for x in f]
    code = [CODE[3, s, 0:E, 0:W] for s in range(SB)]
    for s in range(SB):
        u = jnp.where(code[s] == 1, under[1], jnp.where(code[s] == 0, under[0], 0.0))
        div[s] = div[s] + (f[s][:, 0:W] - u)
    v = [x[0:E, 0:W] for x in upd]
    last, first = zw == E - 1, zw == 0
    up = [jnp.where(last, lroll(v[1], E - 1), lroll(v[0], -1)), lroll(v[1], -1)]
    f = [LZ[s, 0:E, 0:W] * (up[s] - v[s]) for s in range(SB)]
    under = [
        jnp.where(first, 0.0, lroll(f[0], 1)),
        jnp.where(first, lroll(f[0], 1 - E), lroll(f[1], 1)),
    ]
    for s in range(SB):
        r = R[s, 0:E, 0:W] - (v[s] - div[s] - (f[s] - under[s]))
        TO[s] = sol[s] + (coef[1][0][0:E, 0:W] * v[s] + coef[1][1][0:E, 0:W] * r)

    def x_face(b, side):
        shape = (8, W)
        df = -1 if side == 0 else 1
        dirn = 2 if side == 0 else 1
        bf = base_of(df, 0)
        main_id = nbr[b, dirn - 1]
        a = XR[side, slot(main_id, bf, FB)]
        val = a
        ids = jnp.full(shape, main_id)
        for r, p in enumerate(PX[side]):
            _, cy, cz = C[p]
            if r == 0:
                continue
            cid = nbr[b, OPP[p] - 1]
            if cy:
                which = jnp.full((8, H), slot(cid, base_of(df, -cy), FB))
                first, second, third = corner_rows(CORNER_OF[p])
                corner = jnp.where(which == 1, second, first)
                corner = jnp.where(which == 2, third, corner)
                corner = jnp.concatenate([corner, corner], axis=1)
                edge = l8 < E if cy > 0 else l8 >= W - E
                cand = jnp.where(edge, corner, a)
            else:
                edge = z8 == 0 if cz > 0 else z8 == E - 1
                cand = jnp.where(edge, XR[side, slot(cid, bf, FB)], a)
            val = jnp.where(r8 == r, cand, val)
            ids = jnp.where((r8 == r) & edge, jnp.full(shape, cid), ids)
        fall = FX[1 - side, b]
        wid = wall[b, dirn - 1]
        row = 7 if side == 0 else 0
        tw = XR[side, FB + slot(wid, bf, SB), row : row + 1, :]
        hot = (r8 == HEAT) & (jnp.full(shape, wid) >= 0)
        fall = jnp.where(hot, 2.0 * tw - fall, fall)
        return jnp.where(ids >= 0, val, fall)

    for b in range(FB):
        for side in range(2):
            xf = x_face(b, side)
            x = 0 if side == 0 else E - 1
            for r, p in enumerate(PX[side]):
                GO[b, p, x : x + 1, :] = xf[r : r + 1]
            QO[b, 1 + side, x : x + 1, :] = xf[HEAT : HEAT + 1]

    for i in range(N_COPY):

        @pl.when(near(*steps[i]))
        def _():
            copies[i].wait_send()


def store_kernel(fluid, heat, solid, fluid_out, heat_out, solid_out, sem):
    pairs = [(fluid, fluid_out), (heat, heat_out), (solid, solid_out)]
    for i, (src, dst) in enumerate(pairs):
        for x in range(E):
            pltpu.make_async_copy(
                src.at[..., x, :], dst.at[..., pl.ds(W * x, W)], sem.at[i]
            ).start()
    for i, (src, dst) in enumerate(pairs):
        pltpu.make_async_copy(src, src, sem.at[i]).wait()


def body(nf, nc, fluid_pop, heat_pop, solid_temp, material, cond, nbr, wall, snbr, sflu):
    hbm = pl.BlockSpec(memory_space=pltpu.HBM)

    def vm(*shape):
        return pltpu.VMEM(shape, F32)

    vmem = pl.BlockSpec(memory_space=pltpu.VMEM)
    fields = pl.pallas_call(
        functools.partial(kernel, nf, nc),
        out_shape=(
            vm(FB, 19, E, W),
            vm(FB, 7, E, W),
            vm(SB, E, W),
        ),
        in_specs=[hbm] * 9,
        out_specs=(vmem, vmem, vmem),
        scratch_shapes=[
            vm(FB, 19, E, W),
            vm(FB, 7, E, W),
            vm(SB, E, W),
            pltpu.VMEM((SB, E, W), jnp.int32),
            vm(SB, E, W),
            vm(2, FB, 8, W),
            vm(2, FB, E, H),
            vm(2, FB + SB, 8, W),
            vm(2, FB + SB, 8, W),
            vm(2, FB + SB, E, H),
            vm(2, FB + SB, E, H),
            vm(4, 1 + SB, 8, H),
            vm(4, 1 + SB, 8, H),
        ]
        + [vm(SB, EX, EL)] * 9
        + [
            pltpu.VMEM((4, SB, EX, EL), jnp.int32),
            pltpu.SMEM(cond.shape, F32),
            pltpu.SMEM(nbr.shape, jnp.int32),
            pltpu.SMEM(wall.shape, jnp.int32),
            pltpu.SMEM(snbr.shape, jnp.int32),
            pltpu.SMEM(sflu.shape, jnp.int32),
            pltpu.SemaphoreType.DMA((9,)),
            pltpu.SemaphoreType.DMA((N_COPY,)),
            pltpu.SemaphoreType.DMA((N_COPY,)),
        ],
        compiler_params=pltpu.CompilerParams(
            collective_id=0, has_side_effects=True, vmem_limit_bytes=LIMIT
        ),
    )(fluid_pop, heat_pop, solid_temp, material, cond, nbr, wall, snbr, sflu)
    return pl.pallas_call(
        store_kernel,
        out_shape=(
            jax.ShapeDtypeStruct(fluid_pop.shape, F32),
            jax.ShapeDtypeStruct(heat_pop.shape, F32),
            jax.ShapeDtypeStruct(solid_temp.shape, F32),
        ),
        in_specs=[pl.BlockSpec(memory_space=pl.ANY)] * 3,
        out_specs=(hbm, hbm, hbm),
        scratch_shapes=[pltpu.SemaphoreType.DMA((3,))],
        compiler_params=pltpu.CompilerParams(vmem_limit_bytes=8 * 1024 * 1024),
    )(*fields)


def solution(mesh):
    both = ("flow", "cross")
    in_specs = (
        P(both, None, None),
        P(both, None, None),
        P(both, None),
        P(both, None),
        P(),
        P(both, None),
        P(both, None),
        P(both, None),
        P(both, None),
    )
    out_specs = (P(both, None, None), P(both, None, None), P(both, None))
    return jax.shard_map(
        functools.partial(body, mesh.shape["flow"], mesh.shape["cross"]),
        mesh=mesh,
        in_specs=in_specs,
        out_specs=out_specs,
        check_vma=False,
    )
```

```python
import functools

import jax
import jax.numpy as jnp
from jax import lax
from jax.experimental import pallas as pl
from jax.experimental.pallas import tpu as pltpu
from jax.sharding import PartitionSpec as P

MESH = pl.DeviceIdType.MESH
F32 = jnp.float32
E = 16
W = 256
H = 128
FB = 3
SB = 2
C = [
    (0, 0, 0),
    (1, 0, 0),
    (-1, 0, 0),
    (0, 1, 0),
    (0, -1, 0),
    (0, 0, 1),
    (0, 0, -1),
    (1, 1, 0),
    (-1, -1, 0),
    (1, -1, 0),
    (-1, 1, 0),
    (1, 0, 1),
    (-1, 0, -1),
    (1, 0, -1),
    (-1, 0, 1),
    (0, 1, 1),
    (0, -1, -1),
    (0, 1, -1),
    (0, -1, 1),
]
OPP = [0, 2, 1, 4, 3, 6, 5, 8, 7, 10, 9, 12, 11, 14, 13, 16, 15, 18, 17]
PX = ([1, 7, 9, 11, 13], [2, 8, 10, 12, 14])
PY = ([3, 7, 10, 15, 17], [4, 8, 9, 16, 18])
HEAT = 5
SIDES = [(1, 0), (-1, 0), (0, 1), (0, -1)]
CORNERS = [(1, 1), (1, -1), (-1, -1), (-1, 1)]
PEERS = CORNERS + SIDES
CORNER_SRC = [(0, 1, 1), (0, 2, 0), (1, 1, 0), (1, 2, 1)]
CORNER_OF = {7: 0, 9: 1, 8: 2, 10: 3}
EDGE_Z = 6
CROSS = 7
N_COPY = 8
NZ = 5
NONE = -9
EX = 24
EL = 384
LIMIT = 60 * 1024 * 1024


def lroll(v, s):
    n = v.shape[1]
    s = s % n
    return v if s == 0 else pltpu.roll(v, s, axis=1)


def rroll(v, s):
    n = v.shape[0]
    s = s % n
    return v if s == 0 else pltpu.roll(v, s, axis=0)


def lanes(shape):
    return lax.broadcasted_iota(jnp.int32, shape, 1)


def rows(shape):
    return lax.broadcasted_iota(jnp.int32, shape, 0)


def collide_tile(G, Q, b, rs, ls):
    def ld(p):
        return G[b, p, rs, ls]

    f = [ld(p) for p in range(19)]
    w = [v * (1.0 / 3.0 if p == 0 else 1.0 / 18.0 if p < 7 else 1.0 / 36.0) for p, v in enumerate(f)]
    d = [None] * 19
    for p in (1, 3, 5, 7, 9, 11, 13, 15, 17):
        d[p] = w[p] - w[p + 1]
    s1 = ((w[1] + w[2]) + (w[3] + w[4])) + (w[5] + w[6])
    s2 = (((w[7] + w[8]) + (w[9] + w[10])) + ((w[11] + w[12]) + (w[13] + w[14]))) + (
        (w[15] + w[16]) + (w[17] + w[18])
    )
    rho = (w[0] + s1) + s2
    jx = d[1] + ((d[7] + d[9]) + (d[11] + d[13]))
    jy = d[3] + ((d[7] - d[9]) + (d[15] + d[17]))
    jz = d[5] + ((d[11] - d[13]) + (d[15] - d[17]))
    inv = 1.0 / rho
    u = (jx * inv, jy * inv, jz * inv)
    j = (jx, jy, jz)
    base = 1.25 * rho - 1.875 * (jx * u[0] + jy * u[1] + jz * u[2])
    G[b, 0, rs, ls] = base - 0.25 * f[0]
    cus = {}
    for p in (1, 3, 5, 7, 9, 11, 13, 15, 17):
        cj = None
        cu = None
        for a in range(3):
            s = C[p][a]
            if s == 0:
                continue
            if cj is None:
                cj, cu = j[a], u[a]
            elif s > 0:
                cj, cu = cj + j[a], cu + u[a]
            else:
                cj, cu = cj - j[a], cu - u[a]
        even = base + 5.625 * (cj * cu)
        odd = 3.75 * cj
        G[b, p, rs, ls] = (even + odd) - 0.25 * f[p]
        G[b, p + 1, rs, ls] = (even - odd) - 0.25 * f[p + 1]
        cus[p] = cu
    h = [Q[b, k, rs, ls] for k in range(7)]
    g = [v * (0.25 if k == 0 else 0.125) for k, v in enumerate(h)]
    gs = ((g[1] + g[2]) + (g[3] + g[4])) + (g[5] + g[6])
    t11 = (g[0] + gs) * 1.1
    t44 = 4.0 * t11
    Q[b, 0, rs, ls] = t11 - 0.1 * h[0]
    for k in (1, 3, 5):
        o = t44 * cus[k]
        Q[b, k, rs, ls] = (t11 + o) - 0.1 * h[k]
        Q[b, k + 1, rs, ls] = (t11 - o) - 0.1 * h[k + 1]


def kernel(
    nf,
    nc,
    fluid_in,
    heat_in,
    temp_in,
    mat_in,
    cond_in,
    nbr_in,
    wall_in,
    snbr_in,
    sflu_in,
    GO,
    QO,
    TO,
    G,
    Q,
    T,
    M,
    KAP,
    FX,
    FY,
    XS,
    XR,
    YS,
    YR,
    CS,
    CR,
    TE,
    KE,
    WX,
    WY,
    WZ,
    LX,
    LY,
    LZ,
    R,
    CODE,
    cond,
    nbr,
    wall,
    snbr,
    sflu,
    in_sem,
    send_sem,
    recv_sem,
):
    fl = lax.axis_index("flow")
    cr = lax.axis_index("cross")
    inside = {-1: (fl > 0, cr > 0), 0: (True, True), 1: (fl < nf - 1, cr < nc - 1)}

    def near(df, dc):
        a, b = inside[df][0], inside[dc][1]
        if df == 0:
            return b
        return a if dc == 0 else jnp.logical_and(a, b)

    barrier = pltpu.get_barrier_semaphore()
    for df, dc in PEERS:

        @pl.when(near(df, dc))
        def _():
            pl.semaphore_signal(
                barrier, inc=1, device_id=(fl + df, cr + dc), device_id_type=MESH
            )

    nx = 2 - (fl == 0).astype(jnp.int32) - (fl == nf - 1).astype(jnp.int32)
    ny = 2 - (cr == 0).astype(jnp.int32) - (cr == nc - 1).astype(jnp.int32)
    n_peers = nx + ny + nx * ny

    def load(src, dst, sem):
        for x in range(E):
            pltpu.make_async_copy(
                src.at[..., pl.ds(W * x, W)], dst.at[..., x, :], sem
            ).start()

    def all_of(ref, sem):
        return pltpu.make_async_copy(ref, ref, sem)

    tables = [
        (cond_in, cond, 4),
        (nbr_in, nbr, 5),
        (wall_in, wall, 6),
        (snbr_in, snbr, 7),
        (sflu_in, sflu, 8),
    ]
    tables = [pltpu.make_async_copy(a, b, in_sem.at[i]) for a, b, i in tables]
    for c in tables:
        c.start()
    load(temp_in, T, in_sem.at[0])
    load(mat_in, M, in_sem.at[1])
    load(fluid_in, G, in_sem.at[2])
    load(heat_in, Q, in_sem.at[3])

    copies = {}
    steps = {}

    def send(i, src, dst, df, dc):
        copies[i] = pltpu.make_async_remote_copy(
            src_ref=src,
            dst_ref=dst,
            send_sem=send_sem.at[i],
            recv_sem=recv_sem.at[i],
            device_id=(fl + df, cr + dc),
            device_id_type=MESH,
        )
        steps[i] = (df, dc)

        @pl.when(near(df, dc))
        def _():
            copies[i].start()

    def received(i):
        @pl.when(near(-steps[i][0], -steps[i][1]))
        def _():
            copies[i].wait_recv()

    wide = (E, W)
    lw = lanes(wide)
    zw = jnp.bitwise_and(lw, E - 1)
    lh = lanes((E, H))
    zh = jnp.bitwise_and(lh, E - 1)
    group = jnp.right_shift(lh, 4)
    r8 = rows((8, W))
    l8 = lanes((8, W))
    z8 = jnp.bitwise_and(l8, E - 1)
    q8 = rows((8, H))
    g8 = jnp.right_shift(lanes((8, H)), 4)

    def base_of(df, dc):
        return (fl + df) * nc + (cr + dc)

    def slot(idv, base, n):
        return jnp.clip(idv - base * n, 0, n - 1)

    def num(flag):
        return jnp.where(flag, 1, 0)

    def on(flag, like):
        return jnp.full(like.shape, flag) > 0

    for c in tables:
        c.wait()

    here = base_of(0, 0)
    below0 = sflu[0, 5]
    below1 = sflu[1, 5]
    z0 = jnp.where(below0 >= 0, slot(below0, here, FB) + 1, 0)
    z1 = jnp.where(below1 >= 0, slot(below1, here, FB) + 2, z0 + 1)
    own_z = (z0, z1)
    flu_z = [b + num(b >= z0) + num(b + 1 >= z1) for b in range(FB)]

    def fluid_slot(za, zb, z):
        return jnp.clip(z - num(za < z) - num(zb < z), 0, FB - 1)

    nbr_z = []
    nbr_has = []
    for k in range(4):
        df, dc = C[k + 1][0], C[k + 1][1]
        first = base_of(df, dc) * SB
        za = zb = 0
        pairs = [(wall[b, k], flu_z[b]) for b in range(FB)]
        pairs += [(snbr[s, k], own_z[s]) for s in range(SB)]
        for idv, z in pairs:
            za = za + jnp.where(idv == first, z, 0)
            zb = zb + jnp.where(idv == first + 1, z, 0)
        has = num(near(df, dc))
        nbr_has.append(has)
        nbr_z.append((jnp.where(has > 0, za, NONE), jnp.where(has > 0, zb, NONE)))

    with jax.named_scope("wait_solid"):
        all_of(T, in_sem.at[0]).wait()
        all_of(M, in_sem.at[1]).wait()
    for s in range(SB):
        m = M[s]
        k = jnp.full(wide, cond[0], F32)
        for i in range(1, 8):
            k = jnp.where(m == i, cond[i], k)
        KAP[s] = k
        zf = jnp.full((8, W), own_z[s]).astype(F32)
        t = T[s]
        XS[0, FB + s] = jnp.where(r8 > 4, t[8:], jnp.where(r8 == 4, zf, rroll(k[8:], 4)))
        XS[1, FB + s] = jnp.where(r8 < 3, t[:8], jnp.where(r8 == 3, zf, rroll(k[:8], 4)))
        YS[0, FB + s] = jnp.where(lh >= 64, t[:, H:], lroll(k[:, H:], 64))
        YS[1, FB + s] = jnp.where(lh < 64, t[:, :H], lroll(k[:, :H], 64))

    def pack_y(pieces, side):
        acc = None
        for g, v in enumerate(pieces):
            r = lroll(v, E * g - (H - E)) if side == 0 else lroll(v, E * g)
            acc = r if acc is None else jnp.where(group == g, r, acc)
        return acc

    def ahead(v, p, z):
        _, cy, cz = C[p]
        if cz:
            edge = z == 0 if cz > 0 else z == E - 1
            return jnp.where(edge, lroll(v, -(E - 1) * cz), lroll(v, cz))
        return lroll(v, E * cy)

    def two(v, first, second, z):
        return jnp.where((z == 0) | (z == E - 1), v, jnp.where(z < 8, first, second))

    with jax.named_scope("wait_pops"):
        all_of(G, in_sem.at[2]).wait()
        all_of(Q, in_sem.at[3]).wait()
    for b in range(FB):
        with jax.named_scope("collide"):
            for xh in range(2):
                for yh in range(2):
                    collide_tile(G, Q, b, pl.ds(8 * xh, 8), pl.ds(H * yh, H))
        for side in range(2):
            x = E - 1 if side == 0 else 0
            inner = E - 2 if side == 0 else 1

            def line(x_at, lo, n):
                zz = jnp.bitwise_and(lanes((1, n)), E - 1)
                up = Q[b, 6, x_at : x_at + 1, lo : lo + n]
                return jnp.where(zz < 8, up, Q[b, 5, x_at : x_at + 1, lo : lo + n])

            for r in range(5):
                FX[side, b, r : r + 1, :] = G[b, PX[side][r], x : x + 1, :]
            FX[side, b, HEAT : HEAT + 1, :] = Q[b, 1 + side, x : x + 1, :]
            z1w = jnp.bitwise_and(lanes((1, W)), E - 1)
            v = line(inner, 0, W)
            FX[side, b, EDGE_Z : EDGE_Z + 1, :] = two(
                line(x, 0, W), lroll(v, 1), lroll(v, -1), z1w
            )
            FX[side, b, CROSS : CROSS + 1, :H] = Q[b, 4, x : x + 1, :H]
            FX[side, b, CROSS : CROSS + 1, H:] = Q[b, 3, x : x + 1, H:]

            raw = FX[side, b]
            out = raw
            for r, p in enumerate(PX[side]):
                if r:
                    out = jnp.where(r8 == r, ahead(raw, p, z8), out)
            XS[side, b] = out

            half = pl.ds(H, H) if side == 0 else pl.ds(0, H)
            sgn = 1 if side == 0 else -1
            hz = jnp.where(zh < 8, Q[b, 6, :, half], Q[b, 5, :, half])
            hx = jnp.concatenate([Q[b, 2, 0:8, half], Q[b, 1, 8:16, half]], axis=0)
            raw = pack_y(
                [G[b, PY[side][r], :, half] for r in range(5)]
                + [
                    Q[b, 3 + side, :, half],
                    two(hz, lroll(hz, sgn * E + 1), lroll(hz, sgn * E - 1), zh),
                    hx,
                ],
                side,
            )
            FY[side, b] = raw
            out = raw
            for q, p in enumerate(PY[side]):
                cx = C[p][0]
                if q:
                    v = rroll(raw, cx) if cx else ahead(raw, p, zh)
                    out = jnp.where(group == q, v, out)
            YS[side, b] = out
            for i in range(4):
                cs, row, ch = CORNER_SRC[i]
                if cs != side:
                    continue
                sg = -1 if ch else 1
                hp = 3 if ch else 4
                lo = H * ch
                gg = jnp.right_shift(lanes((1, H)), 4)
                at = (lambda d: 7 - d) if ch else (lambda d: d)
                acc = Q[b, 1 + side, x : x + 1, lo : lo + H]
                extra = [
                    (2, line(x, lo, H)),
                    (7, G[b, PX[side][row], x : x + 1, lo : lo + H]),
                    (4, Q[b, hp, x : x + 1, lo : lo + H]),
                    (5, Q[b, hp, inner : inner + 1, lo : lo + H]),
                ]
                for d, v in extra:
                    acc = jnp.where(gg == at(d), lroll(v, sg * E * d), acc)
                CS[i, 0, b : b + 1, :] = acc

    for i in range(4):
        side, _, ch = CORNER_SRC[i]
        for s in range(SB):
            CS[i, 1 + s] = XS[side, FB + s, :, H * ch : H * ch + H]

    with jax.named_scope("entry_barrier"):
        pl.semaphore_wait(barrier, n_peers)
    for i, (df, dc) in enumerate(CORNERS):
        send(4 + i, CS.at[i], CR.at[i], df, dc)
    for i, (df, dc) in list(enumerate(SIDES))[::-1]:
        side = i % 2
        if i < 2:
            send(i, XS.at[side], XR.at[side], df, dc)
        else:
            send(i, YS.at[side], YR.at[side], df, dc)

    def stream(b):
        def main(ref, p):
            cx, cy, cz = C[p]
            s = E * cy + cz
            out = lroll(rroll(ref[b, p], cx), s)
            if cz:
                back = ref[b, OPP[p]]
                adj = (b - cz) % FB
                if ref is Q:
                    wid = wall[b, (6 if cz > 0 else 5) - 1]
                    tw = lroll(T[slot(wid, here, SB)], -(E - 1) * cz)
                    back = jnp.where(jnp.full(wide, wid) >= 0, 2.0 * tw - back, back)
                if 0 <= b - cz < FB:
                    other = lroll(rroll(ref[adj, p], cx), E * cy - (E - 1) * cz)
                    zid = nbr[b, (6 if cz > 0 else 5) - 1]
                    back = jnp.where(jnp.full(wide, zid) >= 0, other, back)
                edge = zw == 0 if cz > 0 else zw == E - 1
                out = jnp.where(edge, back, out)
            return out

        GO[b, 0] = G[b, 0]
        QO[b, 0] = Q[b, 0]
        for p in range(1, 19):
            GO[b, p] = main(G, p)
        for p in range(1, 7):
            QO[b, p] = main(Q, p)

    with jax.named_scope("stream"):
        for b in range(FB):
            stream(b)

    ext = (EX, EL)
    ze = jnp.bitwise_and(lanes(ext), E - 1)

    def piece(flag, v):
        return jnp.where(on(flag, v), v, 0.0)

    kmax = cond[0]
    for i in range(1, 8):
        kmax = jnp.maximum(kmax, cond[i])
    radius = jnp.full((8, H), kmax * 6.0, F32)
    center = radius + 1.0
    sigma = center / radius

    def grow(v):
        v = jnp.concatenate([v] * (EX // 8), axis=0)
        return jnp.concatenate([v] * (EL // H), axis=1)

    inv_center = grow(1.0 / center)
    rho0 = 1.0 / sigma
    rho1 = 1.0 / (2.0 * sigma - rho0)
    rho2 = 1.0 / (2.0 * sigma - rho1)
    coef = [
        (grow(rho1 * rho0), grow(2.0 * rho1 / radius)),
        (grow(rho2 * rho1), grow(2.0 * rho2 / radius)),
    ]


    with jax.named_scope("wait_y"):
        for i in (2, 3):
            received(i)

    def y_face(b, side):
        shape = (E, H)
        dc = -1 if side == 0 else 1
        dirn = 4 if side == 0 else 3
        bf = base_of(0, dc)
        main_id = nbr[b, dirn - 1]
        a = YR[side, slot(main_id, bf, FB)]
        val = a
        ids = jnp.full(shape, main_id)
        for r, p in enumerate(PY[side]):
            cx, _, cz = C[p]
            if r == 0:
                continue
            if cx:
                continue
            cid = nbr[b, OPP[p] - 1]
            edge = (group == r) & (zh == 0 if cz > 0 else zh == E - 1)
            val = jnp.where(edge, YR[side, slot(cid, bf, FB)], val)
            ids = jnp.where(edge, jnp.full(shape, cid), ids)
        fall = FY[1 - side, b]
        wid = wall[b, dirn - 1]
        tw = YR[side, FB + slot(wid, bf, SB)]
        tw = lroll(tw, -2 * E if side == 0 else HEAT * E)
        hot = (group == HEAT) & (jnp.full(shape, wid) >= 0)
        fall = jnp.where(hot, 2.0 * tw - fall, fall)
        return jnp.where(ids >= 0, val, fall)

    for b in range(FB):
        for side in range(2):
            yf = y_face(b, side)
            half = pl.ds(0, H) if side == 0 else pl.ds(H, H)
            edge = lh < E if side == 0 else lh >= H - E
            back = 0 if side == 0 else H - E
            for q, p in enumerate(PY[side]):
                v = lroll(yf, back - E * q)
                GO[b, p, :, half] = jnp.where(edge, v, GO[b, p, :, half])
            v = lroll(yf, back - E * HEAT)
            QO[b, 3 + side, :, half] = jnp.where(edge, v, QO[b, 3 + side, :, half])
    with jax.named_scope("wait_x"):
        for i in (0, 1, 4, 5, 6, 7):
            received(i)

    def corner_z(i):
        side = CORNER_SRC[i][0]
        r = 4 if side == 0 else 3
        return [
            jnp.broadcast_to(CR[i, 1 + s, r : r + 1, :], (8, H))
            for s in range(SB)
        ]

    quad = [[2, 3], [1, 0]]
    chas = [jnp.full((8, H), num(near(-df, -dc))) > 0 for df, dc in CORNERS]
    cz = [[jnp.where(chas[i], v, float(NONE)) for v in corner_z(i)] for i in range(4)]

    def quadrants(fn):
        up = jnp.where(g8 < 4, fn(quad[0][0]), fn(quad[0][1]))
        down = jnp.where(g8 < 4, fn(quad[1][0]), fn(quad[1][1]))
        return jnp.where(q8 < 4, up, down)

    def splat(shape, v):
        return jnp.full(shape, v).astype(F32)

    Z = []
    for s in range(SB):
        TE[s, 0:E, 0:W] = T[s]
        KE[s, 0:E, 0:W] = KAP[s]
        a = piece(nbr_has[0], XR[1, FB + s])
        c = piece(nbr_has[1], XR[0, FB + s])
        TE[s, E:EX, 0:W] = jnp.where(r8 < 4, a, c)
        KE[s, E:EX, 0:W] = rroll(jnp.where(r8 < 4, c, a), 4)
        zx = jnp.where(r8 < 4, splat((8, W), nbr_z[0][s]), splat((8, W), nbr_z[1][s]))
        a = piece(nbr_has[2], YR[1, FB + s])
        c = piece(nbr_has[3], YR[0, FB + s])
        TE[s, 0:E, W:EL] = jnp.where(group < 4, a, c)
        KE[s, 0:E, W:EL] = lroll(jnp.where(group < 4, c, a), 64)
        zy = jnp.where(group < 4, splat((E, H), nbr_z[2][s]), splat((E, H), nbr_z[3][s]))

        def corner_solid(i):
            return jnp.where(chas[i], CR[i, 1 + s], 0.0)

        TE[s, E:EX, W:EL] = quadrants(corner_solid)
        KE[s, E:EX, W:EL] = quadrants(lambda i: rroll(corner_solid(i), 4))
        top = jnp.concatenate([splat(wide, own_z[s]), zy], axis=1)
        low = jnp.concatenate([zx, quadrants(lambda i: cz[i][s])], axis=1)
        Z.append(jnp.concatenate([top, low], axis=0))

    def link(k, kb):
        total = jnp.maximum(k + kb, 0.05)
        inv = pl.reciprocal(total, approx=True)
        inv = inv * (2.0 - total * inv)
        inv = inv * (2.0 - total * inv)
        return (2.0 * k * kb) * inv

    def toward(k, v):
        return rroll(v, -1 if k == 0 else 1) if k < 2 else lroll(v, -E if k == 2 else E)

    wet = [[0.0, 0.0] for _ in range(SB)]
    for k in range(4):
        za, zb = toward(k, Z[0]), toward(k, Z[1])
        for s in range(SB):
            code = jnp.where(zb == Z[s], 1, jnp.where(za == Z[s], 0, 2))
            CODE[k, s] = code
            wet[s][k // 2] = jnp.where((code == 2) & (za >= 0.0), 1.0, wet[s][k // 2])
    adj = Z[1] == Z[0] + 1.0
    top, bottom = ze == E - 1, ze == 0
    wet_z = [
        (top & (~adj) & (Z[0] < NZ - 1.0) & (Z[0] >= 0.0)) | (bottom & (Z[0] > 0.0)),
        (top & (Z[1] < NZ - 1.0) & (Z[1] >= 0.0)) | (bottom & (~adj) & (Z[1] >= 0.0)),
    ]
    for s in range(SB):
        WX[s] = wet[s][0]
        WY[s] = wet[s][1]
        WZ[s] = jnp.where(wet_z[s], 1.0, 0.0)

    def chosen(k, s, v):
        code = CODE[k, s]
        return jnp.where(code == 1, v[1], jnp.where(code == 0, v[0], 0.0))

    def z_up(v):
        return [jnp.where(top, lroll(v[1], E - 1), lroll(v[0], -1)), lroll(v[1], -1)]

    def divergence(v):
        div = []
        for k, links in ((0, LX), (2, LY)):
            over = [toward(k, x) for x in v]
            f = [
                links[s] * (jnp.where(CODE[k, s] == 1, over[1], over[0]) - v[s])
                for s in range(SB)
            ]
            under = [toward(k + 1, x) for x in f]
            part = [f[s] - chosen(k + 1, s, under) for s in range(SB)]
            div = part if k == 0 else [a + b for a, b in zip(div, part)]
        up = z_up(v)
        f = [LZ[s] * (up[s] - v[s]) for s in range(SB)]
        under = [
            jnp.where(bottom, 0.0, lroll(f[0], 1)),
            jnp.where(bottom, lroll(f[0], 1 - E), lroll(f[1], 1)),
        ]
        return [div[s] + (f[s] - under[s]) for s in range(SB)]

    kk = [KE[s] for s in range(SB)]
    for k, links in ((0, LX), (2, LY)):
        over = [toward(k, x) for x in kk]
        for s in range(SB):
            links[s] = link(kk[s], chosen(k, s, over))
    up = z_up(kk)
    LZ[0] = link(kk[0], jnp.where(top & ~adj, 0.0, up[0]))
    LZ[1] = link(kk[1], jnp.where(top, 0.0, up[1]))
    tt = [TE[s] for s in range(SB)]
    div = divergence(tt)
    for s in range(SB):
        R[s] = div[s] - (WX[s] + WY[s] + WZ[s]) * tt[s]

    def corner_rows(i):
        return [jnp.broadcast_to(CR[i, 0, j : j + 1, :], (8, H)) for j in range(FB)]

    def corner_heat(i, z):
        f = z - jnp.where(cz[i][0] < z, 1.0, 0.0) - jnp.where(cz[i][1] < z, 1.0, 0.0)
        a, b, c = corner_rows(i)
        return jnp.where(f < 0.5, a, jnp.where(f < 1.5, b, c))

    def of_three(za, zb, z, fn):
        f = z - jnp.where(za < z, 1.0, 0.0) - jnp.where(zb < z, 1.0, 0.0)
        return jnp.where(f < 0.5, fn(0), jnp.where(f < 1.5, fn(1), fn(2)))

    row_edge = (q8 == 0) | (q8 == 7)
    wide_edge = (r8 == 0) | (r8 == 7)

    def stack(v):
        return jnp.concatenate([v, v], axis=0)

    for s in range(SB):
        oz = own_z[s]
        nz = [nbr_z[k][s] for k in range(4)]
        ozf = splat((8, H), oz)
        nzf = [splat((8, H), z) for z in nz]
        f_side = [fluid_slot(nbr_z[k][0], nbr_z[k][1], oz) for k in range(4)]
        f_own = [fluid_slot(z0, z1, nz[k]) for k in range(4)]

        own_lo = jnp.broadcast_to(XR[0, f_side[1], HEAT : HEAT + 1, :], (8, W))
        own_hi = jnp.broadcast_to(XR[1, f_side[0], HEAT : HEAT + 1, :], (8, W))
        x_tile = jnp.where(
            r8 < 4,
            jnp.broadcast_to(Q[f_own[0], 1, E - 1 : E, :], (8, W)),
            jnp.broadcast_to(Q[f_own[1], 2, 0:1, :], (8, W)),
        )
        y_lo = jnp.where(g8 < 4, corner_heat(1, nzf[2]), corner_heat(0, nzf[3]))
        y_hi = jnp.where(g8 < 4, corner_heat(2, nzf[2]), corner_heat(3, nzf[3]))

        def from_y(i):
            half = CORNER_SRC[i][2]
            k = 3 if half else 2
            row = 0 if i < 2 else E - 1
            v = of_three(
                nbr_z[k][0],
                nbr_z[k][1],
                cz[i][s],
                lambda j: jnp.broadcast_to(YR[1 - half, j, row : row + 1, :], (8, H))
                if not half
                else jnp.broadcast_to(YR[0, j, row : row + 1, :], (8, H)),
            )
            return v if half else lroll(v, E)

        heat = jnp.concatenate(
            [
                jnp.concatenate([own_lo, y_lo], axis=1),
                jnp.concatenate([own_hi, y_hi], axis=1),
                jnp.concatenate([x_tile, quadrants(from_y)], axis=1),
            ],
            axis=0,
        )
        acc = R[s] + jnp.where(WX[s] > 0.5, heat, 0.0)

        left = lroll(YR[0, f_side[3]], -5 * E)
        right = lroll(YR[1, f_side[2]], 2 * E)

        def from_corner(i, z):
            v = corner_heat(i, z)
            if CORNER_SRC[i][2]:
                return jnp.where(row_edge, lroll(v, -3 * E), lroll(v, -2 * E))
            return jnp.where(row_edge, lroll(v, 3 * E), lroll(v, 2 * E))

        x_left = jnp.where(q8 < 4, from_corner(3, nzf[0]), from_corner(0, nzf[1]))
        x_right = jnp.where(q8 < 4, from_corner(2, nzf[0]), from_corner(1, nzf[1]))
        y_tile = jnp.where(
            group < 4,
            lroll(Q[f_own[2], 3, :, H:W], E),
            lroll(Q[f_own[3], 4, :, 0:H], -E),
        )

        def from_x(i):
            half = CORNER_SRC[i][2]
            k = 1 if i < 2 else 0
            lo = 0 if half else H
            v = of_three(
                nbr_z[k][0],
                nbr_z[k][1],
                cz[i][s],
                lambda j: jnp.broadcast_to(
                    XR[1 - k, j, CROSS : CROSS + 1, lo : lo + H], (8, H)
                ),
            )
            return lroll(v, -E if half else E)

        heat = jnp.concatenate(
            [
                jnp.concatenate([left, right, y_tile], axis=1),
                jnp.concatenate([x_left, x_right, quadrants(from_x)], axis=1),
            ],
            axis=0,
        )
        acc = acc + jnp.where(WY[s] > 0.5, heat, 0.0)

        def updown(k):
            za, zb = nbr_z[k]
            return fluid_slot(za, zb, nz[k] + 1), fluid_slot(za, zb, nz[k] - 1)

        tile = jnp.where(
            zw < 8,
            lroll(Q[fluid_slot(z0, z1, oz - 1), 5], 1 - E),
            lroll(Q[fluid_slot(z0, z1, oz + 1), 6], E - 1),
        )
        a, c = [], []
        for k in range(2):
            u, d = updown(k)
            a.append(jnp.broadcast_to(XR[1 - k, u, EDGE_Z : EDGE_Z + 1, :], (8, W)))
            c.append(jnp.broadcast_to(XR[1 - k, d, EDGE_Z : EDGE_Z + 1, :], (8, W)))
        a = jnp.where(r8 < 4, a[0], a[1])
        c = jnp.where(r8 < 4, c[0], c[1])
        x_tile = jnp.where(
            z8 < 8,
            jnp.where(wide_edge, lroll(c, 1 - E), lroll(c, 2 - E)),
            jnp.where(wide_edge, lroll(a, E - 1), lroll(a, E - 2)),
        )
        u, d = updown(2)
        a, c = YR[1, u], YR[1, d]
        y_up = jnp.where(
            zh < 8,
            jnp.where(group == 0, lroll(c, -7 * E + 1), lroll(c, -6 * E + 2)),
            jnp.where(group == 0, lroll(a, -5 * E - 1), lroll(a, -4 * E - 2)),
        )
        u, d = updown(3)
        a, c = YR[0, u], YR[0, d]
        y_down = jnp.where(
            zh < 8,
            jnp.where(group == 7, lroll(c, 1), lroll(c, 2 - E)),
            jnp.where(group == 7, lroll(a, 2 * E - 1), lroll(a, E - 2)),
        )

        def from_z(i):
            shift = 2 * E if CORNER_SRC[i][2] else -2 * E
            a = lroll(corner_heat(i, cz[i][s] + 1.0), shift + E - 1)
            c = lroll(corner_heat(i, cz[i][s] - 1.0), shift + 1 - E)
            return jnp.where(z8[:, :H] < 8, c, a)

        heat = jnp.concatenate(
            [
                jnp.concatenate([tile, jnp.where(group < 4, y_up, y_down)], axis=1),
                jnp.concatenate([x_tile, quadrants(from_z)], axis=1),
            ],
            axis=0,
        )
        R[s] = acc + jnp.where(WZ[s] > 0.5, heat, 0.0)

    upd = []
    sol = []
    for s in range(SB):
        d = R[s] * inv_center
        upd.append(d)
        sol.append(T[s] + d[0:E, 0:W])
    div = divergence(upd)
    for s in range(SB):
        r = R[s] - (upd[s] - div[s])
        R[s] = r
        upd[s] = coef[0][0] * upd[s] + coef[0][1] * r
        sol[s] = sol[s] + upd[s][0:E, 0:W]

    v = [x[:, 0:W] for x in upd]
    over = [rroll(x, -1) for x in v]
    f = [
        LX[s, :, 0:W] * (jnp.where(CODE[0, s, :, 0:W] == 1, over[1], over[0]) - v[s])
        for s in range(SB)
    ]
    under = [rroll(x, 1)[0:E] for x in f]
    code = [CODE[1, s, 0:E, 0:W] for s in range(SB)]
    div = []
    for s in range(SB):
        u = jnp.where(code[s] == 1, under[1], jnp.where(code[s] == 0, under[0], 0.0))
        div.append(f[s][0:E] - u)
    v = [x[0:E] for x in upd]
    over = [lroll(x, -E) for x in v]
    f = [
        LY[s, 0:E] * (jnp.where(CODE[2, s, 0:E] == 1, over[1], over[0]) - v[s])
        for s in range(SB)
    ]
    under = [lroll(x, E)[:, 0:W] for x in f]
    code = [CODE[3, s, 0:E, 0:W] for s in range(SB)]
    for s in range(SB):
        u = jnp.where(code[s] == 1, under[1], jnp.where(code[s] == 0, under[0], 0.0))
        div[s] = div[s] + (f[s][:, 0:W] - u)
    v = [x[0:E, 0:W] for x in upd]
    last, first = zw == E - 1, zw == 0
    up = [jnp.where(last, lroll(v[1], E - 1), lroll(v[0], -1)), lroll(v[1], -1)]
    f = [LZ[s, 0:E, 0:W] * (up[s] - v[s]) for s in range(SB)]
    under = [
        jnp.where(first, 0.0, lroll(f[0], 1)),
        jnp.where(first, lroll(f[0], 1 - E), lroll(f[1], 1)),
    ]
    for s in range(SB):
        r = R[s, 0:E, 0:W] - (v[s] - div[s] - (f[s] - under[s]))
        TO[s] = sol[s] + (coef[1][0][0:E, 0:W] * v[s] + coef[1][1][0:E, 0:W] * r)

    def x_face(b, side):
        shape = (8, W)
        df = -1 if side == 0 else 1
        dirn = 2 if side == 0 else 1
        bf = base_of(df, 0)
        main_id = nbr[b, dirn - 1]
        a = XR[side, slot(main_id, bf, FB)]
        val = a
        ids = jnp.full(shape, main_id)
        for r, p in enumerate(PX[side]):
            _, cy, cz = C[p]
            if r == 0:
                continue
            cid = nbr[b, OPP[p] - 1]
            if cy:
                which = jnp.full((8, H), slot(cid, base_of(df, -cy), FB))
                first, second, third = corner_rows(CORNER_OF[p])
                corner = jnp.where(which == 1, second, first)
                corner = jnp.where(which == 2, third, corner)
                corner = jnp.concatenate([corner, corner], axis=1)
                edge = l8 < E if cy > 0 else l8 >= W - E
                cand = jnp.where(edge, corner, a)
            else:
                edge = z8 == 0 if cz > 0 else z8 == E - 1
                cand = jnp.where(edge, XR[side, slot(cid, bf, FB)], a)
            val = jnp.where(r8 == r, cand, val)
            ids = jnp.where((r8 == r) & edge, jnp.full(shape, cid), ids)
        fall = FX[1 - side, b]
        wid = wall[b, dirn - 1]
        row = 7 if side == 0 else 0
        tw = XR[side, FB + slot(wid, bf, SB), row : row + 1, :]
        hot = (r8 == HEAT) & (jnp.full(shape, wid) >= 0)
        fall = jnp.where(hot, 2.0 * tw - fall, fall)
        return jnp.where(ids >= 0, val, fall)

    for b in range(FB):
        for side in range(2):
            xf = x_face(b, side)
            x = 0 if side == 0 else E - 1
            for r, p in enumerate(PX[side]):
                GO[b, p, x : x + 1, :] = xf[r : r + 1]
            QO[b, 1 + side, x : x + 1, :] = xf[HEAT : HEAT + 1]

    for i in range(N_COPY):

        @pl.when(near(*steps[i]))
        def _():
            copies[i].wait_send()


def store_kernel(fluid, heat, solid, fluid_out, heat_out, solid_out, sem):
    pairs = [(fluid, fluid_out), (heat, heat_out), (solid, solid_out)]
    for i, (src, dst) in enumerate(pairs):
        for x in range(E):
            pltpu.make_async_copy(
                src.at[..., x, :], dst.at[..., pl.ds(W * x, W)], sem.at[i]
            ).start()
    for i, (src, dst) in enumerate(pairs):
        pltpu.make_async_copy(src, src, sem.at[i]).wait()


def body(nf, nc, fluid_pop, heat_pop, solid_temp, material, cond, nbr, wall, snbr, sflu):
    hbm = pl.BlockSpec(memory_space=pltpu.HBM)

    def vm(*shape):
        return pltpu.VMEM(shape, F32)

    vmem = pl.BlockSpec(memory_space=pltpu.VMEM)
    fields = pl.pallas_call(
        functools.partial(kernel, nf, nc),
        out_shape=(
            vm(FB, 19, E, W),
            vm(FB, 7, E, W),
            vm(SB, E, W),
        ),
        in_specs=[hbm] * 9,
        out_specs=(vmem, vmem, vmem),
        scratch_shapes=[
            vm(FB, 19, E, W),
            vm(FB, 7, E, W),
            vm(SB, E, W),
            pltpu.VMEM((SB, E, W), jnp.int32),
            vm(SB, E, W),
            vm(2, FB, 8, W),
            vm(2, FB, E, H),
            vm(2, FB + SB, 8, W),
            vm(2, FB + SB, 8, W),
            vm(2, FB + SB, E, H),
            vm(2, FB + SB, E, H),
            vm(4, 1 + SB, 8, H),
            vm(4, 1 + SB, 8, H),
        ]
        + [vm(SB, EX, EL)] * 9
        + [
            pltpu.VMEM((4, SB, EX, EL), jnp.int32),
            pltpu.SMEM(cond.shape, F32),
            pltpu.SMEM(nbr.shape, jnp.int32),
            pltpu.SMEM(wall.shape, jnp.int32),
            pltpu.SMEM(snbr.shape, jnp.int32),
            pltpu.SMEM(sflu.shape, jnp.int32),
            pltpu.SemaphoreType.DMA((9,)),
            pltpu.SemaphoreType.DMA((N_COPY,)),
            pltpu.SemaphoreType.DMA((N_COPY,)),
        ],
        compiler_params=pltpu.CompilerParams(
            collective_id=0, has_side_effects=True, vmem_limit_bytes=LIMIT
        ),
    )(fluid_pop, heat_pop, solid_temp, material, cond, nbr, wall, snbr, sflu)
    return pl.pallas_call(
        store_kernel,
        out_shape=(
            jax.ShapeDtypeStruct(fluid_pop.shape, F32),
            jax.ShapeDtypeStruct(heat_pop.shape, F32),
            jax.ShapeDtypeStruct(solid_temp.shape, F32),
        ),
        in_specs=[pl.BlockSpec(memory_space=pl.ANY)] * 3,
        out_specs=(hbm, hbm, hbm),
        scratch_shapes=[pltpu.SemaphoreType.DMA((3,))],
        compiler_params=pltpu.CompilerParams(vmem_limit_bytes=8 * 1024 * 1024),
    )(*fields)


def solution(mesh):
    both = ("flow", "cross")
    in_specs = (
        P(both, None, None),
        P(both, None, None),
        P(both, None),
        P(both, None),
        P(),
        P(both, None),
        P(both, None),
        P(both, None),
        P(both, None),
    )
    out_specs = (P(both, None, None), P(both, None, None), P(both, None))
    return jax.shard_map(
        functools.partial(body, mesh.shape["flow"], mesh.shape["cross"]),
        mesh=mesh,
        in_specs=in_specs,
        out_specs=out_specs,
        check_vma=False,
    )
```

```python
import functools

import jax
import jax.numpy as jnp
from jax import lax
from jax.experimental import pallas as pl
from jax.experimental.pallas import tpu as pltpu
from jax.sharding import PartitionSpec as P

MESH = pl.DeviceIdType.MESH
F32 = jnp.float32
E = 16
W = 256
H = 128
FB = 3
SB = 2
C = [
    (0, 0, 0),
    (1, 0, 0),
    (-1, 0, 0),
    (0, 1, 0),
    (0, -1, 0),
    (0, 0, 1),
    (0, 0, -1),
    (1, 1, 0),
    (-1, -1, 0),
    (1, -1, 0),
    (-1, 1, 0),
    (1, 0, 1),
    (-1, 0, -1),
    (1, 0, -1),
    (-1, 0, 1),
    (0, 1, 1),
    (0, -1, -1),
    (0, 1, -1),
    (0, -1, 1),
]
OPP = [0, 2, 1, 4, 3, 6, 5, 8, 7, 10, 9, 12, 11, 14, 13, 16, 15, 18, 17]
PX = ([1, 7, 9, 11, 13], [2, 8, 10, 12, 14])
PY = ([3, 7, 10, 15, 17], [4, 8, 9, 16, 18])
HEAT = 5
SIDES = [(1, 0), (-1, 0), (0, 1), (0, -1)]
CORNERS = [(1, 1), (1, -1), (-1, -1), (-1, 1)]
PEERS = CORNERS + SIDES
CORNER_SRC = [(0, 1, 1), (0, 2, 0), (1, 1, 0), (1, 2, 1)]
CORNER_OF = {7: 0, 9: 1, 8: 2, 10: 3}
EDGE_Z = 6
CROSS = 7
N_COPY = 8
NZ = 5
NONE = -9
EX = 24
EL = 384
LIMIT = 60 * 1024 * 1024


def lroll(v, s):
    n = v.shape[1]
    s = s % n
    return v if s == 0 else pltpu.roll(v, s, axis=1)


def rroll(v, s):
    n = v.shape[0]
    s = s % n
    return v if s == 0 else pltpu.roll(v, s, axis=0)


def lanes(shape):
    return lax.broadcasted_iota(jnp.int32, shape, 1)


def rows(shape):
    return lax.broadcasted_iota(jnp.int32, shape, 0)


def collide_tile(G, Q, b, rs, ls):
    def ld(p):
        return G[b, p, rs, ls]

    f = [ld(p) for p in range(19)]
    w = [v * (1.0 / 3.0 if p == 0 else 1.0 / 18.0 if p < 7 else 1.0 / 36.0) for p, v in enumerate(f)]
    d = [None] * 19
    for p in (1, 3, 5, 7, 9, 11, 13, 15, 17):
        d[p] = w[p] - w[p + 1]
    s1 = ((w[1] + w[2]) + (w[3] + w[4])) + (w[5] + w[6])
    s2 = (((w[7] + w[8]) + (w[9] + w[10])) + ((w[11] + w[12]) + (w[13] + w[14]))) + (
        (w[15] + w[16]) + (w[17] + w[18])
    )
    rho = (w[0] + s1) + s2
    jx = d[1] + ((d[7] + d[9]) + (d[11] + d[13]))
    jy = d[3] + ((d[7] - d[9]) + (d[15] + d[17]))
    jz = d[5] + ((d[11] - d[13]) + (d[15] - d[17]))
    inv = 1.0 / rho
    u = (jx * inv, jy * inv, jz * inv)
    j = (jx, jy, jz)
    base = 1.25 * rho - 1.875 * (jx * u[0] + jy * u[1] + jz * u[2])
    G[b, 0, rs, ls] = base - 0.25 * f[0]
    cus = {}
    for p in (1, 3, 5, 7, 9, 11, 13, 15, 17):
        cj = None
        cu = None
        for a in range(3):
            s = C[p][a]
            if s == 0:
                continue
            if cj is None:
                cj, cu = j[a], u[a]
            elif s > 0:
                cj, cu = cj + j[a], cu + u[a]
            else:
                cj, cu = cj - j[a], cu - u[a]
        even = base + 5.625 * (cj * cu)
        odd = 3.75 * cj
        G[b, p, rs, ls] = (even + odd) - 0.25 * f[p]
        G[b, p + 1, rs, ls] = (even - odd) - 0.25 * f[p + 1]
        cus[p] = cu
    h = [Q[b, k, rs, ls] for k in range(7)]
    g = [v * (0.25 if k == 0 else 0.125) for k, v in enumerate(h)]
    gs = ((g[1] + g[2]) + (g[3] + g[4])) + (g[5] + g[6])
    t11 = (g[0] + gs) * 1.1
    t44 = 4.0 * t11
    Q[b, 0, rs, ls] = t11 - 0.1 * h[0]
    for k in (1, 3, 5):
        o = t44 * cus[k]
        Q[b, k, rs, ls] = (t11 + o) - 0.1 * h[k]
        Q[b, k + 1, rs, ls] = (t11 - o) - 0.1 * h[k + 1]


def kernel(
    nf,
    nc,
    fluid_in,
    heat_in,
    temp_in,
    mat_in,
    cond_in,
    nbr_in,
    wall_in,
    snbr_in,
    sflu_in,
    GO,
    QO,
    TO,
    G,
    Q,
    T,
    M,
    KAP,
    FX,
    FY,
    XS,
    XR,
    YS,
    YR,
    CS,
    CR,
    TE,
    KE,
    WX,
    WY,
    WZ,
    LX,
    LY,
    LZ,
    R,
    CODE,
    cond,
    nbr,
    wall,
    snbr,
    sflu,
    in_sem,
    send_sem,
    recv_sem,
):
    fl = lax.axis_index("flow")
    cr = lax.axis_index("cross")
    inside = {-1: (fl > 0, cr > 0), 0: (True, True), 1: (fl < nf - 1, cr < nc - 1)}

    def near(df, dc):
        a, b = inside[df][0], inside[dc][1]
        if df == 0:
            return b
        return a if dc == 0 else jnp.logical_and(a, b)

    barrier = pltpu.get_barrier_semaphore()
    for df, dc in PEERS:

        @pl.when(near(df, dc))
        def _():
            pl.semaphore_signal(
                barrier, inc=1, device_id=(fl + df, cr + dc), device_id_type=MESH
            )

    nx = 2 - (fl == 0).astype(jnp.int32) - (fl == nf - 1).astype(jnp.int32)
    ny = 2 - (cr == 0).astype(jnp.int32) - (cr == nc - 1).astype(jnp.int32)
    n_peers = nx + ny + nx * ny

    def load(src, dst, sem):
        for x in range(E):
            pltpu.make_async_copy(
                src.at[..., pl.ds(W * x, W)], dst.at[..., x, :], sem
            ).start()

    def all_of(ref, sem):
        return pltpu.make_async_copy(ref, ref, sem)

    tables = [
        (cond_in, cond, 4),
        (nbr_in, nbr, 5),
        (wall_in, wall, 6),
        (snbr_in, snbr, 7),
        (sflu_in, sflu, 8),
    ]
    tables = [pltpu.make_async_copy(a, b, in_sem.at[i]) for a, b, i in tables]
    for c in tables:
        c.start()
    load(temp_in, T, in_sem.at[0])
    load(mat_in, M, in_sem.at[1])
    load(fluid_in, G, in_sem.at[2])
    load(heat_in, Q, in_sem.at[3])

    copies = {}
    steps = {}

    def send(i, src, dst, df, dc):
        copies[i] = pltpu.make_async_remote_copy(
            src_ref=src,
            dst_ref=dst,
            send_sem=send_sem.at[i],
            recv_sem=recv_sem.at[i],
            device_id=(fl + df, cr + dc),
            device_id_type=MESH,
        )
        steps[i] = (df, dc)

        @pl.when(near(df, dc))
        def _():
            copies[i].start()

    def received(i):
        @pl.when(near(-steps[i][0], -steps[i][1]))
        def _():
            copies[i].wait_recv()

    wide = (E, W)
    lw = lanes(wide)
    zw = jnp.bitwise_and(lw, E - 1)
    lh = lanes((E, H))
    zh = jnp.bitwise_and(lh, E - 1)
    group = jnp.right_shift(lh, 4)
    r8 = rows((8, W))
    l8 = lanes((8, W))
    z8 = jnp.bitwise_and(l8, E - 1)
    q8 = rows((8, H))
    g8 = jnp.right_shift(lanes((8, H)), 4)

    def base_of(df, dc):
        return (fl + df) * nc + (cr + dc)

    def slot(idv, base, n):
        return jnp.clip(idv - base * n, 0, n - 1)

    def num(flag):
        return jnp.where(flag, 1, 0)

    def on(flag, like):
        return jnp.full(like.shape, flag) > 0

    for c in tables:
        c.wait()

    here = base_of(0, 0)
    below0 = sflu[0, 5]
    below1 = sflu[1, 5]
    z0 = jnp.where(below0 >= 0, slot(below0, here, FB) + 1, 0)
    z1 = jnp.where(below1 >= 0, slot(below1, here, FB) + 2, z0 + 1)
    own_z = (z0, z1)
    flu_z = [b + num(b >= z0) + num(b + 1 >= z1) for b in range(FB)]

    def fluid_slot(za, zb, z):
        return jnp.clip(z - num(za < z) - num(zb < z), 0, FB - 1)

    nbr_z = []
    nbr_has = []
    for k in range(4):
        df, dc = C[k + 1][0], C[k + 1][1]
        first = base_of(df, dc) * SB
        za = zb = 0
        pairs = [(wall[b, k], flu_z[b]) for b in range(FB)]
        pairs += [(snbr[s, k], own_z[s]) for s in range(SB)]
        for idv, z in pairs:
            za = za + jnp.where(idv == first, z, 0)
            zb = zb + jnp.where(idv == first + 1, z, 0)
        has = num(near(df, dc))
        nbr_has.append(has)
        nbr_z.append((jnp.where(has > 0, za, NONE), jnp.where(has > 0, zb, NONE)))

    all_of(T, in_sem.at[0]).wait()
    all_of(M, in_sem.at[1]).wait()
    for s in range(SB):
        m = M[s]
        k = jnp.full(wide, cond[0], F32)
        for i in range(1, 8):
            k = jnp.where(m == i, cond[i], k)
        KAP[s] = k
        zf = jnp.full((8, W), own_z[s]).astype(F32)
        t = T[s]
        XS[0, FB + s] = jnp.where(r8 > 4, t[8:], jnp.where(r8 == 4, zf, rroll(k[8:], 4)))
        XS[1, FB + s] = jnp.where(r8 < 3, t[:8], jnp.where(r8 == 3, zf, rroll(k[:8], 4)))
        YS[0, FB + s] = jnp.where(lh >= 64, t[:, H:], lroll(k[:, H:], 64))
        YS[1, FB + s] = jnp.where(lh < 64, t[:, :H], lroll(k[:, :H], 64))

    def pack_y(pieces, side):
        acc = None
        for g, v in enumerate(pieces):
            r = lroll(v, E * g - (H - E)) if side == 0 else lroll(v, E * g)
            acc = r if acc is None else jnp.where(group == g, r, acc)
        return acc

    def ahead(v, p, z):
        _, cy, cz = C[p]
        if cz:
            edge = z == 0 if cz > 0 else z == E - 1
            return jnp.where(edge, lroll(v, -(E - 1) * cz), lroll(v, cz))
        return lroll(v, E * cy)

    def two(v, first, second, z):
        return jnp.where((z == 0) | (z == E - 1), v, jnp.where(z < 8, first, second))

    all_of(G, in_sem.at[2]).wait()
    all_of(Q, in_sem.at[3]).wait()
    for b in range(FB):
        for xh in range(2):
            for yh in range(2):
                collide_tile(G, Q, b, pl.ds(8 * xh, 8), pl.ds(H * yh, H))
        for side in range(2):
            x = E - 1 if side == 0 else 0
            inner = E - 2 if side == 0 else 1

            def line(x_at, lo, n):
                zz = jnp.bitwise_and(lanes((1, n)), E - 1)
                up = Q[b, 6, x_at : x_at + 1, lo : lo + n]
                return jnp.where(zz < 8, up, Q[b, 5, x_at : x_at + 1, lo : lo + n])

            for r in range(5):
                FX[side, b, r : r + 1, :] = G[b, PX[side][r], x : x + 1, :]
            FX[side, b, HEAT : HEAT + 1, :] = Q[b, 1 + side, x : x + 1, :]
            z1w = jnp.bitwise_and(lanes((1, W)), E - 1)
            v = line(inner, 0, W)
            FX[side, b, EDGE_Z : EDGE_Z + 1, :] = two(
                line(x, 0, W), lroll(v, 1), lroll(v, -1), z1w
            )
            FX[side, b, CROSS : CROSS + 1, :H] = Q[b, 4, x : x + 1, :H]
            FX[side, b, CROSS : CROSS + 1, H:] = Q[b, 3, x : x + 1, H:]

            raw = FX[side, b]
            out = raw
            for r, p in enumerate(PX[side]):
                if r:
                    out = jnp.where(r8 == r, ahead(raw, p, z8), out)
            XS[side, b] = out

            half = pl.ds(H, H) if side == 0 else pl.ds(0, H)
            sgn = 1 if side == 0 else -1
            hz = jnp.where(zh < 8, Q[b, 6, :, half], Q[b, 5, :, half])
            hx = jnp.concatenate([Q[b, 2, 0:8, half], Q[b, 1, 8:16, half]], axis=0)
            raw = pack_y(
                [G[b, PY[side][r], :, half] for r in range(5)]
                + [
                    Q[b, 3 + side, :, half],
                    two(hz, lroll(hz, sgn * E + 1), lroll(hz, sgn * E - 1), zh),
                    hx,
                ],
                side,
            )
            FY[side, b] = raw
            out = raw
            for q, p in enumerate(PY[side]):
                cx = C[p][0]
                if q:
                    v = rroll(raw, cx) if cx else ahead(raw, p, zh)
                    out = jnp.where(group == q, v, out)
            YS[side, b] = out
            for i in range(4):
                cs, row, ch = CORNER_SRC[i]
                if cs != side:
                    continue
                sg = -1 if ch else 1
                hp = 3 if ch else 4
                lo = H * ch
                gg = jnp.right_shift(lanes((1, H)), 4)
                at = (lambda d: 7 - d) if ch else (lambda d: d)
                acc = Q[b, 1 + side, x : x + 1, lo : lo + H]
                extra = [
                    (2, line(x, lo, H)),
                    (7, G[b, PX[side][row], x : x + 1, lo : lo + H]),
                    (4, Q[b, hp, x : x + 1, lo : lo + H]),
                    (5, Q[b, hp, inner : inner + 1, lo : lo + H]),
                ]
                for d, v in extra:
                    acc = jnp.where(gg == at(d), lroll(v, sg * E * d), acc)
                CS[i, 0, b : b + 1, :] = acc

    for i in range(4):
        side, _, ch = CORNER_SRC[i]
        for s in range(SB):
            CS[i, 1 + s] = XS[side, FB + s, :, H * ch : H * ch + H]

    pl.semaphore_wait(barrier, n_peers)
    for i, (df, dc) in enumerate(CORNERS):
        send(4 + i, CS.at[i], CR.at[i], df, dc)
    for i, (df, dc) in list(enumerate(SIDES))[::-1]:
        side = i % 2
        if i < 2:
            send(i, XS.at[side], XR.at[side], df, dc)
        else:
            send(i, YS.at[side], YR.at[side], df, dc)

    def stream(b):
        def main(ref, p):
            cx, cy, cz = C[p]
            s = E * cy + cz
            out = lroll(rroll(ref[b, p], cx), s)
            if cz:
                back = ref[b, OPP[p]]
                adj = (b - cz) % FB
                if ref is Q:
                    wid = wall[b, (6 if cz > 0 else 5) - 1]
                    tw = lroll(T[slot(wid, here, SB)], -(E - 1) * cz)
                    back = jnp.where(jnp.full(wide, wid) >= 0, 2.0 * tw - back, back)
                if 0 <= b - cz < FB:
                    other = lroll(rroll(ref[adj, p], cx), E * cy - (E - 1) * cz)
                    zid = nbr[b, (6 if cz > 0 else 5) - 1]
                    back = jnp.where(jnp.full(wide, zid) >= 0, other, back)
                edge = zw == 0 if cz > 0 else zw == E - 1
                out = jnp.where(edge, back, out)
            return out

        GO[b, 0] = G[b, 0]
        QO[b, 0] = Q[b, 0]
        for p in range(1, 19):
            GO[b, p] = main(G, p)
        for p in range(1, 7):
            QO[b, p] = main(Q, p)

    for b in range(FB):
        stream(b)

    ext = (EX, EL)
    ze = jnp.bitwise_and(lanes(ext), E - 1)

    def piece(flag, v):
        return jnp.where(on(flag, v), v, 0.0)

    for i in (2, 3):
        received(i)

    def y_face(b, side):
        shape = (E, H)
        dc = -1 if side == 0 else 1
        dirn = 4 if side == 0 else 3
        bf = base_of(0, dc)
        main_id = nbr[b, dirn - 1]
        a = YR[side, slot(main_id, bf, FB)]
        val = a
        ids = jnp.full(shape, main_id)
        for r, p in enumerate(PY[side]):
            cx, _, cz = C[p]
            if r == 0:
                continue
            if cx:
                continue
            cid = nbr[b, OPP[p] - 1]
            edge = (group == r) & (zh == 0 if cz > 0 else zh == E - 1)
            val = jnp.where(edge, YR[side, slot(cid, bf, FB)], val)
            ids = jnp.where(edge, jnp.full(shape, cid), ids)
        fall = FY[1 - side, b]
        wid = wall[b, dirn - 1]
        tw = YR[side, FB + slot(wid, bf, SB)]
        tw = lroll(tw, -2 * E if side == 0 else HEAT * E)
        hot = (group == HEAT) & (jnp.full(shape, wid) >= 0)
        fall = jnp.where(hot, 2.0 * tw - fall, fall)
        return jnp.where(ids >= 0, val, fall)

    for b in range(FB):
        for side in range(2):
            yf = y_face(b, side)
            half = pl.ds(0, H) if side == 0 else pl.ds(H, H)
            edge = lh < E if side == 0 else lh >= H - E
            back = 0 if side == 0 else H - E
            for q, p in enumerate(PY[side]):
                v = lroll(yf, back - E * q)
                GO[b, p, :, half] = jnp.where(edge, v, GO[b, p, :, half])
            v = lroll(yf, back - E * HEAT)
            QO[b, 3 + side, :, half] = jnp.where(edge, v, QO[b, 3 + side, :, half])
    for i in (0, 1, 4, 5, 6, 7):
        received(i)

    def corner_z(i):
        side = CORNER_SRC[i][0]
        r = 4 if side == 0 else 3
        return [
            jnp.broadcast_to(CR[i, 1 + s, r : r + 1, :], (8, H))
            for s in range(SB)
        ]

    quad = [[2, 3], [1, 0]]
    chas = [jnp.full((8, H), num(near(-df, -dc))) > 0 for df, dc in CORNERS]
    cz = [[jnp.where(chas[i], v, float(NONE)) for v in corner_z(i)] for i in range(4)]

    def quadrants(fn):
        up = jnp.where(g8 < 4, fn(quad[0][0]), fn(quad[0][1]))
        down = jnp.where(g8 < 4, fn(quad[1][0]), fn(quad[1][1]))
        return jnp.where(q8 < 4, up, down)

    def splat(shape, v):
        return jnp.full(shape, v).astype(F32)

    Z = []
    for s in range(SB):
        TE[s, 0:E, 0:W] = T[s]
        KE[s, 0:E, 0:W] = KAP[s]
        a = piece(nbr_has[0], XR[1, FB + s])
        c = piece(nbr_has[1], XR[0, FB + s])
        TE[s, E:EX, 0:W] = jnp.where(r8 < 4, a, c)
        KE[s, E:EX, 0:W] = rroll(jnp.where(r8 < 4, c, a), 4)
        zx = jnp.where(r8 < 4, splat((8, W), nbr_z[0][s]), splat((8, W), nbr_z[1][s]))
        a = piece(nbr_has[2], YR[1, FB + s])
        c = piece(nbr_has[3], YR[0, FB + s])
        TE[s, 0:E, W:EL] = jnp.where(group < 4, a, c)
        KE[s, 0:E, W:EL] = lroll(jnp.where(group < 4, c, a), 64)
        zy = jnp.where(group < 4, splat((E, H), nbr_z[2][s]), splat((E, H), nbr_z[3][s]))

        def corner_solid(i):
            return jnp.where(chas[i], CR[i, 1 + s], 0.0)

        TE[s, E:EX, W:EL] = quadrants(corner_solid)
        KE[s, E:EX, W:EL] = quadrants(lambda i: rroll(corner_solid(i), 4))
        top = jnp.concatenate([splat(wide, own_z[s]), zy], axis=1)
        low = jnp.concatenate([zx, quadrants(lambda i: cz[i][s])], axis=1)
        Z.append(jnp.concatenate([top, low], axis=0))

    def link(k, kb):
        return (2.0 * k * kb) / jnp.maximum(k + kb, 0.05)

    def toward(k, v):
        return rroll(v, -1 if k == 0 else 1) if k < 2 else lroll(v, -E if k == 2 else E)

    wet = [[0.0, 0.0] for _ in range(SB)]
    for k in range(4):
        za, zb = toward(k, Z[0]), toward(k, Z[1])
        for s in range(SB):
            code = jnp.where(zb == Z[s], 1, jnp.where(za == Z[s], 0, 2))
            CODE[k, s] = code
            wet[s][k // 2] = jnp.where((code == 2) & (za >= 0.0), 1.0, wet[s][k // 2])
    adj = Z[1] == Z[0] + 1.0
    top, bottom = ze == E - 1, ze == 0
    wet_z = [
        (top & (~adj) & (Z[0] < NZ - 1.0) & (Z[0] >= 0.0)) | (bottom & (Z[0] > 0.0)),
        (top & (Z[1] < NZ - 1.0) & (Z[1] >= 0.0)) | (bottom & (~adj) & (Z[1] >= 0.0)),
    ]
    for s in range(SB):
        WX[s] = wet[s][0]
        WY[s] = wet[s][1]
        WZ[s] = jnp.where(wet_z[s], 1.0, 0.0)

    def chosen(k, s, v):
        code = CODE[k, s]
        return jnp.where(code == 1, v[1], jnp.where(code == 0, v[0], 0.0))

    def z_up(v):
        return [jnp.where(top, lroll(v[1], E - 1), lroll(v[0], -1)), lroll(v[1], -1)]

    def divergence(v):
        div = []
        for k, links in ((0, LX), (2, LY)):
            over = [toward(k, x) for x in v]
            f = [
                links[s] * (jnp.where(CODE[k, s] == 1, over[1], over[0]) - v[s])
                for s in range(SB)
            ]
            under = [toward(k + 1, x) for x in f]
            part = [f[s] - chosen(k + 1, s, under) for s in range(SB)]
            div = part if k == 0 else [a + b for a, b in zip(div, part)]
        up = z_up(v)
        f = [LZ[s] * (up[s] - v[s]) for s in range(SB)]
        under = [
            jnp.where(bottom, 0.0, lroll(f[0], 1)),
            jnp.where(bottom, lroll(f[0], 1 - E), lroll(f[1], 1)),
        ]
        return [div[s] + (f[s] - under[s]) for s in range(SB)]

    kk = [KE[s] for s in range(SB)]
    for k, links in ((0, LX), (2, LY)):
        over = [toward(k, x) for x in kk]
        for s in range(SB):
            links[s] = link(kk[s], chosen(k, s, over))
    up = z_up(kk)
    LZ[0] = link(kk[0], jnp.where(top & ~adj, 0.0, up[0]))
    LZ[1] = link(kk[1], jnp.where(top, 0.0, up[1]))
    tt = [TE[s] for s in range(SB)]
    div = divergence(tt)
    for s in range(SB):
        R[s] = div[s] - (WX[s] + WY[s] + WZ[s]) * tt[s]

    kmax = cond[0]
    for i in range(1, 8):
        kmax = jnp.maximum(kmax, cond[i])
    radius = jnp.full((8, H), kmax * 6.0, F32)
    center = radius + 1.0
    sigma = center / radius

    def grow(v):
        v = jnp.concatenate([v] * (EX // 8), axis=0)
        return jnp.concatenate([v] * (EL // H), axis=1)

    inv_center = grow(1.0 / center)
    rho0 = 1.0 / sigma
    rho1 = 1.0 / (2.0 * sigma - rho0)
    rho2 = 1.0 / (2.0 * sigma - rho1)
    coef = [
        (grow(rho1 * rho0), grow(2.0 * rho1 / radius)),
        (grow(rho2 * rho1), grow(2.0 * rho2 / radius)),
    ]


    def corner_rows(i):
        return [jnp.broadcast_to(CR[i, 0, j : j + 1, :], (8, H)) for j in range(FB)]

    def corner_heat(i, z):
        f = z - jnp.where(cz[i][0] < z, 1.0, 0.0) - jnp.where(cz[i][1] < z, 1.0, 0.0)
        a, b, c = corner_rows(i)
        return jnp.where(f < 0.5, a, jnp.where(f < 1.5, b, c))

    def of_three(za, zb, z, fn):
        f = z - jnp.where(za < z, 1.0, 0.0) - jnp.where(zb < z, 1.0, 0.0)
        return jnp.where(f < 0.5, fn(0), jnp.where(f < 1.5, fn(1), fn(2)))

    row_edge = (q8 == 0) | (q8 == 7)
    wide_edge = (r8 == 0) | (r8 == 7)

    def stack(v):
        return jnp.concatenate([v, v], axis=0)

    for s in range(SB):
        oz = own_z[s]
        nz = [nbr_z[k][s] for k in range(4)]
        ozf = splat((8, H), oz)
        nzf = [splat((8, H), z) for z in nz]
        f_side = [fluid_slot(nbr_z[k][0], nbr_z[k][1], oz) for k in range(4)]
        f_own = [fluid_slot(z0, z1, nz[k]) for k in range(4)]

        own_lo = jnp.broadcast_to(XR[0, f_side[1], HEAT : HEAT + 1, :], (8, W))
        own_hi = jnp.broadcast_to(XR[1, f_side[0], HEAT : HEAT + 1, :], (8, W))
        x_tile = jnp.where(
            r8 < 4,
            jnp.broadcast_to(Q[f_own[0], 1, E - 1 : E, :], (8, W)),
            jnp.broadcast_to(Q[f_own[1], 2, 0:1, :], (8, W)),
        )
        y_lo = jnp.where(g8 < 4, corner_heat(1, nzf[2]), corner_heat(0, nzf[3]))
        y_hi = jnp.where(g8 < 4, corner_heat(2, nzf[2]), corner_heat(3, nzf[3]))

        def from_y(i):
            half = CORNER_SRC[i][2]
            k = 3 if half else 2
            row = 0 if i < 2 else E - 1
            v = of_three(
                nbr_z[k][0],
                nbr_z[k][1],
                cz[i][s],
                lambda j: jnp.broadcast_to(YR[1 - half, j, row : row + 1, :], (8, H))
                if not half
                else jnp.broadcast_to(YR[0, j, row : row + 1, :], (8, H)),
            )
            return v if half else lroll(v, E)

        heat = jnp.concatenate(
            [
                jnp.concatenate([own_lo, y_lo], axis=1),
                jnp.concatenate([own_hi, y_hi], axis=1),
                jnp.concatenate([x_tile, quadrants(from_y)], axis=1),
            ],
            axis=0,
        )
        acc = R[s] + jnp.where(WX[s] > 0.5, heat, 0.0)

        left = lroll(YR[0, f_side[3]], -5 * E)
        right = lroll(YR[1, f_side[2]], 2 * E)

        def from_corner(i, z):
            v = corner_heat(i, z)
            if CORNER_SRC[i][2]:
                return jnp.where(row_edge, lroll(v, -3 * E), lroll(v, -2 * E))
            return jnp.where(row_edge, lroll(v, 3 * E), lroll(v, 2 * E))

        x_left = jnp.where(q8 < 4, from_corner(3, nzf[0]), from_corner(0, nzf[1]))
        x_right = jnp.where(q8 < 4, from_corner(2, nzf[0]), from_corner(1, nzf[1]))
        y_tile = jnp.where(
            group < 4,
            lroll(Q[f_own[2], 3, :, H:W], E),
            lroll(Q[f_own[3], 4, :, 0:H], -E),
        )

        def from_x(i):
            half = CORNER_SRC[i][2]
            k = 1 if i < 2 else 0
            lo = 0 if half else H
            v = of_three(
                nbr_z[k][0],
                nbr_z[k][1],
                cz[i][s],
                lambda j: jnp.broadcast_to(
                    XR[1 - k, j, CROSS : CROSS + 1, lo : lo + H], (8, H)
                ),
            )
            return lroll(v, -E if half else E)

        heat = jnp.concatenate(
            [
                jnp.concatenate([left, right, y_tile], axis=1),
                jnp.concatenate([x_left, x_right, quadrants(from_x)], axis=1),
            ],
            axis=0,
        )
        acc = acc + jnp.where(WY[s] > 0.5, heat, 0.0)

        def updown(k):
            za, zb = nbr_z[k]
            return fluid_slot(za, zb, nz[k] + 1), fluid_slot(za, zb, nz[k] - 1)

        tile = jnp.where(
            zw < 8,
            lroll(Q[fluid_slot(z0, z1, oz - 1), 5], 1 - E),
            lroll(Q[fluid_slot(z0, z1, oz + 1), 6], E - 1),
        )
        a, c = [], []
        for k in range(2):
            u, d = updown(k)
            a.append(jnp.broadcast_to(XR[1 - k, u, EDGE_Z : EDGE_Z + 1, :], (8, W)))
            c.append(jnp.broadcast_to(XR[1 - k, d, EDGE_Z : EDGE_Z + 1, :], (8, W)))
        a = jnp.where(r8 < 4, a[0], a[1])
        c = jnp.where(r8 < 4, c[0], c[1])
        x_tile = jnp.where(
            z8 < 8,
            jnp.where(wide_edge, lroll(c, 1 - E), lroll(c, 2 - E)),
            jnp.where(wide_edge, lroll(a, E - 1), lroll(a, E - 2)),
        )
        u, d = updown(2)
        a, c = YR[1, u], YR[1, d]
        y_up = jnp.where(
            zh < 8,
            jnp.where(group == 0, lroll(c, -7 * E + 1), lroll(c, -6 * E + 2)),
            jnp.where(group == 0, lroll(a, -5 * E - 1), lroll(a, -4 * E - 2)),
        )
        u, d = updown(3)
        a, c = YR[0, u], YR[0, d]
        y_down = jnp.where(
            zh < 8,
            jnp.where(group == 7, lroll(c, 1), lroll(c, 2 - E)),
            jnp.where(group == 7, lroll(a, 2 * E - 1), lroll(a, E - 2)),
        )

        def from_z(i):
            shift = 2 * E if CORNER_SRC[i][2] else -2 * E
            a = lroll(corner_heat(i, cz[i][s] + 1.0), shift + E - 1)
            c = lroll(corner_heat(i, cz[i][s] - 1.0), shift + 1 - E)
            return jnp.where(z8[:, :H] < 8, c, a)

        heat = jnp.concatenate(
            [
                jnp.concatenate([tile, jnp.where(group < 4, y_up, y_down)], axis=1),
                jnp.concatenate([x_tile, quadrants(from_z)], axis=1),
            ],
            axis=0,
        )
        R[s] = acc + jnp.where(WZ[s] > 0.5, heat, 0.0)

    upd = []
    sol = []
    for s in range(SB):
        d = R[s] * inv_center
        upd.append(d)
        sol.append(T[s] + d[0:E, 0:W])
    div = divergence(upd)
    for s in range(SB):
        r = R[s] - (upd[s] - div[s])
        R[s] = r
        upd[s] = coef[0][0] * upd[s] + coef[0][1] * r
        sol[s] = sol[s] + upd[s][0:E, 0:W]

    v = [x[:, 0:W] for x in upd]
    over = [rroll(x, -1) for x in v]
    f = [
        LX[s, :, 0:W] * (jnp.where(CODE[0, s, :, 0:W] == 1, over[1], over[0]) - v[s])
        for s in range(SB)
    ]
    under = [rroll(x, 1)[0:E] for x in f]
    code = [CODE[1, s, 0:E, 0:W] for s in range(SB)]
    div = []
    for s in range(SB):
        u = jnp.where(code[s] == 1, under[1], jnp.where(code[s] == 0, under[0], 0.0))
        div.append(f[s][0:E] - u)
    v = [x[0:E] for x in upd]
    over = [lroll(x, -E) for x in v]
    f = [
        LY[s, 0:E] * (jnp.where(CODE[2, s, 0:E] == 1, over[1], over[0]) - v[s])
        for s in range(SB)
    ]
    under = [lroll(x, E)[:, 0:W] for x in f]
    code = [CODE[3, s, 0:E, 0:W] for s in range(SB)]
    for s in range(SB):
        u = jnp.where(code[s] == 1, under[1], jnp.where(code[s] == 0, under[0], 0.0))
        div[s] = div[s] + (f[s][:, 0:W] - u)
    v = [x[0:E, 0:W] for x in upd]
    last, first = zw == E - 1, zw == 0
    up = [jnp.where(last, lroll(v[1], E - 1), lroll(v[0], -1)), lroll(v[1], -1)]
    f = [LZ[s, 0:E, 0:W] * (up[s] - v[s]) for s in range(SB)]
    under = [
        jnp.where(first, 0.0, lroll(f[0], 1)),
        jnp.where(first, lroll(f[0], 1 - E), lroll(f[1], 1)),
    ]
    for s in range(SB):
        r = R[s, 0:E, 0:W] - (v[s] - div[s] - (f[s] - under[s]))
        TO[s] = sol[s] + (coef[1][0][0:E, 0:W] * v[s] + coef[1][1][0:E, 0:W] * r)

    def x_face(b, side):
        shape = (8, W)
        df = -1 if side == 0 else 1
        dirn = 2 if side == 0 else 1
        bf = base_of(df, 0)
        main_id = nbr[b, dirn - 1]
        a = XR[side, slot(main_id, bf, FB)]
        val = a
        ids = jnp.full(shape, main_id)
        for r, p in enumerate(PX[side]):
            _, cy, cz = C[p]
            if r == 0:
                continue
            cid = nbr[b, OPP[p] - 1]
            if cy:
                which = jnp.full((8, H), slot(cid, base_of(df, -cy), FB))
                first, second, third = corner_rows(CORNER_OF[p])
                corner = jnp.where(which == 1, second, first)
                corner = jnp.where(which == 2, third, corner)
                corner = jnp.concatenate([corner, corner], axis=1)
                edge = l8 < E if cy > 0 else l8 >= W - E
                cand = jnp.where(edge, corner, a)
            else:
                edge = z8 == 0 if cz > 0 else z8 == E - 1
                cand = jnp.where(edge, XR[side, slot(cid, bf, FB)], a)
            val = jnp.where(r8 == r, cand, val)
            ids = jnp.where((r8 == r) & edge, jnp.full(shape, cid), ids)
        fall = FX[1 - side, b]
        wid = wall[b, dirn - 1]
        row = 7 if side == 0 else 0
        tw = XR[side, FB + slot(wid, bf, SB), row : row + 1, :]
        hot = (r8 == HEAT) & (jnp.full(shape, wid) >= 0)
        fall = jnp.where(hot, 2.0 * tw - fall, fall)
        return jnp.where(ids >= 0, val, fall)

    for b in range(FB):
        for side in range(2):
            xf = x_face(b, side)
            x = 0 if side == 0 else E - 1
            for r, p in enumerate(PX[side]):
                GO[b, p, x : x + 1, :] = xf[r : r + 1]
            QO[b, 1 + side, x : x + 1, :] = xf[HEAT : HEAT + 1]

    for i in range(N_COPY):

        @pl.when(near(*steps[i]))
        def _():
            copies[i].wait_send()


def store_kernel(fluid, heat, solid, fluid_out, heat_out, solid_out, sem):
    pairs = [(fluid, fluid_out), (heat, heat_out), (solid, solid_out)]
    for i, (src, dst) in enumerate(pairs):
        for x in range(E):
            pltpu.make_async_copy(
                src.at[..., x, :], dst.at[..., pl.ds(W * x, W)], sem.at[i]
            ).start(priority=x % 2)
    for i, (src, dst) in enumerate(pairs):
        pltpu.make_async_copy(src, src, sem.at[i]).wait()


def body(nf, nc, fluid_pop, heat_pop, solid_temp, material, cond, nbr, wall, snbr, sflu):
    hbm = pl.BlockSpec(memory_space=pltpu.HBM)

    def vm(*shape):
        return pltpu.VMEM(shape, F32)

    vmem = pl.BlockSpec(memory_space=pltpu.VMEM)
    fields = pl.pallas_call(
        functools.partial(kernel, nf, nc),
        out_shape=(
            vm(FB, 19, E, W),
            vm(FB, 7, E, W),
            vm(SB, E, W),
        ),
        in_specs=[hbm] * 9,
        out_specs=(vmem, vmem, vmem),
        scratch_shapes=[
            vm(FB, 19, E, W),
            vm(FB, 7, E, W),
            vm(SB, E, W),
            pltpu.VMEM((SB, E, W), jnp.int32),
            vm(SB, E, W),
            vm(2, FB, 8, W),
            vm(2, FB, E, H),
            vm(2, FB + SB, 8, W),
            vm(2, FB + SB, 8, W),
            vm(2, FB + SB, E, H),
            vm(2, FB + SB, E, H),
            vm(4, 1 + SB, 8, H),
            vm(4, 1 + SB, 8, H),
        ]
        + [vm(SB, EX, EL)] * 9
        + [
            pltpu.VMEM((4, SB, EX, EL), jnp.int32),
            pltpu.SMEM(cond.shape, F32),
            pltpu.SMEM(nbr.shape, jnp.int32),
            pltpu.SMEM(wall.shape, jnp.int32),
            pltpu.SMEM(snbr.shape, jnp.int32),
            pltpu.SMEM(sflu.shape, jnp.int32),
            pltpu.SemaphoreType.DMA((9,)),
            pltpu.SemaphoreType.DMA((N_COPY,)),
            pltpu.SemaphoreType.DMA((N_COPY,)),
        ],
        compiler_params=pltpu.CompilerParams(
            collective_id=0, has_side_effects=True, vmem_limit_bytes=LIMIT
        ),
    )(fluid_pop, heat_pop, solid_temp, material, cond, nbr, wall, snbr, sflu)
    return pl.pallas_call(
        store_kernel,
        out_shape=(
            jax.ShapeDtypeStruct(fluid_pop.shape, F32),
            jax.ShapeDtypeStruct(heat_pop.shape, F32),
            jax.ShapeDtypeStruct(solid_temp.shape, F32),
        ),
        in_specs=[pl.BlockSpec(memory_space=pl.ANY)] * 3,
        out_specs=(hbm, hbm, hbm),
        scratch_shapes=[pltpu.SemaphoreType.DMA((3,))],
        compiler_params=pltpu.CompilerParams(vmem_limit_bytes=8 * 1024 * 1024),
    )(*fields)


def solution(mesh):
    both = ("flow", "cross")
    in_specs = (
        P(both, None, None),
        P(both, None, None),
        P(both, None),
        P(both, None),
        P(),
        P(both, None),
        P(both, None),
        P(both, None),
        P(both, None),
    )
    out_specs = (P(both, None, None), P(both, None, None), P(both, None))
    return jax.shard_map(
        functools.partial(body, mesh.shape["flow"], mesh.shape["cross"]),
        mesh=mesh,
        in_specs=in_specs,
        out_specs=out_specs,
        check_vma=False,
    )
```
